32 devices in a mesh: rows: 8 (over z, y), tm: 4 (over x, core).
Axes of the slice: x: 2, y: 2, z: 4, core: 2. Of those that a mesh axis runs over, the one named last changes fastest.
Arguments:
- frames: bfloat16 [8, 1024, 1024], P('rows', 'tm'), may hold values from -6 to 6
- segments: int32 [8, 1024], P('rows'), may hold values from 0 to 2, never falling along the last dimension, each value on 1 to 682 neighbouring positions
- ffn1_in: bfloat16 [1024, 4096], P('rows', 'tm'), may hold values from -0.1875 to 0.1875
- ffn1_out: bfloat16 [4096, 1024], P('rows', 'tm'), may hold values from -0.09375 to 0.09375
- query_w: bfloat16 [1024, 1024], P('rows', 'tm'), may hold values from -0.1875 to 0.1875
- key_w: bfloat16 [1024, 1024], P('rows', 'tm'), may hold values from -0.1875 to 0.1875
- value_w: bfloat16 [1024, 1024], P('rows', 'tm'), may hold values from -0.1875 to 0.1875
- attn_out: bfloat16 [1024, 1024], P('rows', 'tm'), may hold values from -2 to 2
- conv_in: bfloat16 [1024, 2048], P('rows', 'tm'), may hold values from -0.1875 to 0.1875
- conv_out: bfloat16 [1024, 1024], P('rows', 'tm'), may hold values from -0.1875 to 0.1875
- ffn2_in: bfloat16 [1024, 4096], P('rows', 'tm'), may hold values from -0.1875 to 0.1875
- ffn2_out: bfloat16 [4096, 1024], P('rows', 'tm'), may hold values from -0.09375 to 0.09375
- norm_gains: float32 [5, 1024], replicated, may hold values from 0.5 to 1.5
- conv_kernel: float32 [5, 1024], replicated, may hold values from -3 to 3
- bn_gain: float32 [1024], replicated, may hold values from 0.5 to 1.5
- bn_bias: float32 [1024], replicated, may hold values from -3 to 3
- rel_table: float32 [8, 17], replicated, may hold values from -4 to 4
- cotangent: bfloat16 [8, 1024, 1024], P('rows', 'tm'), may hold values from -6 to 6
Outputs:
- output: bfloat16 [8, 1024, 1024], P('rows', 'tm')
- grad_frames: bfloat16 [8, 1024, 1024], P('rows', 'tm')
- grad_ffn1_in: float32 [1024, 4096], P('rows', 'tm')
- grad_ffn1_out: float32 [4096, 1024], P('rows', 'tm')
- grad_query: float32 [1024, 1024], P('rows', 'tm')
- grad_key: float32 [1024, 1024], P('rows', 'tm')
- grad_value: float32 [1024, 1024], P('rows', 'tm')
- grad_attn_out: float32 [1024, 1024], P('rows', 'tm')
- grad_conv_in: float32 [1024, 2048], P('rows', 'tm')
- grad_conv_out: float32 [1024, 1024], P('rows', 'tm')
- grad_ffn2_in: float32 [1024, 4096], P('rows', 'tm')
- grad_ffn2_out: float32 [4096, 1024], P('rows', 'tm')
- grad_norm_gains: float32 [5, 1024], replicated
- grad_conv_kernel: float32 [5, 1024], replicated
- grad_bn_gain: float32 [1024], replicated
- grad_bn_bias: float32 [1024], replicated
- grad_rel_table: float32 [8, 17], replicated
The draws below stay inside these ranges and needn't reach their ends.
Inputs may be any that keep to these rules, and one draw needn't show every extreme that they name: `segments`: in each row the ids never fall, each of the 3 utterances has 1 to 682 frames, and one has exactly 682.
All inputs are finite; a program needn't handle non-finite values.
Results may differ from the reference program's by a relative error of at most 0.025.
Values may be sent and summed in bfloat16 or wider, within the bound.
No kernel may reach another device: no remote copies, remote signals or barrier semaphores. Data moves between devices by JAX's collectives and lax.ppermute only.
A program may use at most 640 MiB of HBM per device.

```python
import math
import jax
import jax.numpy as jnp
import numpy as np
from jax import lax

D = 1024
FF = 4096
HEADS = 8
HEAD_DIM = 128
KERNEL = 5
RELMAX = 8
BUCKETS = 17
LENGTH = 1024
SEGS = 3
SEG_MOST = 682
ROWS = 8


def shard_levels(stream_key, extent, shards, smallest, high):
    gain = 1.0
    for axis_at, blocks in shards:
        draws = jax.random.uniform(jax.random.fold_in(jax.random.fold_in(stream_key, 6), axis_at), (blocks,), jnp.float32, smallest / len(shards), high / len(shards))
        gain = gain * jnp.repeat(jnp.exp(draws), extent[axis_at] // blocks).reshape((-1,) + (1,) * (len(extent) - 1 - axis_at))
    return gain


def length_profile(number_of, total, most, slope):
    weights = [(1 << 20) // math.isqrt(standing ** slope) + 1 for standing in range(2, number_of + 1)]
    surplus, holding = total - most - (number_of - 1), [1] * (number_of - 1)
    while surplus > 0:
        movable = [i for i in range(number_of - 1) if holding[i] < most]
        mass, left = sum([weights[i] for i in movable]), surplus
        for i in movable:
            extra = min(most - holding[i], max(1, left * weights[i] // mass), surplus)
            holding[i] = holding[i] + extra
            surplus = surplus - extra
    return np.array([most] + holding)


def ragged(stream_key, amount, total, bound, slope):
    if amount == 2:
        one = jax.random.randint(stream_key, (), max(1, total - bound), min(bound, total - 1) + 1)
        return jnp.stack([one, total - one])
    tallies = jnp.asarray(length_profile(amount, total, bound, slope), jnp.int32)
    twos = (amount - 1) // 2
    donor, taker = tallies[1:1 + 2 * twos:2], tallies[2:2 + 2 * twos:2]
    slack = jnp.minimum(donor - 1, bound - taker)
    passed = jax.random.randint(jax.random.fold_in(stream_key, 1), (twos,), 0, 1 << 20) % (slack + 1)
    tallies = tallies.at[1:1 + 2 * twos:2].set(donor - passed).at[2:2 + 2 * twos:2].set(taker + passed)
    return tallies[jax.random.permutation(jax.random.fold_in(stream_key, 2), amount)]


def scatter_about(key, shape, scale, reach, pieces=(), kind=jnp.bfloat16):
    entries = jax.random.normal(key, shape, jnp.float32) * scale
    if len(pieces) > 0:
        entries = shard_levels(key, shape, pieces, -0.22, 0.18) * entries
    return jnp.clip(entries, min=-reach, max=reach).astype(kind)


def setup_inputs(seed: int = 0) -> dict:
    streams_of = jax.random.split(jax.random.key(seed), 19)
    return {
        "frames": scatter_about(streams_of[0], (ROWS, LENGTH, D), 1.0, 6.0, ((0, 8), (1, 4))),
        "segments": jax.vmap(lambda own: jnp.searchsorted(jnp.cumsum(ragged(own, SEGS, LENGTH, SEG_MOST, 0)), jnp.arange(LENGTH), side="right"))(jax.random.split(streams_of[1], ROWS)).reshape((ROWS, LENGTH)).astype(jnp.int32),
        "ffn1_in": scatter_about(streams_of[2], (D, FF), D ** -0.5, 0.1875, ((0, 8), (1, 4))),
        "ffn1_out": scatter_about(streams_of[3], (FF, D), FF ** -0.5, 0.09375, ((0, 8), (1, 4))),
        "query_w": scatter_about(streams_of[4], (D, D), D ** -0.5, 0.1875, ((0, 8), (1, 4))),
        "key_w": scatter_about(streams_of[5], (D, D), D ** -0.5, 0.1875, ((0, 8), (1, 4))),
        "value_w": scatter_about(streams_of[6], (D, D), D ** -0.5, 0.1875, ((0, 8), (1, 4))),
        "attn_out": scatter_about(streams_of[7], (D, D), (max(D * 8 // LENGTH, 1)) ** -0.5, 2.0, ((0, 8), (1, 4))),
        "conv_in": scatter_about(streams_of[8], (D, 2 * D), D ** -0.5, 0.1875, ((0, 8), (1, 4))),
        "conv_out": scatter_about(streams_of[9], (D, D), D ** -0.5, 0.1875, ((0, 8), (1, 4))),
        "ffn2_in": scatter_about(streams_of[10], (D, FF), D ** -0.5, 0.1875, ((0, 8), (1, 4))),
        "ffn2_out": scatter_about(streams_of[11], (FF, D), FF ** -0.5, 0.09375, ((0, 8), (1, 4))),
        "norm_gains": jnp.clip(1.0 + 0.1 * jax.random.normal(streams_of[12], (5, D), jnp.float32), 0.5, 1.5),
        "conv_kernel": scatter_about(streams_of[13], (KERNEL, D), 0.5, 3.0, (), jnp.float32),
        "bn_gain": jnp.clip(1.0 + 0.1 * jax.random.normal(streams_of[14], (D,), jnp.float32), 0.5, 1.5),
        "bn_bias": scatter_about(streams_of[15], (D,), 0.5, 3.0, (), jnp.float32),
        "rel_table": scatter_about(streams_of[16], (HEADS, BUCKETS), 1.0, 4.0, (), jnp.float32),
        "cotangent": scatter_about(streams_of[17], (ROWS, LENGTH, D), 1.0, 6.0, ((0, 8), (1, 4))),
    }


epsilon = 1e-05

@jax.custom_vjp
def low(v):
    return lax.optimization_barrier(v.astype(jnp.bfloat16)).astype(jnp.float32)

@jax.custom_vjp
def low_back(v):
    return v

def low_keep(v):
    return (low(v), None)

def low_pass(kept, grad):
    return (grad,)

def back_keep(v):
    return (v, None)

def back_low(kept, grad):
    return (low(grad),)
low.defvjp(low_keep, low_pass)
low_back.defvjp(back_keep, back_low)

def matmul_hi(first_op, second_op):
    return jnp.dot(first_op, second_op, precision=lax.Precision.HIGHEST)

def layer_norm(inputs, gain_row):
    center = inputs - lax.optimization_barrier(jnp.mean(inputs, axis=-1, keepdims=True))
    spread = lax.optimization_barrier(jnp.mean(center * center, axis=-1, keepdims=True))
    return center * lax.rsqrt(spread + epsilon) * gain_row

def half_ffn(inputs, gain_row, weight_in, weight_out):
    hidden = low(layer_norm(inputs, gain_row))
    preact = low_back(matmul_hi(hidden, weight_in))
    active = low(jax.nn.silu(preact))
    return inputs + 0.5 * low_back(matmul_hi(active, weight_out))

def section_one(inputs, seg_row, ffn1_in, ffn1_out, query_w, key_w, value_w, attn_out, conv_in, norm_gains, conv_kernel, rel_table):
    resid_one = half_ffn(inputs, norm_gains[0], ffn1_in, ffn1_out)
    hidden = low(layer_norm(resid_one, norm_gains[1]))
    queries = low(low_back(matmul_hi(hidden, query_w))).reshape(LENGTH, HEADS, HEAD_DIM)
    key_rows = low(low_back(matmul_hi(hidden, key_w))).reshape(LENGTH, HEADS, HEAD_DIM)
    values = low(low_back(matmul_hi(hidden, value_w))).reshape(LENGTH, HEADS, HEAD_DIM)
    raw_scores = jnp.einsum('qhd,khd->hqk', queries, key_rows, precision=lax.Precision.HIGHEST) * HEAD_DIM ** (-0.5)
    positions = jnp.arange(LENGTH, dtype=jnp.int32)
    bucket = jnp.clip(positions[None, :] - positions[:, None], -RELMAX, RELMAX) + RELMAX
    raw_scores = low_back(raw_scores + rel_table[:, bucket])
    same_seg = seg_row[:, None] == seg_row[None, :]
    scores = jnp.where(same_seg[None], raw_scores, -jnp.inf)
    logsum = jax.nn.logsumexp(scores, axis=-1, keepdims=True)
    soft_probs = jnp.exp(scores - logsum)
    mixed = jnp.einsum('hqk,khd->qhd', low(soft_probs), values, precision=lax.Precision.HIGHEST).reshape(LENGTH, D)
    mixed = low(low_back(mixed))
    resid_two = resid_one + low_back(matmul_hi(mixed, attn_out))
    hidden_conv = low(layer_norm(resid_two, norm_gains[2]))
    upper_proj = low_back(matmul_hi(hidden_conv, conv_in))
    gated_glu = low(upper_proj[:, :D] * jax.nn.sigmoid(upper_proj[:, D:]))
    half_span = KERNEL // 2
    padded_glu = jnp.pad(gated_glu, ((half_span, half_span), (0, 0)))
    padded_seg = jnp.pad(seg_row, (half_span, half_span), constant_values=-1)
    conv_sum = jnp.zeros((LENGTH, D), jnp.float32)
    for tap_id in range(KERNEL):
        tap_same = (padded_seg[tap_id:tap_id + LENGTH] == seg_row)[:, None]
        conv_sum = conv_sum + jnp.where(tap_same, padded_glu[tap_id:tap_id + LENGTH] * conv_kernel[tap_id], 0.0)
    return (resid_two, low_back(conv_sum))

def section_two(resid_two, conv_row, centre, inverse, conv_out, ffn2_in, ffn2_out, norm_gains, bn_gain, bn_bias):
    shifted = (conv_row - centre) * inverse * bn_gain + bn_bias
    active = low(jax.nn.silu(shifted))
    resid_three = resid_two + low_back(matmul_hi(active, conv_out))
    resid_four = half_ffn(resid_three, norm_gains[3], ffn2_in, ffn2_out)
    return layer_norm(resid_four, norm_gains[4])

def forward(inputs, segments, ffn1_in, ffn1_out, query_w, key_w, value_w, attn_out, conv_in, conv_out, ffn2_in, ffn2_out, norm_gains, conv_kernel, bn_gain, bn_bias, rel_table):

    def row_one(row_pair):
        return section_one(row_pair[0], row_pair[1], ffn1_in, ffn1_out, query_w, key_w, value_w, attn_out, conv_in, norm_gains, conv_kernel, rel_table)
    resid_two, conv_all = lax.map(jax.checkpoint(row_one), (inputs, segments))
    centre = lax.optimization_barrier(jnp.mean(conv_all, axis=(0, 1)))
    spread = lax.optimization_barrier(jnp.mean(conv_all * conv_all, axis=(0, 1))) - centre * centre
    inverse = lax.rsqrt(spread + epsilon)

    def row_two(row_pair):
        return section_two(row_pair[0], row_pair[1], centre, inverse, conv_out, ffn2_in, ffn2_out, norm_gains, bn_gain, bn_bias)
    return lax.map(jax.checkpoint(row_two), (resid_two, conv_all))

def reference(frames, segments, ffn1_in, ffn1_out, query_w, key_w, value_w, attn_out, conv_in, conv_out, ffn2_in, ffn2_out, norm_gains, conv_kernel, bn_gain, bn_bias, rel_table, cotangent):

    def wrapped(inputs, w_a, w_b, w_q, w_k, w_v, w_o, w_c, w_d, w_e, w_f, gains, kernel_taps, gain_bn, bias_bn, table):
        return forward(inputs, segments, w_a, w_b, w_q, w_k, w_v, w_o, w_c, w_d, w_e, w_f, gains, kernel_taps, gain_bn, bias_bn, table)
    output, pullback = jax.vjp(wrapped, frames.astype(jnp.float32), ffn1_in.astype(jnp.float32), ffn1_out.astype(jnp.float32), query_w.astype(jnp.float32), key_w.astype(jnp.float32), value_w.astype(jnp.float32), attn_out.astype(jnp.float32), conv_in.astype(jnp.float32), conv_out.astype(jnp.float32), ffn2_in.astype(jnp.float32), ffn2_out.astype(jnp.float32), norm_gains, conv_kernel, bn_gain, bn_bias, rel_table)
    grads = pullback(cotangent.astype(jnp.float32))
    return (output.astype(jnp.bfloat16), grads[0].astype(jnp.bfloat16), grads[1], grads[2], grads[3], grads[4], grads[5], grads[6], grads[7], grads[8], grads[9], grads[10], grads[11], grads[12], grads[13], grads[14], grads[15])
```

```python
import functools

import jax
import jax.numpy as jnp
from jax import lax
from jax.experimental import pallas as pl
from jax.experimental.pallas import tpu as pltpu
from jax.sharding import PartitionSpec as P

HEAD_DIM = 128
RELMAX = 8
LANES = 128
EPS = 1e-05
BF = jnp.bfloat16
F32 = jnp.float32


def mm(a, b):
    return jnp.dot(a, b, preferred_element_type=F32)


def mm_tn(a, b):
    return lax.dot_general(a, b, (((0,), (0,)), ((), ())), preferred_element_type=F32)


def mm_nt(a, b):
    return lax.dot_general(a, b, (((1,), (1,)), ((), ())), preferred_element_type=F32)


def silu_slope(a):
    s = jax.nn.sigmoid(a)
    return s * (1.0 + a * (1.0 - s))


def norm_rows(v, g):
    center = v - jnp.mean(v, axis=-1, keepdims=True)
    spread = jnp.mean(center * center, axis=-1, keepdims=True)
    inverse = lax.rsqrt(spread + EPS)
    normed = center * inverse
    return normed * g, normed, inverse


def norm_back(grad, normed, inverse, g):
    scaled = grad * g
    back = inverse * (
        scaled
        - jnp.mean(scaled, axis=-1, keepdims=True)
        - normed * jnp.mean(scaled * normed, axis=-1, keepdims=True)
    )
    return back, jnp.sum(grad * normed, axis=0)


def tm_peer(dx, dc):
    size = lax.axis_size("tm")
    chips = size // 2
    return [
        (((t // 2 + dx) % chips) * 2 + ((t % 2) ^ dc), t) for t in range(size)
    ]


def from_peer(a, dx, dc):
    return lax.ppermute(a, "tm", tm_peer(dx, dc))


def peer_index(dx, dc):
    chips = lax.axis_size("tm") // 2
    t = lax.axis_index("tm")
    return lax.rem(t // 2 + dx, chips) * 2 + jnp.bitwise_xor(t % 2, dc)


def gather_tm(a):
    size = lax.axis_size("tm")
    n, w = a.shape
    far = [from_peer(a, dx, 0) for dx in range(1, size // 2)]
    held = {(0, 0): a, (0, 1): from_peer(a, 0, 1)}
    for dx, b in enumerate(far, 1):
        held[dx, 0] = b
        held[dx, 1] = from_peer(b, 0, 1)
    out = jnp.zeros((size, n, w), a.dtype)
    for (dx, dc), b in held.items():
        out = lax.dynamic_update_index_in_dim(out, b, peer_index(dx, dc), 0)
    return out.reshape(size * n, w)


def scatter_tm(p):
    size = lax.axis_size("tm")
    chips = size // 2
    t = lax.axis_index("tm")
    x, c = t // 2, t % 2
    w = p.shape[1]
    p = p.reshape(chips, 2, p.shape[0] // size, w)
    mine = lax.dynamic_index_in_dim(p, c, 1, keepdims=False)
    theirs = lax.dynamic_index_in_dim(p, 1 - c, 1, keepdims=False).astype(BF)
    q = mine.astype(F32) + from_peer(theirs, 0, 1).astype(F32)
    total = lax.dynamic_index_in_dim(q, x, 0, keepdims=False)
    for dx in range(1, chips):
        piece = lax.dynamic_index_in_dim(q, lax.rem(x + chips - dx, chips), 0, keepdims=False)
        total = total + from_peer(piece.astype(BF), dx, 0).astype(F32)
    return total


def exchange_tm(pieces):
    size = lax.axis_size("tm")
    chips = size // 2
    t = lax.axis_index("tm")
    out = jnp.zeros(pieces.shape, pieces.dtype)
    out = lax.dynamic_update_index_in_dim(
        out, lax.dynamic_index_in_dim(pieces, t, 0, keepdims=False), t, 0
    )
    for dx in range(chips):
        for dc in range(2):
            if dx or dc:
                piece = lax.dynamic_index_in_dim(
                    pieces, peer_index(chips - dx, dc), 0, keepdims=False
                )
                out = lax.dynamic_update_index_in_dim(
                    out, from_peer(piece, dx, dc), peer_index(dx, dc), 0
                )
    return out


def sum_axis(v, axis):
    size, bit = lax.axis_size(axis), 1
    while bit < size:
        v = v + lax.ppermute(v, axis, [(i, i ^ bit) for i in range(size)])
        bit *= 2
    return v


def ffn_pieces(w_in, w_out):
    rows, size = lax.axis_size("rows"), lax.axis_size("tm")
    unit = w_out.shape[0] // size
    m, w = w_in.shape
    a = w_in.reshape(m, w // (size * unit), size, unit).transpose(2, 0, 1, 3)
    return a.reshape(size, m, w // size), w_out.reshape(size, unit, w_out.shape[1])


def ffn_ready(w_in, w_out):
    size = lax.axis_size("tm")
    a, b = ffn_pieces(w_in, w_out)
    if a.shape == b.shape:
        both = exchange_tm(jnp.concatenate([a, b], axis=1))
        a, b = both[:, : a.shape[1]], both[:, a.shape[1] :]
    else:
        a, b = exchange_tm(a), exchange_tm(b)
    a = a.transpose(1, 0, 2).reshape(a.shape[1], -1)
    b = b.transpose(1, 0, 2).reshape(b.shape[1], -1)
    if a.shape == b.shape:
        full = lax.all_gather(jnp.concatenate([a, b], axis=1), "rows", axis=0, tiled=True)
        return full[:, : a.shape[1]], full[:, a.shape[1] :]
    return tuple(lax.all_gather(v, "rows", axis=0, tiled=True) for v in (a, b))


def ffn_return(g_in, g_out, like_in, like_out):
    rows, size = lax.axis_size("rows"), lax.axis_size("tm")
    if g_in.shape == g_out.shape:
        both = lax.psum_scatter(
            jnp.concatenate([g_in, g_out], axis=1), "rows", scatter_dimension=0, tiled=True
        )
        a, b = both[:, : g_in.shape[1]], both[:, g_in.shape[1] :]
    else:
        a, b = (lax.psum_scatter(v, "rows", scatter_dimension=0, tiled=True) for v in (g_in, g_out))
    a = a.reshape(a.shape[0], size, -1).transpose(1, 0, 2)
    b = b.reshape(b.shape[0], size, -1).transpose(1, 0, 2)
    if a.shape == b.shape:
        both = exchange_tm(jnp.concatenate([a, b], axis=1))
        a, b = both[:, : a.shape[1]], both[:, a.shape[1] :]
    else:
        a, b = exchange_tm(a), exchange_tm(b)
    unit = like_out[0] // size
    m, w = like_in
    a = a.reshape(size, m, w // (size * unit), unit).transpose(1, 2, 0, 3).reshape(m, w)
    return a.astype(F32), b.reshape(like_out).astype(F32)


def head_rows_perm():
    rows, size = lax.axis_size("rows"), lax.axis_size("tm")
    perm = []
    for r in range(rows):
        for t in range(size):
            k, u = divmod(r, size)
            perm.append(((t * (rows // size) + k) * size + u, r * size + t))
    return perm


def fill_bias(tab_ref, head, strip, length):
    lo, hi = length - LANES, length + 2 * LANES
    first, last = tab_ref[head, 0], tab_ref[head, 2 * RELMAX]
    offset = (
        lax.broadcasted_iota(jnp.int32, (LANES, hi - lo), 1)
        - LANES
        - lax.broadcasted_iota(jnp.int32, (LANES, hi - lo), 0)
    )
    tile = jnp.where(offset <= -RELMAX, first, last)
    for b in range(1, 2 * RELMAX):
        tile = jnp.where(offset == b - RELMAX, tab_ref[head, b], tile)
    strip[:, :lo] = jnp.full((LANES, lo), first, F32)
    strip[:, lo:hi] = tile
    strip[:, hi:] = jnp.full((LANES, 2 * length - hi), last, F32)


def biased(q, k, seg_col, seg_row, strip, first, length):
    raw = mm_nt(q, k) * HEAD_DIM ** (-0.5)
    parts = [
        strip[:, length - (first + a) : 2 * length - (first + a)]
        for a in range(0, q.shape[0], LANES)
    ]
    bias = parts[0] if len(parts) == 1 else jnp.concatenate(parts, axis=0)
    return jnp.where(seg_col == seg_row, raw + bias, -jnp.inf)


def attend_kernel(tab_ref, seg_row_ref, seg_col_ref, q_ref, k_ref, v_ref, o_ref, lse_ref, strip):
    length = q_ref.shape[0]
    block = min(256, length)
    fill_bias(tab_ref, pl.program_id(0), strip, length)
    k, v = k_ref[...], v_ref[...]
    for first in range(0, length, block):
        own = slice(first, first + block)
        sc = biased(q_ref[own, :], k, seg_col_ref[own, :], seg_row_ref[...], strip, first, length)
        peak = jnp.max(sc, axis=1, keepdims=True)
        e = jnp.exp(sc - peak)
        total = jnp.sum(e, axis=1, keepdims=True)
        p = (e * (1.0 / total)).astype(BF)
        o_ref[own, :] = mm(p, v).astype(BF)
        lse_ref[0, own, :] = peak + jnp.log(total)


def attend(qkv, seg_row, table):
    length = qkv.shape[0]
    heads = table.shape[0]
    column = lambda first: pl.BlockSpec((length, HEAD_DIM), lambda h: (0, first + h))
    return pl.pallas_call(
        attend_kernel,
        grid=(heads,),
        in_specs=[
            pl.BlockSpec(memory_space=pltpu.SMEM),
            pl.BlockSpec((1, length), lambda h: (0, 0)),
            pl.BlockSpec((length, 1), lambda h: (0, 0)),
            column(0),
            column(heads),
            column(2 * heads),
        ],
        out_specs=[column(0), pl.BlockSpec((1, length, 1), lambda h: (h, 0, 0))],
        out_shape=[
            jax.ShapeDtypeStruct((length, heads * HEAD_DIM), BF),
            jax.ShapeDtypeStruct((heads, length, 1), F32),
        ],
        scratch_shapes=[pltpu.VMEM((LANES, 2 * length), F32)],
        compiler_params=pltpu.CompilerParams(vmem_limit_bytes=40 * 1024 * 1024),
        cost_estimate=pl.CostEstimate(
            flops=4 * heads * length * length * HEAD_DIM,
            bytes_accessed=8 * length * heads * HEAD_DIM,
            transcendentals=heads * length * length,
        ),
    )(table, seg_row.reshape(1, length), seg_row.reshape(length, 1), qkv, qkv, qkv)


def attend_back_kernel(
    tab_ref, seg_row_ref, seg_col_ref, q_ref, k_ref, v_ref, do_ref, lse_ref, dqkv_ref, band_ref,
    strip, dk_sum, dv_sum,
):
    length = q_ref.shape[0]
    block = min(256, length)
    head, heads = pl.program_id(0), pl.num_programs(0)
    fill_bias(tab_ref, head, strip, length)
    k, v = k_ref[...], v_ref[...]
    scale = HEAD_DIM ** (-0.5)
    at = lambda n: pl.ds(pl.multiple_of((n * heads + head) * HEAD_DIM, HEAD_DIM), HEAD_DIM)
    low = jnp.zeros((LANES, LANES), F32)
    high = jnp.zeros((LANES, LANES), F32)
    band = [jnp.zeros((LANES, LANES), F32) for _ in range(3)]
    for first in range(0, length, block):
        own = slice(first, first + block)
        q, do = q_ref[own, :], do_ref[own, :]
        sc = biased(q, k, seg_col_ref[own, :], seg_row_ref[...], strip, first, length)
        p = jnp.exp(sc - lse_ref[0, own, :])
        dp = mm_nt(do, v)
        inner = jnp.sum(p * dp, axis=1, keepdims=True)
        ds = (p * (dp - inner)).astype(BF)
        dv = mm_tn(p.astype(BF), do)
        dk = mm_tn(ds, q)
        if first == 0:
            dv_sum[...] = dv
            dk_sum[...] = dk
        else:
            dv_sum[...] += dv
            dk_sum[...] += dk
        dqkv_ref[own, at(0)] = (mm(ds, k) * scale).astype(BF)
        wide = ds.astype(F32)
        for a in range(0, block, LANES):
            for b in range(0, length, LANES):
                part = wide[a : a + LANES, b : b + LANES]
                apart = (b - first - a) // LANES
                if apart < -1:
                    low = low + part
                elif apart > 1:
                    high = high + part
                else:
                    band[apart + 1] = band[apart + 1] + part
    dqkv_ref[:, at(1)] = (dk_sum[...] * scale).astype(BF)
    dqkv_ref[:, at(2)] = dv_sum[...].astype(BF)
    for i, part in enumerate([low] + band + [high]):
        band_ref[0, :, i * LANES : (i + 1) * LANES] = part


def attend_back(qkv, seg_row, table, lse, grad):
    length = qkv.shape[0]
    heads = table.shape[0]
    column = lambda first: pl.BlockSpec((length, HEAD_DIM), lambda h: (0, first + h))
    dqkv, band = pl.pallas_call(
        attend_back_kernel,
        grid=(heads,),
        in_specs=[
            pl.BlockSpec(memory_space=pltpu.SMEM),
            pl.BlockSpec((1, length), lambda h: (0, 0)),
            pl.BlockSpec((length, 1), lambda h: (0, 0)),
            column(0),
            column(heads),
            column(2 * heads),
            column(0),
            pl.BlockSpec((1, length, 1), lambda h: (h, 0, 0)),
        ],
        out_specs=[
            pl.BlockSpec((length, 3 * heads * HEAD_DIM), lambda h: (0, 0)),
            pl.BlockSpec((1, LANES, 5 * LANES), lambda h: (h, 0, 0)),
        ],
        out_shape=[
            jax.ShapeDtypeStruct((length, 3 * heads * HEAD_DIM), BF),
            jax.ShapeDtypeStruct((heads, LANES, 5 * LANES), F32),
        ],
        scratch_shapes=[
            pltpu.VMEM((LANES, 2 * length), F32),
            pltpu.VMEM((length, HEAD_DIM), F32),
            pltpu.VMEM((length, HEAD_DIM), F32),
        ],
        compiler_params=pltpu.CompilerParams(vmem_limit_bytes=48 * 1024 * 1024),
        cost_estimate=pl.CostEstimate(
            flops=10 * heads * length * length * HEAD_DIM,
            bytes_accessed=16 * length * heads * HEAD_DIM,
            transcendentals=heads * length * length,
        ),
    )(table, seg_row.reshape(1, length), seg_row.reshape(length, 1), qkv, qkv, qkv, grad, lse)
    offset = (
        lax.broadcasted_iota(jnp.int32, (LANES, 3 * LANES), 1)
        - LANES
        - lax.broadcasted_iota(jnp.int32, (LANES, 3 * LANES), 0)
    )
    middle = band[:, :, LANES : 4 * LANES]
    inner = [
        jnp.sum(jnp.where(offset == b, middle, 0.0), axis=(1, 2)) for b in range(1 - RELMAX, RELMAX)
    ]
    lower = jnp.sum(jnp.where(offset <= -RELMAX, middle, 0.0), axis=(1, 2))
    upper = jnp.sum(jnp.where(offset >= RELMAX, middle, 0.0), axis=(1, 2))
    lower = lower + jnp.sum(band[:, :, :LANES], axis=(1, 2))
    upper = upper + jnp.sum(band[:, :, 4 * LANES :], axis=(1, 2))
    return dqkv, jnp.stack([lower] + inner + [upper], axis=1)


def shards(
    frames,
    segments,
    ffn1_in,
    ffn1_out,
    query_w,
    key_w,
    value_w,
    attn_out,
    conv_in,
    conv_out,
    ffn2_in,
    ffn2_out,
    norm_gains,
    conv_kernel,
    bn_gain,
    bn_bias,
    rel_table,
    cotangent,
):
    rows, size = lax.axis_size("rows"), lax.axis_size("tm")
    t = lax.axis_index("tm")
    own, width = frames.shape[1], frames.shape[2]
    length = own * size
    share = width // size
    heads = rel_table.shape[0] // size
    taps = conv_kernel.shape[0]
    reach = taps // 2
    frame_total = float(length * rows)
    seg = segments[0]
    table = lax.dynamic_slice_in_dim(rel_table, t * heads, heads, 0)
    depth = width // rows
    unit = depth // size

    def mine(v):
        v = v.reshape(-1, rows, size, unit)
        return lax.dynamic_index_in_dim(v, t, 2, keepdims=False).reshape(-1, share)

    def placed(v):
        n = v.shape[0]
        out = jnp.zeros((n, rows, size, unit), F32)
        return lax.dynamic_update_index_in_dim(
            out, v.reshape(n, rows, unit), t, 2
        ).reshape(n, width)

    kernel_own = mine(conv_kernel)
    bn_gain_own, bn_bias_own = mine(bn_gain[None]), mine(bn_bias[None])

    f1_in, f1_out = ffn_ready(ffn1_in, ffn1_out)
    perm = head_rows_perm()
    out_block = lax.ppermute(attn_out, ("rows", "tm"), perm)
    attn_w = lax.all_gather(
        jnp.concatenate([query_w, key_w, value_w, out_block], axis=1), "rows", axis=0, tiled=True
    )
    qkv_w = attn_w[:, : 3 * share]
    groups = rows // size
    attn_out_w = (
        attn_w[:, 3 * share :]
        .reshape(groups, size, depth, share)
        .transpose(0, 2, 1, 3)
        .reshape(share, width)
    )
    wide = conv_in.shape[1]
    conv_in_x = exchange_tm(
        conv_in.reshape(depth, wide // depth, size, unit)
        .transpose(2, 0, 1, 3)
        .reshape(size, depth, wide // size)
    )
    conv_in_x = conv_in_x.transpose(1, 0, 2).reshape(depth, wide)
    conv_out_x = exchange_tm(conv_out.reshape(size, unit, share)).reshape(depth, share)
    conv_w = lax.all_gather(
        jnp.concatenate([conv_in_x, conv_out_x], axis=1), "rows", axis=0, tiled=True
    )
    conv_in_w = conv_w[:, :wide]
    conv_out_w = (
        conv_w[:, wide:]
        .reshape(rows, size, unit, share)
        .transpose(0, 2, 1, 3)
        .reshape(share, width)
    )
    f2_in, f2_out = ffn_ready(ffn2_in, ffn2_out)

    inputs = frames[0].astype(F32)
    n1, normed_one, inverse_one = norm_rows(inputs, norm_gains[0])
    h1 = gather_tm(n1.astype(BF))
    a1 = mm(h1, f1_in)
    s1 = (a1 * jax.nn.sigmoid(a1)).astype(BF)
    x1 = inputs + 0.5 * scatter_tm(mm(s1, f1_out).astype(BF))

    n2, normed_two, inverse_two = norm_rows(x1, norm_gains[1])
    h2 = gather_tm(n2.astype(BF))
    qkv = mm(h2, qkv_w).astype(BF)
    att, lse = attend(qkv, seg, table)
    x2 = x1 + scatter_tm(mm(att, attn_out_w).astype(BF))

    n3, normed_three, inverse_three = norm_rows(x2, norm_gains[2])
    h3 = gather_tm(n3.astype(BF))
    u = mm(h3, conv_in_w)
    u_lin, u_sig = u[:, :share], jax.nn.sigmoid(u[:, share:])
    z = (u_lin * u_sig).astype(BF)
    seg_pad = jnp.pad(seg, (reach, reach), constant_values=-1)
    same = [(seg_pad[k : k + length] == seg)[:, None] for k in range(taps)]

    def shifted_rows(v):
        v = jnp.pad(v, ((reach, reach), (0, 0)))
        return [v[k : k + length] for k in range(taps)]

    z_near = shifted_rows(z)
    conv = jnp.zeros((length, share), F32)
    for k in range(taps):
        conv = conv + jnp.where(same[k], z_near[k].astype(F32) * kernel_own[k], 0.0)
    moments = sum_axis(
        jnp.stack([jnp.sum(conv, axis=0), jnp.sum(conv * conv, axis=0)]), "rows"
    )
    centre = moments[0] / frame_total
    inverse_bn = lax.rsqrt(moments[1] / frame_total - centre * centre + EPS)
    normed_bn = (conv - centre) * inverse_bn
    shifted = normed_bn * bn_gain_own + bn_bias_own
    e = (shifted * jax.nn.sigmoid(shifted)).astype(BF)
    x3 = x2 + scatter_tm(mm(e, conv_out_w).astype(BF))

    n4, normed_four, inverse_four = norm_rows(x3, norm_gains[3])
    h4 = gather_tm(n4.astype(BF))
    a4 = mm(h4, f2_in)
    s4 = (a4 * jax.nn.sigmoid(a4)).astype(BF)
    x4 = x3 + 0.5 * scatter_tm(mm(s4, f2_out).astype(BF))
    n5, normed_five, inverse_five = norm_rows(x4, norm_gains[4])
    output = n5.astype(BF)[None]

    d4, gain_five = norm_back(cotangent[0].astype(F32), normed_five, inverse_five, norm_gains[4])
    g4 = gather_tm((0.5 * d4).astype(BF))
    d_f2_out = mm_tn(s4, g4).astype(BF)
    da4 = (mm_nt(g4, f2_out) * silu_slope(a4)).astype(BF)
    d_f2_in = mm_tn(h4, da4).astype(BF)
    back, gain_four = norm_back(
        scatter_tm(mm_nt(da4, f2_in).astype(BF)), normed_four, inverse_four, norm_gains[3]
    )
    d3 = d4 + back
    grad_ffn2_in, grad_ffn2_out = ffn_return(d_f2_in, d_f2_out, ffn2_in.shape, ffn2_out.shape)

    g3 = gather_tm(d3.astype(BF))
    d_conv_out = mm_tn(e, g3).astype(BF)
    dn = mm_nt(g3, conv_out_w) * silu_slope(shifted)
    bn_part = jnp.stack([jnp.sum(dn, axis=0), jnp.sum(dn * normed_bn, axis=0)])
    bn_sums = sum_axis(bn_part, "rows")
    dc = (
        bn_gain_own
        * inverse_bn
        * (dn - bn_sums[0] / frame_total - normed_bn * (bn_sums[1] / frame_total))
    ).astype(BF)
    dc_near = shifted_rows(dc)
    dc_wide = dc.astype(F32)
    dz = jnp.zeros((length, share), F32)
    d_kernel = []
    for k in range(taps):
        mirror = taps - 1 - k
        dz = dz + jnp.where(same[mirror], dc_near[mirror].astype(F32) * kernel_own[k], 0.0)
        d_kernel.append(
            jnp.sum(jnp.where(same[k], z_near[k].astype(F32) * dc_wide, 0.0), axis=0)
        )
    du = jnp.concatenate([dz * u_sig, dz * u_lin * u_sig * (1.0 - u_sig)], axis=1).astype(BF)
    d_conv_in = mm_tn(h3, du).astype(BF)
    back, gain_three = norm_back(
        scatter_tm(mm_nt(du, conv_in_w).astype(BF)), normed_three, inverse_three, norm_gains[2]
    )
    d2 = d3 + back

    g2 = gather_tm(d2.astype(BF))
    d_attn_out = mm_tn(att, g2).astype(BF)
    d_att = mm_nt(g2, attn_out_w).astype(BF)
    dqkv, d_table = attend_back(qkv, seg, table, lse, d_att)
    d_qkv = mm_tn(h2, dqkv).astype(BF)
    back, gain_two = norm_back(
        scatter_tm(mm_nt(dqkv, qkv_w).astype(BF)), normed_two, inverse_two, norm_gains[1]
    )
    d1 = d2 + back

    d_attn_blocks = (
        d_attn_out.reshape(groups, depth, size, share).transpose(0, 2, 1, 3).reshape(width, share)
    )
    d_conv_blocks = (
        d_conv_out.reshape(rows, unit, size, share).transpose(0, 2, 1, 3).reshape(width, share)
    )
    middle = lax.psum_scatter(
        jnp.concatenate([d_qkv, d_attn_blocks, d_conv_in, d_conv_blocks], axis=1),
        "rows",
        scatter_dimension=0,
        tiled=True,
    )
    grad_query, grad_key, grad_value = (
        middle[:, i * share : (i + 1) * share].astype(F32) for i in range(3)
    )
    grad_attn_out = lax.ppermute(
        middle[:, 3 * share : 4 * share], ("rows", "tm"), [(b, a) for a, b in perm]
    ).astype(F32)
    d_in = middle[:, 4 * share : 4 * share + wide].reshape(depth, size, -1).transpose(1, 0, 2)
    grad_conv_in = (
        exchange_tm(d_in)
        .reshape(size, depth, wide // depth, unit)
        .transpose(1, 2, 0, 3)
        .reshape(depth, wide)
        .astype(F32)
    )
    grad_conv_out = (
        exchange_tm(middle[:, 4 * share + wide :].reshape(size, unit, share))
        .reshape(depth, share)
        .astype(F32)
    )

    g1 = gather_tm((0.5 * d1).astype(BF))
    d_f1_out = mm_tn(s1, g1).astype(BF)
    da1 = (mm_nt(g1, f1_out) * silu_slope(a1)).astype(BF)
    d_f1_in = mm_tn(h1, da1).astype(BF)
    grad_ffn1_in, grad_ffn1_out = ffn_return(d_f1_in, d_f1_out, ffn1_in.shape, ffn1_out.shape)
    back, gain_one = norm_back(
        scatter_tm(mm_nt(da1, f1_in).astype(BF)), normed_one, inverse_one, norm_gains[0]
    )
    grad_frames = (d1 + back).astype(BF)[None]

    table_row = lax.dynamic_update_slice_in_dim(
        jnp.zeros(rel_table.shape, F32), d_table, t * heads, 0
    ).reshape(1, -1)
    table_row = jnp.pad(table_row, ((0, 0), (0, width - table_row.shape[1])))
    small = jnp.concatenate(
        [
            jnp.stack([gain_one, gain_two, gain_three, gain_four, gain_five]),
            placed(jnp.stack(d_kernel)),
            placed(bn_part),
            table_row,
        ],
        axis=0,
    )
    small = sum_axis(sum_axis(small, "tm"), "rows")
    table_size = rel_table.shape[0] * rel_table.shape[1]
    return (
        output,
        grad_frames,
        grad_ffn1_in,
        grad_ffn1_out,
        grad_query,
        grad_key,
        grad_value,
        grad_attn_out,
        grad_conv_in,
        grad_conv_out,
        grad_ffn2_in,
        grad_ffn2_out,
        small[:5],
        small[5 : 5 + taps],
        small[6 + taps],
        small[5 + taps],
        small[7 + taps, :table_size].reshape(rel_table.shape),
    )


def solution(mesh):
    split, copied = P("rows", "tm"), P()
    sequence = P("rows", "tm", None)
    return jax.shard_map(
        shards,
        mesh=mesh,
        in_specs=(sequence, P("rows", None)) + (split,) * 10 + (copied,) * 5 + (sequence,),
        out_specs=(sequence, sequence) + (split,) * 10 + (copied,) * 5,
        check_vma=False,
    )
```

```python
import functools

import jax
import jax.numpy as jnp
from jax import lax
from jax.experimental import pallas as pl
from jax.experimental.pallas import tpu as pltpu
from jax.sharding import PartitionSpec as P

HEAD_DIM = 128
RELMAX = 8
LANES = 128
EPS = 1e-05
BF = jnp.bfloat16
F32 = jnp.float32


def mm(a, b):
    return jnp.dot(a, b, preferred_element_type=F32)


def mm_tn(a, b):
    return lax.dot_general(a, b, (((0,), (0,)), ((), ())), preferred_element_type=F32)


def mm_nt(a, b):
    return lax.dot_general(a, b, (((1,), (1,)), ((), ())), preferred_element_type=F32)


def silu_slope(a):
    s = jax.nn.sigmoid(a)
    return s * (1.0 + a * (1.0 - s))


def norm_rows(v, g):
    center = v - jnp.mean(v, axis=-1, keepdims=True)
    spread = jnp.mean(center * center, axis=-1, keepdims=True)
    inverse = lax.rsqrt(spread + EPS)
    normed = center * inverse
    return normed * g, normed, inverse


def norm_back(grad, normed, inverse, g):
    scaled = grad * g
    back = inverse * (
        scaled
        - jnp.mean(scaled, axis=-1, keepdims=True)
        - normed * jnp.mean(scaled * normed, axis=-1, keepdims=True)
    )
    return back, jnp.sum(grad * normed, axis=0)


def tm_peer(dx, dc):
    size = lax.axis_size("tm")
    chips = size // 2
    return [
        (((t // 2 + dx) % chips) * 2 + ((t % 2) ^ dc), t) for t in range(size)
    ]


def from_peer(a, dx, dc):
    return lax.ppermute(a, "tm", tm_peer(dx, dc))


def peer_index(dx, dc):
    chips = lax.axis_size("tm") // 2
    t = lax.axis_index("tm")
    return lax.rem(t // 2 + dx, chips) * 2 + jnp.bitwise_xor(t % 2, dc)


def gather_tm(a):
    size = lax.axis_size("tm")
    n, w = a.shape
    far = [from_peer(a, dx, 0) for dx in range(1, size // 2)]
    held = {(0, 0): a, (0, 1): from_peer(a, 0, 1)}
    for dx, b in enumerate(far, 1):
        held[dx, 0] = b
        held[dx, 1] = from_peer(b, 0, 1)
    out = jnp.zeros((size, n, w), a.dtype)
    for (dx, dc), b in held.items():
        out = lax.dynamic_update_index_in_dim(out, b, peer_index(dx, dc), 0)
    return out.reshape(size * n, w)


def scatter_tm(p, beside=()):
    size = lax.axis_size("tm")
    chips = size // 2
    t = lax.axis_index("tm")
    x, c = t // 2, t % 2
    w = p.shape[1]
    p = p.reshape(chips, 2, p.shape[0] // size, w)
    mine = lax.dynamic_index_in_dim(p, c, 1, keepdims=False)
    theirs = lax.dynamic_index_in_dim(p, 1 - c, 1, keepdims=False).astype(BF)
    q = mine.astype(F32) + from_peer(theirs, 0, 1).astype(F32)
    total = lax.dynamic_index_in_dim(q, x, 0, keepdims=False)
    for dx in range(1, chips):
        piece = lax.dynamic_index_in_dim(q, lax.rem(x + chips - dx, chips), 0, keepdims=False)
        total = total + after(from_peer(piece.astype(BF), dx, 0), *beside).astype(F32)
    return total


def spread(a, local):
    chips = lax.axis_size("tm") // 2
    far = [from_peer(a, dx, 0) for dx in range(1, chips)]
    near = (a, from_peer(a, 0, 1))
    done = local(near)
    far = [after(b, *jax.tree.leaves(done)) for b in far]
    return [near] + [(b, from_peer(b, 0, 1)) for b in far], done


def collect(mine, theirs, beside=()):
    chips = lax.axis_size("tm") // 2
    got = []
    for dx in range(1, chips):
        q = mine[dx] + from_peer(theirs[dx], 0, 1).astype(F32)
        got.append(from_peer(q.astype(BF), chips - dx, 0))
    near = from_peer(theirs[0], 0, 1)
    got = [after(v, near, *beside) for v in got]
    return [mine[0], near] + got


def exchange_tm(pieces):
    size = lax.axis_size("tm")
    chips = size // 2
    t = lax.axis_index("tm")
    out = jnp.zeros(pieces.shape, pieces.dtype)
    out = lax.dynamic_update_index_in_dim(
        out, lax.dynamic_index_in_dim(pieces, t, 0, keepdims=False), t, 0
    )
    for dx in range(chips):
        for dc in range(2):
            if dx or dc:
                piece = lax.dynamic_index_in_dim(
                    pieces, peer_index(chips - dx, dc), 0, keepdims=False
                )
                out = lax.dynamic_update_index_in_dim(
                    out, from_peer(piece, dx, dc), peer_index(dx, dc), 0
                )
    return out


def sum_axis(v, axis):
    size, bit = lax.axis_size(axis), 1
    while bit < size:
        v = v + lax.ppermute(v, axis, [(i, i ^ bit) for i in range(size)])
        bit *= 2
    return v


def pack(a, width):
    m, w = a.shape
    f = width // w
    if f * w != width or m % f:
        return a.reshape(-1, width)
    return jnp.concatenate([a[i * (m // f) : (i + 1) * (m // f)] for i in range(f)], axis=1)


def unpack(full, w):
    rows, n, width = full.shape
    f = width // w
    if f * w != width:
        return full.reshape(-1, w)
    if f == 1:
        return full.reshape(-1, w)
    parts = [full[:, None, :, i * w : (i + 1) * w] for i in range(f)]
    return jnp.concatenate(parts, axis=1).reshape(-1, w)


def gather_rows(parts):
    width = max(p.shape[1] for p in parts)
    packed = [pack(p, width) for p in parts]
    full = lax.all_gather(jnp.concatenate(packed, axis=0), "rows", axis=0, tiled=False)
    out, at = [], 0
    for p, q in zip(parts, packed):
        out.append(unpack(full[:, at : at + q.shape[0]], p.shape[1]))
        at += q.shape[0]
    return out


def pack_rows(p, width):
    rows = lax.axis_size("rows")
    m, w = p.shape[0] // rows, p.shape[1]
    f = width // w
    q = p.reshape(rows, m, w)
    if f * w != width or m % f:
        return q.reshape(rows, -1, width)
    return jnp.concatenate([q[:, i * (m // f) : (i + 1) * (m // f)] for i in range(f)], axis=2)


def pack_grads(parts):
    width = max(p.shape[1] for p in parts)
    return jnp.concatenate([pack_rows(p, width) for p in parts], axis=1)


def unpack_grads(total, parts):
    rows = lax.axis_size("rows")
    width = total.shape[1]
    out, at = [], 0
    for p in parts:
        n = p.size // (rows * width)
        out.append(unpack(total[None, at : at + n], p.shape[1]))
        at += n
    return out


def scatter_rows(packed):
    return lax.psum_scatter(packed, "rows", scatter_dimension=0, tiled=False)


def scatter_rows_near(packed):
    got = lax.all_to_all(packed, "rows", 0, 0, tiled=True)
    return jnp.sum(got.astype(F32), axis=0).astype(BF)


def gather_weights(pair, more=None):
    parts = list(pair) + ([] if more is None else [more])
    m, width = parts[0].shape
    if all(p.shape == (m, width) for p in parts) and m % 16 == 0:
        full = lax.all_gather(jnp.concatenate(parts, axis=0), "rows", axis=0, tiled=False)
        out = [Weight(full, i * m, m) for i in range(len(parts))]
    else:
        out = [Weight(lax.all_gather(p, "rows", axis=0, tiled=True)) for p in parts]
    return (out[:2], out[2]) if more is not None else out


def exchange_all(pieces):
    size = lax.axis_size("tm")
    width = max(p.shape[2] for p in pieces)
    if any(p[0].size % width for p in pieces):
        return [exchange_tm(p) for p in pieces]
    flat = [p.reshape(size, -1, width) for p in pieces]
    got = exchange_tm(jnp.concatenate(flat, axis=1))
    out, at = [], 0
    for p, q in zip(pieces, flat):
        out.append(got[:, at : at + q.shape[1]].reshape(p.shape))
        at += q.shape[1]
    return out


def after(a, *others):
    return lax.optimization_barrier((a,) + others)[0]


def ffn_pieces(w_in, w_out):
    size = lax.axis_size("tm")
    unit = w_out.shape[0] // size
    m, w = w_in.shape
    a = w_in.reshape(m, w // (size * unit), size, unit).transpose(2, 0, 1, 3)
    return [a.reshape(size, m, w // size), w_out.reshape(size, unit, w_out.shape[1])]


def side_by_side(pieces):
    return pieces.transpose(1, 0, 2).reshape(pieces.shape[1], -1)


def ffn_return(a, b, like_in, like_out):
    size = lax.axis_size("tm")
    a = a.reshape(a.shape[0], size, -1).transpose(1, 0, 2)
    b = b.reshape(b.shape[0], size, -1).transpose(1, 0, 2)
    a, b = exchange_all([a, b])
    unit = like_out[0] // size
    m, w = like_in
    a = a.reshape(size, m, w // (size * unit), unit).transpose(1, 2, 0, 3).reshape(m, w)
    return a.astype(F32), b.reshape(like_out).astype(F32)


def head_rows_perm():
    rows, size = lax.axis_size("rows"), lax.axis_size("tm")
    perm = []
    for r in range(rows):
        for t in range(size):
            k, u = divmod(r, size)
            perm.append(((t * (rows // size) + k) * size + u, r * size + t))
    return perm


def params(limit):
    return pltpu.CompilerParams(vmem_limit_bytes=limit * 1024 * 1024)


def whole(shape):
    return pl.BlockSpec(shape, lambda *_: (0,) * len(shape))


def flat(v):
    return v.reshape(-1, v.shape[-1])


def cost(flops, *arrays):
    return pl.CostEstimate(
        flops=flops, bytes_accessed=sum(a.size * a.dtype.itemsize for a in arrays), transcendentals=0
    )


class Weight:
    def __init__(self, array, first=0, m=None):
        self.array, self.first, self.m = array, first, m
        if m is not None:
            self.shape = (array.shape[0] * m, array.shape[2])
        else:
            self.shape = array.shape

    def all(self):
        if self.m is None:
            return whole(self.shape)
        unit = self.first // self.m
        return pl.BlockSpec(
            (self.array.shape[0], self.m, self.shape[1]), lambda *_: (0, unit, 0)
        )

    def value(self):
        if self.m is None:
            return self.array
        return flat(self.array[:, self.first : self.first + self.m])


def ffn_kernel(h0, h1, w_in, w_out, s_ref, slope_ref, mine, theirs):
    n = h0.shape[0]
    h = jnp.concatenate([h0[...], h1[...]], axis=0)
    w_a, w_b = flat(w_in[...]), flat(w_out[...])
    units = w_a.shape[1]
    total = None
    for half in range(2):
        at = slice(half * units // 2, (half + 1) * units // 2)
        a = mm(h, w_a[:, at])
        sig = jax.nn.sigmoid(a)
        act = (a * sig).astype(BF)
        s_ref[:, at] = act
        slope_ref[:, at] = (sig * (1.0 + a * (1.0 - sig))).astype(BF)
        p = mm(act, w_b[at])
        total = p if total is None else total + p
    mine[...] = total[:n]
    theirs[...] = total[n:].astype(BF)


def ffn(pair, w_in, w_out):
    n, d = pair[0].shape
    units = w_in.shape[1]
    return pl.pallas_call(
        ffn_kernel,
        grid=(1,),
        in_specs=[whole((n, d)), whole((n, d)), w_in.all(), w_out.all()],
        out_specs=[whole((2 * n, units))] * 2 + [whole((n, d))] * 2,
        out_shape=[jax.ShapeDtypeStruct((2 * n, units), BF)] * 2
        + [jax.ShapeDtypeStruct((n, d), F32), jax.ShapeDtypeStruct((n, d), BF)],
        compiler_params=params(24),
        cost_estimate=cost(8 * n * d * units, w_in.array),
    )(*pair, w_in.array, w_out.array)


def ffn_back_kernel(g0, g1, slope, w_in, w_out, da_ref, mine, theirs):
    n = g0.shape[0]
    g = jnp.concatenate([g0[...], g1[...]], axis=0)
    w_a, w_b = flat(w_in[...]), flat(w_out[...])
    units = w_a.shape[1]
    total = None
    for half in range(2):
        at = slice(half * units // 2, (half + 1) * units // 2)
        da = (mm_nt(g, w_b[at]) * slope[:, at].astype(F32)).astype(BF)
        da_ref[:, at] = da
        p = mm_nt(da, w_a[:, at])
        total = p if total is None else total + p
    mine[...] = total[:n]
    theirs[...] = total[n:].astype(BF)


def ffn_back(pair, slope, w_in, w_out):
    n, d = pair[0].shape
    units = w_in.shape[1]
    return pl.pallas_call(
        ffn_back_kernel,
        grid=(1,),
        in_specs=[whole((n, d))] * 2 + [whole((2 * n, units)), w_in.all(), w_out.all()],
        out_specs=[whole((2 * n, units))] + [whole((n, d))] * 2,
        out_shape=[
            jax.ShapeDtypeStruct((2 * n, units), BF),
            jax.ShapeDtypeStruct((n, d), F32),
            jax.ShapeDtypeStruct((n, d), BF),
        ],
        compiler_params=params(24),
        cost_estimate=cost(8 * n * d * units, w_in.array),
    )(*pair, slope, w_in.array, w_out.array)


def ffn_grads_kernel(*refs):
    out = refs[-1]
    count = (len(refs) - 1) // 6
    h, g = refs[: 2 * count], refs[2 * count : 4 * count]
    da, s = refs[4 * count : 5 * count], refs[5 * count : 6 * count]
    half = out.shape[1] // 2
    join = lambda v: jnp.concatenate([r[...] for r in v], axis=0)
    out[:, :half, :] = mm_tn(join(h), join(da)).astype(BF).reshape(out.shape[0], half, -1)
    out[:, half:, :] = mm_tn(join(s), join(g)).astype(BF).reshape(out.shape[0], half, -1)


def ffn_grads(h, g, da, s):
    rows = lax.axis_size("rows")
    n, d = h[0].shape
    units, tile = da[0].shape[1], d // 2
    m = d // rows
    if units != d or tile % m:
        h, g, da, s = (jnp.concatenate(v, axis=0) for v in (h, g, da, s))
        return pack_grads([mm_tn(h, da).astype(BF), mm_tn(s, g).astype(BF)])
    part = pl.BlockSpec((n, tile), lambda j: (0, j))
    column = pl.BlockSpec((2 * n, tile), lambda j: (0, j))
    return pl.pallas_call(
        ffn_grads_kernel,
        grid=(d // tile,),
        in_specs=[part] * len(h)
        + [whole((n, d))] * len(g)
        + [whole((2 * n, units))] * len(da)
        + [column] * len(s),
        out_specs=pl.BlockSpec((tile // m, 2 * m, d), lambda j: (j, 0, 0)),
        out_shape=jax.ShapeDtypeStruct((rows, 2 * m, d), BF),
        compiler_params=params(36),
        cost_estimate=cost(4 * len(h) * n * d * units, *h),
    )(*h, *g, *da, *s)


def add_norm_kernel(*refs, scale):
    x_ref, gain, x_new, h_ref = refs[-4:]
    total = refs[0][...]
    for r in refs[1:-4]:
        total = total + r[...].astype(F32)
    x = x_ref[...] + scale * total
    x_new[...] = x
    h_ref[...] = norm_rows(x, gain[...])[0].astype(BF)


def add_norm(parts, x, gain, scale):
    n, d = x.shape
    return pl.pallas_call(
        functools.partial(add_norm_kernel, scale=scale),
        out_shape=[jax.ShapeDtypeStruct((n, d), F32), jax.ShapeDtypeStruct((n, d), BF)],
        compiler_params=params(12),
        cost_estimate=cost(0, x, x, x),
    )(*parts, x, gain[None])


def turn_kernel(*refs):
    x_ref, gain, cot, out, d_ref, g_ref, gain_ref = refs[-7:]
    total = refs[0][...]
    for r in refs[1:-7]:
        total = total + r[...].astype(F32)
    y, normed, inverse = norm_rows(x_ref[...] + 0.5 * total, gain[...])
    out[...] = y.astype(BF)
    back, gain_sum = norm_back(cot[...].astype(F32), normed, inverse, gain[...])
    d_ref[...] = back
    g_ref[...] = (0.5 * back).astype(BF)
    gain_ref[...] = gain_sum[None]


def turn(parts, x, gain, cot):
    n, d = x.shape
    return pl.pallas_call(
        turn_kernel,
        out_shape=[
            jax.ShapeDtypeStruct((n, d), BF),
            jax.ShapeDtypeStruct((n, d), F32),
            jax.ShapeDtypeStruct((n, d), BF),
            jax.ShapeDtypeStruct((1, d), F32),
        ],
        compiler_params=params(14),
        cost_estimate=cost(0, x, x, x),
    )(*parts, x, gain[None], cot)


def back_norm_kernel(*refs, scale):
    x_ref, gain, prev, d_ref, g_ref, gain_ref = refs[-6:]
    total = refs[0][...]
    for r in refs[1:-6]:
        total = total + r[...].astype(F32)
    _, normed, inverse = norm_rows(x_ref[...], gain[...])
    back, gain_sum = norm_back(total, normed, inverse, gain[...])
    d = prev[...] + back
    d_ref[...] = d
    g_ref[...] = (scale * d).astype(BF)
    gain_ref[...] = gain_sum[None]


def back_norm(parts, x, gain, prev, scale):
    n, d = x.shape
    return pl.pallas_call(
        functools.partial(back_norm_kernel, scale=scale),
        out_shape=[
            jax.ShapeDtypeStruct((n, d), F32),
            jax.ShapeDtypeStruct((n, d), BF),
            jax.ShapeDtypeStruct((1, d), F32),
        ],
        compiler_params=params(14),
        cost_estimate=cost(0, x, x, x),
    )(*parts, x, gain[None], prev)


def project_kernel(h0, h1, w, out):
    h = jnp.concatenate([h0[...], h1[...]], axis=0)
    out[...] = mm(h, flat(w[...])[:, : out.shape[1]]).astype(BF)


def project(pair, w, width):
    n, d = pair[0].shape
    return pl.pallas_call(
        project_kernel,
        grid=(1,),
        in_specs=[whole((n, d)), whole((n, d)), w.all()],
        out_specs=whole((2 * n, width)),
        out_shape=jax.ShapeDtypeStruct((2 * n, width), BF),
        compiler_params=params(20),
        cost_estimate=cost(4 * n * d * width, w.array),
    )(*pair, w.array)


def joined(v, size, depth):
    groups = v.shape[0] // (size * depth)
    cut = lambda k, u: v[(k * size + u) * depth : (k * size + u + 1) * depth]
    return jnp.concatenate(
        [jnp.concatenate([cut(k, u) for u in range(size)], axis=1) for k in range(groups)], axis=0
    )


def fill_bias(tab_ref, head, strip, length):
    lo, hi = length - LANES, length + 2 * LANES
    first, last = tab_ref[head, 0], tab_ref[head, 2 * RELMAX]
    offset = (
        lax.broadcasted_iota(jnp.int32, (LANES, hi - lo), 1)
        - LANES
        - lax.broadcasted_iota(jnp.int32, (LANES, hi - lo), 0)
    )
    tile = jnp.where(offset <= -RELMAX, first, last)
    for b in range(1, 2 * RELMAX):
        tile = jnp.where(offset == b - RELMAX, tab_ref[head, b], tile)
    strip[:, :lo] = jnp.full((LANES, lo), first, F32)
    strip[:, lo:hi] = tile
    strip[:, hi:] = jnp.full((LANES, 2 * length - hi), last, F32)


def biased(q, k, seg_col, seg_row, strip, first, length):
    raw = mm_nt(q, k) * HEAD_DIM ** (-0.5)
    parts = [
        strip[:, length - (first + a) : 2 * length - (first + a)]
        for a in range(0, q.shape[0], LANES)
    ]
    bias = parts[0] if len(parts) == 1 else jnp.concatenate(parts, axis=0)
    return jnp.where(seg_col == seg_row, raw + bias, -jnp.inf)


def head_columns(n, head, heads):
    return pl.ds(pl.multiple_of((n * heads + head) * HEAD_DIM, HEAD_DIM), HEAD_DIM)


def attend_kernel(order, tab_ref, seg_row_ref, seg_col_ref, w_ref, *refs, size, depth):
    chips = size // 2
    pairs, (qkv, att, lse_ref) = refs[:chips], refs[chips : chips + 3]
    mine, theirs = refs[chips + 3 : 2 * chips + 3], refs[2 * chips + 3 : 3 * chips + 3]
    strip = refs[-1]
    length = qkv.shape[0]
    n = length // size
    head, heads = pl.program_id(0), pl.num_programs(0)
    at = lambda i: pl.ds(pl.multiple_of(order[i] * n, n), n)

    @pl.when(head == 0)
    def _():
        for i in range(size):
            qkv[at(i), :] = pairs[i // 2][(i % 2) * n : (i % 2 + 1) * n, :]

    fill_bias(tab_ref, head, strip, length)
    k, v = qkv[:, head_columns(1, head, heads)], qkv[:, head_columns(2, head, heads)]
    block = min(256, length)
    for first in range(0, length, block):
        own = slice(first, first + block)
        q = qkv[own, head_columns(0, head, heads)]
        sc = biased(q, k, seg_col_ref[own, :], seg_row_ref[...], strip, first, length)
        peak = jnp.max(sc, axis=1, keepdims=True)
        e = jnp.exp(sc - peak)
        total = jnp.sum(e, axis=1, keepdims=True)
        p = (e * (1.0 / total)).astype(BF)
        att[own, head_columns(0, head, heads)] = mm(p, v).astype(BF)
        lse_ref[0, own, :] = peak + jnp.log(total)

    @pl.when(head == heads - 1)
    def _():
        share = att.shape[1]
        w = joined(flat(w_ref[...])[:, -share:], size, depth)
        for i in range(size):
            p = mm(att[at(i), :], w)
            if i % 2:
                theirs[i // 2][...] = p.astype(BF)
            else:
                mine[i // 2][...] = p


def attend(order, pairs, seg_row, table, weight):
    size = 2 * len(pairs)
    length, heads = seg_row.shape[0], table.shape[0]
    share, d = heads * HEAD_DIM, weight.shape[0]
    n = length // size
    depth = d // lax.axis_size("rows")
    shape = jax.ShapeDtypeStruct
    out = pl.pallas_call(
        functools.partial(attend_kernel, size=size, depth=depth),
        grid=(heads,),
        in_specs=[
            pl.BlockSpec(memory_space=pltpu.SMEM),
            pl.BlockSpec(memory_space=pltpu.SMEM),
            whole((1, length)),
            whole((length, 1)),
            weight.all(),
        ]
        + [whole((2 * n, 3 * share))] * len(pairs),
        out_specs=[
            whole((length, 3 * share)),
            whole((length, share)),
            pl.BlockSpec((1, length, 1), lambda h: (h, 0, 0)),
        ]
        + [whole((n, d))] * size,
        out_shape=[
            shape((length, 3 * share), BF),
            shape((length, share), BF),
            shape((heads, length, 1), F32),
        ]
        + [shape((n, d), F32)] * len(pairs)
        + [shape((n, d), BF)] * len(pairs),
        scratch_shapes=[pltpu.VMEM((LANES, 2 * length), F32)],
        compiler_params=params(32),
        cost_estimate=cost(6 * length * length * share, *pairs),
    )(order, table, seg_row.reshape(1, length), seg_row.reshape(length, 1), weight.array, *pairs)
    chips = len(pairs)
    return out[0], out[1], out[2], out[3 : 3 + chips], out[3 + chips :]


def att_grad_kernel(g0, g1, w_ref, out, *, size, depth):
    share = out.shape[1]
    w = joined(flat(w_ref[...])[:, -share:], size, depth)
    g = jnp.concatenate([g0[...], g1[...]], axis=0)
    out[...] = mm_nt(g, w).astype(BF)


def att_grad(pair, weight, share):
    n, d = pair[0].shape
    return pl.pallas_call(
        functools.partial(
            att_grad_kernel, size=lax.axis_size("tm"), depth=d // lax.axis_size("rows")
        ),
        grid=(1,),
        in_specs=[whole((n, d)), whole((n, d)), weight.all()],
        out_specs=whole((2 * n, share)),
        out_shape=jax.ShapeDtypeStruct((2 * n, share), BF),
        compiler_params=params(16),
        cost_estimate=cost(4 * n * d * share, weight.array),
    )(*pair, weight.array)


def attend_back_kernel(
    order, tab_ref, seg_row_ref, seg_col_ref, w_ref, qkv, lse_ref, *refs, size
):
    chips = size // 2
    pairs, (dqkv_ref, band_ref) = refs[:chips], refs[chips : chips + 2]
    mine, theirs = refs[chips + 2 : 2 * chips + 2], refs[2 * chips + 2 : 3 * chips + 2]
    strip, dk_sum, dv_sum, grad = refs[-4:]
    length = qkv.shape[0]
    n = length // size
    block = min(256, length)
    head, heads = pl.program_id(0), pl.num_programs(0)
    rows_of = lambda i: pl.ds(pl.multiple_of(order[i] * n, n), n)

    @pl.when(head == 0)
    def _():
        for i in range(size):
            grad[rows_of(i), :] = pairs[i // 2][(i % 2) * n : (i % 2 + 1) * n, :]

    fill_bias(tab_ref, head, strip, length)
    k, v = qkv[:, head_columns(1, head, heads)], qkv[:, head_columns(2, head, heads)]
    scale = HEAD_DIM ** (-0.5)
    at = lambda n: head_columns(n, head, heads)
    low = jnp.zeros((LANES, LANES), F32)
    high = jnp.zeros((LANES, LANES), F32)
    band = [jnp.zeros((LANES, LANES), F32) for _ in range(3)]
    for first in range(0, length, block):
        own = slice(first, first + block)
        q, do = qkv[own, at(0)], grad[own, at(0)]
        sc = biased(q, k, seg_col_ref[own, :], seg_row_ref[...], strip, first, length)
        p = jnp.exp(sc - lse_ref[0, own, :])
        dp = mm_nt(do, v)
        inner = jnp.sum(p * dp, axis=1, keepdims=True)
        ds = (p * (dp - inner)).astype(BF)
        dv = mm_tn(p.astype(BF), do)
        dk = mm_tn(ds, q)
        if first == 0:
            dv_sum[...] = dv
            dk_sum[...] = dk
        else:
            dv_sum[...] += dv
            dk_sum[...] += dk
        dqkv_ref[own, at(0)] = (mm(ds, k) * scale).astype(BF)
        wide = ds.astype(F32)
        for a in range(0, block, LANES):
            for b in range(0, length, LANES):
                part = wide[a : a + LANES, b : b + LANES]
                apart = (b - first - a) // LANES
                if apart < -1:
                    low = low + part
                elif apart > 1:
                    high = high + part
                else:
                    band[apart + 1] = band[apart + 1] + part
    dqkv_ref[:, at(1)] = (dk_sum[...] * scale).astype(BF)
    dqkv_ref[:, at(2)] = dv_sum[...].astype(BF)
    for i, part in enumerate([low] + band + [high]):
        band_ref[0, :, i * LANES : (i + 1) * LANES] = part

    @pl.when(head == heads - 1)
    def _():
        w = flat(w_ref[...])[:, : dqkv_ref.shape[1]]
        for i in range(size):
            p = mm_nt(dqkv_ref[rows_of(i), :], w)
            if i % 2:
                theirs[i // 2][...] = p.astype(BF)
            else:
                mine[i // 2][...] = p


def attend_back(order, pairs, qkv, seg_row, table, lse, weight):
    size = 2 * len(pairs)
    length, heads = qkv.shape[0], table.shape[0]
    share, d = heads * HEAD_DIM, weight.shape[0]
    n = length // size
    shape = jax.ShapeDtypeStruct
    out = pl.pallas_call(
        functools.partial(attend_back_kernel, size=size),
        grid=(heads,),
        in_specs=[
            pl.BlockSpec(memory_space=pltpu.SMEM),
            pl.BlockSpec(memory_space=pltpu.SMEM),
            whole((1, length)),
            whole((length, 1)),
            weight.all(),
            whole((length, 3 * share)),
            pl.BlockSpec((1, length, 1), lambda h: (h, 0, 0)),
        ]
        + [whole((2 * n, share))] * len(pairs),
        out_specs=[
            whole((length, 3 * share)),
            pl.BlockSpec((1, LANES, 5 * LANES), lambda h: (h, 0, 0)),
        ]
        + [whole((n, d))] * size,
        out_shape=[
            shape((length, 3 * share), BF),
            shape((heads, LANES, 5 * LANES), F32),
        ]
        + [shape((n, d), F32)] * len(pairs)
        + [shape((n, d), BF)] * len(pairs),
        scratch_shapes=[
            pltpu.VMEM((LANES, 2 * length), F32),
            pltpu.VMEM((length, HEAD_DIM), F32),
            pltpu.VMEM((length, HEAD_DIM), F32),
            pltpu.VMEM((length, share), BF),
        ],
        compiler_params=params(36),
        cost_estimate=cost(12 * length * length * share, *pairs),
    )(
        order,
        table,
        seg_row.reshape(1, length),
        seg_row.reshape(length, 1),
        weight.array,
        qkv,
        lse,
        *pairs,
    )
    chips = len(pairs)
    return out[0], out[1], out[2 : 2 + chips], out[2 + chips :]


def table_grad(band):
    offset = (
        lax.broadcasted_iota(jnp.int32, (LANES, 3 * LANES), 1)
        - LANES
        - lax.broadcasted_iota(jnp.int32, (LANES, 3 * LANES), 0)
    )
    middle = band[:, :, LANES : 4 * LANES]
    inner = [
        jnp.sum(jnp.where(offset == b, middle, 0.0), axis=(1, 2)) for b in range(1 - RELMAX, RELMAX)
    ]
    lower = jnp.sum(jnp.where(offset <= -RELMAX, middle, 0.0), axis=(1, 2))
    upper = jnp.sum(jnp.where(offset >= RELMAX, middle, 0.0), axis=(1, 2))
    lower = lower + jnp.sum(band[:, :, :LANES], axis=(1, 2))
    upper = upper + jnp.sum(band[:, :, 4 * LANES :], axis=(1, 2))
    return jnp.stack([lower] + inner + [upper], axis=1)


def attend_grads_kernel(order, dqkv, att, *refs):
    out, h_all, g_all = refs[-3:]
    size = (len(refs) - 3) // 2
    h, g = refs[:size], refs[size : 2 * size]
    n = h[0].shape[0]
    wide = dqkv.shape[1]
    for i in range(size):
        at = pl.ds(pl.multiple_of(order[i] * n, n), n)
        h_all[at, :] = h[i][...]
        g_all[at, :] = g[i][...]
    first = mm_tn(h_all[...], dqkv[...]).astype(BF)
    out[:, :, :wide] = first.reshape(out.shape[0], out.shape[1], wide)
    second = mm_tn(att[...], g_all[...]).astype(BF)
    depth, share = out.shape[1], out.shape[2] - wide
    per = second.shape[1] // share
    for i in range(out.shape[0]):
        k, u = divmod(i, per)
        out[i, :, wide:] = second[k * depth : (k + 1) * depth, u * share : (u + 1) * share]


def attend_grads(order, h, g, dqkv, att):
    rows, size = lax.axis_size("rows"), lax.axis_size("tm")
    n, d = h[0].shape
    length, share = att.shape
    m = d // rows
    if share != 2 * m:
        def place(chunks):
            out = jnp.zeros((size, n, d), BF)
            for i, v in enumerate(chunks):
                out = lax.dynamic_update_index_in_dim(out, v, order[i], 0)
            return out.reshape(length, d)

        first = mm_tn(place(h), dqkv).astype(BF)
        second = mm_tn(att, place(g)).astype(BF)
        second = (
            second.reshape(rows // size, m, size, share).transpose(0, 2, 1, 3).reshape(d, share)
        )
        return jnp.concatenate([first, second], axis=1).reshape(rows, m, -1)
    return pl.pallas_call(
        attend_grads_kernel,
        grid=(1,),
        in_specs=[
            pl.BlockSpec(memory_space=pltpu.SMEM),
            whole(dqkv.shape),
            whole(att.shape),
        ]
        + [whole((n, d))] * (2 * size),
        out_specs=whole((rows, m, 4 * share)),
        out_shape=jax.ShapeDtypeStruct((rows, m, 4 * share), BF),
        scratch_shapes=[pltpu.VMEM((length, d), BF)] * 2,
        compiler_params=params(28),
        cost_estimate=cost(8 * length * d * share, *h),
    )(order, dqkv, att, *h, *g)


def shards(
    frames,
    segments,
    ffn1_in,
    ffn1_out,
    query_w,
    key_w,
    value_w,
    attn_out,
    conv_in,
    conv_out,
    ffn2_in,
    ffn2_out,
    norm_gains,
    conv_kernel,
    bn_gain,
    bn_bias,
    rel_table,
    cotangent,
):
    rows, size = lax.axis_size("rows"), lax.axis_size("tm")
    t = lax.axis_index("tm")
    own, width = frames.shape[1], frames.shape[2]
    length = own * size
    share = width // size
    heads = rel_table.shape[0] // size
    taps = conv_kernel.shape[0]
    reach = taps // 2
    frame_total = float(length * rows)
    seg = segments[0]
    table = lax.dynamic_slice_in_dim(rel_table, t * heads, heads, 0)
    depth = width // rows
    unit = depth // size

    def mine(v):
        v = v.reshape(-1, rows, size, unit)
        return lax.dynamic_index_in_dim(v, t, 2, keepdims=False).reshape(-1, share)

    def placed(v):
        n = v.shape[0]
        out = jnp.zeros((n, rows, size, unit), F32)
        return lax.dynamic_update_index_in_dim(
            out, v.reshape(n, rows, unit), t, 2
        ).reshape(n, width)

    kernel_own = mine(conv_kernel)
    bn_gain_own, bn_bias_own = mine(bn_gain[None]), mine(bn_bias[None])

    perm = head_rows_perm()
    out_block = lax.ppermute(attn_out, ("rows", "tm"), perm)
    order = jnp.stack(
        [peer_index(dx, dc) for dx in range(size // 2) for dc in range(2)]
    ).astype(jnp.int32)
    f1, attn_w = gather_weights(
        [side_by_side(p) for p in exchange_all(ffn_pieces(ffn1_in, ffn1_out))],
        jnp.concatenate([query_w, key_w, value_w, out_block], axis=1),
    )
    wide = conv_in.shape[1]
    later = exchange_all(
        ffn_pieces(ffn2_in, ffn2_out)
        + [
            conv_in.reshape(depth, wide // depth, size, unit)
            .transpose(2, 0, 1, 3)
            .reshape(size, depth, wide // size),
            conv_out.reshape(size, unit, share),
        ]
    )
    later = [side_by_side(p) for p in later]
    f2_in, f2_out, conv_in_w, conv_out_w = gather_rows(later)
    f2 = (Weight(f2_in), Weight(f2_out))

    inputs = frames[0].astype(F32)
    n1 = norm_rows(inputs, norm_gains[0])[0]
    h1, _ = spread(n1.astype(BF), lambda near: ())
    h1[0] = (after(h1[0][0], *later), h1[0][1])
    one = [ffn(pair, *f1) for pair in reversed(h1)][::-1]
    parts = collect([v[2] for v in one], [v[3] for v in one])
    x1, n2 = add_norm(parts, inputs, norm_gains[1], 0.5)

    h2, local = spread(n2, lambda near: project(near, attn_w, 3 * share))
    pairs = [local] + [project(pair, attn_w, 3 * share) for pair in h2[1:]]
    qkv, att, lse, mine, theirs = attend(order, pairs, seg, table, attn_w)
    x2, n3 = add_norm(collect(mine, theirs), x1, norm_gains[2], 1.0)

    h3 = gather_tm(n3)
    u = mm(h3, conv_in_w)
    u_lin, u_sig = u[:, :share], jax.nn.sigmoid(u[:, share:])
    z = (u_lin * u_sig).astype(BF)
    seg_pad = jnp.pad(seg, (reach, reach), constant_values=-1)
    same = [(seg_pad[k : k + length] == seg)[:, None] for k in range(taps)]

    def shifted_rows(v):
        v = jnp.pad(v, ((reach, reach), (0, 0)))
        return [v[k : k + length] for k in range(taps)]

    z_near = shifted_rows(z)
    conv = jnp.zeros((length, share), F32)
    for k in range(taps):
        conv = conv + jnp.where(same[k], z_near[k].astype(F32) * kernel_own[k], 0.0)
    moments = sum_axis(
        jnp.stack([jnp.sum(conv, axis=0), jnp.sum(conv * conv, axis=0)]), "rows"
    )
    centre = moments[0] / frame_total
    inverse_bn = lax.rsqrt(moments[1] / frame_total - centre * centre + EPS)
    normed_bn = (conv - centre) * inverse_bn
    shifted = normed_bn * bn_gain_own + bn_bias_own
    e = (shifted * jax.nn.sigmoid(shifted)).astype(BF)
    x3, n4 = add_norm([scatter_tm(mm(e, conv_out_w).astype(BF))], x2, norm_gains[3], 1.0)

    h4, local = spread(n4, lambda near: ffn(near, *f2))
    four = [local] + [ffn(pair, *f2) for pair in h4[1:]]
    parts = collect([v[2] for v in four], [v[3] for v in four])
    output, d4, g, gain_five = turn(parts, x3, norm_gains[4], cotangent[0])

    def ffn_backward(g, h, kept, w, x, gain, prev, scale):
        g, local = spread(g, lambda near: ffn_back(near, kept[0][1], *w))
        back = [local] + [ffn_back(p, kept[i][1], *w) for i, p in enumerate(g[1:], 1)]
        packed = ffn_grads(
            sum(h, ()), sum(g, ()), [v[0] for v in back], [v[0] for v in kept]
        )
        parts = collect([v[1] for v in back], [v[2] for v in back], (packed,))
        return back_norm(parts, x, gain, prev, scale), packed

    (d3, g, gain_four), packed_four = ffn_backward(
        g, h4, four, f2, x3, norm_gains[3], d4, 1.0
    )
    sum_four = scatter_rows(packed_four)

    g3 = gather_tm(g)
    d_conv_out = mm_tn(e, g3).astype(BF)
    dn = mm_nt(g3, conv_out_w) * silu_slope(shifted)
    bn_part = jnp.stack([jnp.sum(dn, axis=0), jnp.sum(dn * normed_bn, axis=0)])
    bn_sums = sum_axis(bn_part, "rows")
    dc = (
        bn_gain_own
        * inverse_bn
        * (dn - bn_sums[0] / frame_total - normed_bn * (bn_sums[1] / frame_total))
    ).astype(BF)
    dc_near = shifted_rows(dc)
    dc_wide = dc.astype(F32)
    dz = jnp.zeros((length, share), F32)
    d_kernel = []
    for k in range(taps):
        mirror = taps - 1 - k
        dz = dz + jnp.where(same[mirror], dc_near[mirror].astype(F32) * kernel_own[k], 0.0)
        d_kernel.append(
            jnp.sum(jnp.where(same[k], z_near[k].astype(F32) * dc_wide, 0.0), axis=0)
        )
    du = jnp.concatenate([dz * u_sig, dz * u_lin * u_sig * (1.0 - u_sig)], axis=1).astype(BF)
    d_conv_in = mm_tn(h3, du).astype(BF)
    parts_three = [d_conv_in, d_conv_out]
    packed_three = pack_grads(parts_three)
    parts_three = [d_conv_in, d_conv_out]
    packed_three = pack_grads(parts_three)
    d2, g, gain_three = back_norm(
        [scatter_tm(mm_nt(du, conv_in_w).astype(BF), (packed_three,))],
        x2,
        norm_gains[2],
        d3,
        1.0,
    )

    g2, local = spread(g, lambda near: att_grad(near, attn_w, share))
    pairs = [local] + [att_grad(pair, attn_w, share) for pair in g2[1:]]
    dqkv, band, mine, theirs = attend_back(order, pairs, qkv, seg, table, lse, attn_w)
    packed_two = attend_grads(order, sum(h2, ()), sum(g2, ()), dqkv, att)
    packed_mid = jnp.concatenate([pack_grads([packed_two.reshape(width, -1)]), packed_three], axis=1) if packed_two.shape[2] == packed_three.shape[2] else None
    parts = collect(mine, theirs, (packed_two,) if packed_mid is None else (packed_mid,))
    d1, g, gain_two = back_norm(parts, x1, norm_gains[1], d2, 0.5)
    if packed_mid is None:
        sum_two, sum_three = scatter_rows(packed_two), scatter_rows(packed_three)
    else:
        sum_mid = scatter_rows(packed_mid)
        sum_two, sum_three = sum_mid[:depth], sum_mid[depth:]

    (grad, _, gain_one), packed_one = ffn_backward(
        g, h1, one, f1, inputs, norm_gains[0], d1, 1.0
    )
    grad_frames = grad.astype(BF)[None]
    sum_one = scatter_rows(packed_one)

    def ffn_parts(total):
        if total.shape == (2 * depth, width) and ffn1_in.shape[1] == width:
            return total[:depth], total[depth:]
        like = [
            jax.ShapeDtypeStruct((width, ffn1_in.shape[1]), BF),
            jax.ShapeDtypeStruct((ffn1_in.shape[1], width), BF),
        ]
        return unpack_grads(total, like)

    grad_ffn2_in, grad_ffn2_out = ffn_return(
        *ffn_parts(sum_four), ffn2_in.shape, ffn2_out.shape
    )
    grad_query, grad_key, grad_value, d_block = (
        sum_two[:, i * share : (i + 1) * share] for i in range(4)
    )
    grad_query, grad_key, grad_value = (v.astype(F32) for v in (grad_query, grad_key, grad_value))
    grad_attn_out = lax.ppermute(d_block, ("rows", "tm"), [(b, a) for a, b in perm]).astype(F32)
    d_in, d_out = unpack_grads(sum_three, parts_three)
    d_in, d_out = exchange_all(
        [
            d_in.reshape(depth, size, -1).transpose(1, 0, 2),
            d_out.reshape(unit, size, share).transpose(1, 0, 2),
        ]
    )
    grad_conv_in = (
        d_in.reshape(size, depth, wide // depth, unit)
        .transpose(1, 2, 0, 3)
        .reshape(depth, wide)
        .astype(F32)
    )
    grad_conv_out = d_out.reshape(depth, share).astype(F32)
    grad_ffn1_in, grad_ffn1_out = ffn_return(
        *ffn_parts(sum_one), ffn1_in.shape, ffn1_out.shape
    )

    table_row = lax.dynamic_update_slice_in_dim(
        jnp.zeros(rel_table.shape, F32), table_grad(band), t * heads, 0
    ).reshape(1, -1)
    table_row = jnp.pad(table_row, ((0, 0), (0, width - table_row.shape[1])))
    small = jnp.concatenate(
        [
            gain_one,
            gain_two,
            gain_three,
            gain_four,
            gain_five,
            placed(jnp.stack(d_kernel)),
            placed(bn_part),
            table_row,
        ],
        axis=0,
    )
    small = sum_axis(sum_axis(small, "tm"), "rows")
    table_size = rel_table.shape[0] * rel_table.shape[1]
    return (
        output[None],
        grad_frames,
        grad_ffn1_in,
        grad_ffn1_out,
        grad_query,
        grad_key,
        grad_value,
        grad_attn_out,
        grad_conv_in,
        grad_conv_out,
        grad_ffn2_in,
        grad_ffn2_out,
        small[:5],
        small[5 : 5 + taps],
        small[6 + taps],
        small[5 + taps],
        small[7 + taps, :table_size].reshape(rel_table.shape),
    )


def solution(mesh):
    split, copied = P("rows", "tm"), P()
    sequence = P("rows", "tm", None)
    return jax.shard_map(
        shards,
        mesh=mesh,
        in_specs=(sequence, P("rows", None)) + (split,) * 10 + (copied,) * 5 + (sequence,),
        out_specs=(sequence, sequence) + (split,) * 10 + (copied,) * 5,
        check_vma=False,
    )
```

```python
import functools

import jax
import jax.numpy as jnp
from jax import lax
from jax.experimental import pallas as pl
from jax.experimental.pallas import tpu as pltpu
from jax.sharding import PartitionSpec as P

HEAD_DIM = 128
RELMAX = 8
LANES = 128
EPS = 1e-05
BF = jnp.bfloat16
F32 = jnp.float32
SMEM = pl.BlockSpec(memory_space=pltpu.SMEM)


def vmem(count):
    return [pl.BlockSpec(memory_space=pltpu.VMEM)] * count


def params(limit):
    return pltpu.CompilerParams(vmem_limit_bytes=limit * 1024 * 1024)


def cost(flops, *arrays):
    return pl.CostEstimate(
        flops=flops, bytes_accessed=sum(a.size * a.dtype.itemsize for a in arrays), transcendentals=0
    )


def mm(a, b):
    return jnp.dot(a, b, preferred_element_type=F32)


def mm_tn(a, b):
    return lax.dot_general(a, b, (((0,), (0,)), ((), ())), preferred_element_type=F32)


def mm_nt(a, b):
    return lax.dot_general(a, b, (((1,), (1,)), ((), ())), preferred_element_type=F32)


def norm_rows(v, g):
    center = v - jnp.mean(v, axis=-1, keepdims=True)
    spread = jnp.mean(center * center, axis=-1, keepdims=True)
    inverse = lax.rsqrt(spread + EPS)
    normed = center * inverse
    return normed * g, normed, inverse


def norm_back(grad, normed, inverse, g):
    scaled = grad * g
    back = inverse * (
        scaled
        - jnp.mean(scaled, axis=-1, keepdims=True)
        - normed * jnp.mean(scaled * normed, axis=-1, keepdims=True)
    )
    return back, jnp.sum(grad * normed, axis=0)


def tm_peer(dx, dc):
    size = lax.axis_size("tm")
    chips = size // 2
    return [
        (((t // 2 + dx) % chips) * 2 + ((t % 2) ^ dc), t) for t in range(size)
    ]


def from_peer(a, dx, dc):
    return lax.ppermute(a, "tm", tm_peer(dx, dc))


def peer_index(dx, dc):
    chips = lax.axis_size("tm") // 2
    t = lax.axis_index("tm")
    return lax.rem(t // 2 + dx, chips) * 2 + jnp.bitwise_xor(t % 2, dc)


def spread(a, local):
    chips = lax.axis_size("tm") // 2
    far = [from_peer(a, dx, 0) for dx in range(1, chips)]
    near = (a, from_peer(a, 0, 1))
    done = local(near)
    far = [after(b, *jax.tree.leaves(done)) for b in far]
    return [near] + [(b, from_peer(b, 0, 1)) for b in far], done


def collect(mine, theirs, beside=None):
    chips = lax.axis_size("tm") // 2
    sent = [
        (mine[dx] + from_peer(theirs[dx], 0, 1).astype(F32)).astype(BF) for dx in range(1, chips)
    ]
    near = from_peer(theirs[0], 0, 1)
    got = [from_peer(q, chips - dx, 0) for dx, q in enumerate(sent, 1)]
    done = beside(lambda v: after(v, *sent)) if beside else None
    got = [after(v, near, *jax.tree.leaves(done)) for v in got]
    return [mine[0], near] + got, done


def exchange_tm(pieces):
    size = lax.axis_size("tm")
    chips = size // 2
    t = lax.axis_index("tm")
    out = jnp.zeros(pieces.shape, pieces.dtype)
    out = lax.dynamic_update_index_in_dim(
        out, lax.dynamic_index_in_dim(pieces, t, 0, keepdims=False), t, 0
    )
    for dx in range(chips):
        for dc in range(2):
            if dx or dc:
                piece = lax.dynamic_index_in_dim(
                    pieces, peer_index(chips - dx, dc), 0, keepdims=False
                )
                out = lax.dynamic_update_index_in_dim(
                    out, from_peer(piece, dx, dc), peer_index(dx, dc), 0
                )
    return out


def sum_axis(v, axis):
    size, bit = lax.axis_size(axis), 1
    while bit < size:
        v = v + lax.ppermute(v, axis, [(i, i ^ bit) for i in range(size)])
        bit *= 2
    return v


def pack(a, width):
    m, w = a.shape
    f = width // w
    if f * w != width or m % f:
        return a.reshape(-1, width)
    return jnp.concatenate([a[i * (m // f) : (i + 1) * (m // f)] for i in range(f)], axis=1)


def unpack(full, w):
    rows, n, width = full.shape
    f = width // w
    if f * w != width:
        return full.reshape(-1, w)
    if f == 1:
        return full.reshape(-1, w)
    parts = [full[:, None, :, i * w : (i + 1) * w] for i in range(f)]
    return jnp.concatenate(parts, axis=1).reshape(-1, w)


def pack_rows(p, width):
    rows = lax.axis_size("rows")
    m, w = p.shape[0] // rows, p.shape[1]
    f = width // w
    q = p.reshape(rows, m, w)
    if f * w != width or m % f:
        return q.reshape(rows, -1, width)
    return jnp.concatenate([q[:, i * (m // f) : (i + 1) * (m // f)] for i in range(f)], axis=2)


def pack_grads(parts):
    width = max(p.shape[1] for p in parts)
    return jnp.concatenate([pack_rows(p, width) for p in parts], axis=1)


def unpack_grads(total, parts):
    rows = lax.axis_size("rows")
    width = total.shape[1]
    out, at = [], 0
    for p in parts:
        n = p.size // (rows * width)
        out.append(unpack(total[None, at : at + n], p.shape[1]))
        at += n
    return out


def scatter_parity(own, other):
    rows = lax.axis_size("rows")
    near = lax.ppermute(other, "rows", [(i, i ^ 1) for i in range(rows)])
    packed = (own.astype(F32) + near.astype(F32)).astype(BF)
    return lax.psum_scatter(
        packed,
        "rows",
        scatter_dimension=0,
        tiled=False,
        axis_index_groups=[list(range(y, rows, 2)) for y in range(2)],
    )


def scatter_rows(packed):
    return lax.psum_scatter(packed, "rows", scatter_dimension=0, tiled=False)


def gather_ffn(w_in, w_out, more=()):
    m, width = w_in.shape[0], w_out.shape[1] * lax.axis_size("tm")
    side = sum(v.shape[1] for v in more)
    if whole_lanes(w_in.shape, w_out.shape) and (not more or side == width):
        sent = exchanged_ffn(w_in, w_out, more)
        full = lax.all_gather(sent, "rows", axis=0, tiled=False)
        return (Weight(full, 0, m), Weight(full, m, m)), full[:, 2 * m :].reshape(-1, width), sent
    sent = [side_by_side(p) for p in exchange_all(ffn_pieces(w_in, w_out))]
    full = [
        lax.all_gather(p, "rows", axis=0, tiled=True)
        for p in sent + ([jnp.concatenate(more, axis=1)] if more else [])
    ]
    return (Weight(full[0]), Weight(full[1])), full[-1], sent[0]


def exchange_all(pieces):
    size = lax.axis_size("tm")
    width = max(p.shape[2] for p in pieces)
    if any(p[0].size % width for p in pieces):
        return [exchange_tm(p) for p in pieces]
    flat = [p.reshape(size, -1, width) for p in pieces]
    got = exchange_tm(jnp.concatenate(flat, axis=1))
    out, at = [], 0
    for p, q in zip(pieces, flat):
        out.append(got[:, at : at + q.shape[1]].reshape(p.shape))
        at += q.shape[1]
    return out


def after(a, *others):
    return lax.optimization_barrier((a,) + others)[0]


def ffn_pieces(w_in, w_out):
    size = lax.axis_size("tm")
    unit = w_out.shape[0] // size
    m, w = w_in.shape
    a = w_in.reshape(m, w // (size * unit), size, unit).transpose(2, 0, 1, 3)
    return [a.reshape(size, m, w // size), w_out.reshape(size, unit, w_out.shape[1])]


def side_by_side(pieces):
    return pieces.transpose(1, 0, 2).reshape(pieces.shape[1], -1)


def ffn_back_in(a, like_in, like_out):
    size = lax.axis_size("tm")
    m, w = like_in
    unit = like_out[0] // size
    a = exchange_tm(a.reshape(m, size, -1).transpose(1, 0, 2))
    a = a.reshape(size, m, w // (size * unit), unit).transpose(1, 2, 0, 3).reshape(m, w)
    return a.astype(F32)


def ffn_back_out(b, like_out):
    size = lax.axis_size("tm")
    b = exchange_tm(b.reshape(b.shape[0], size, -1).transpose(1, 0, 2))
    return b.reshape(like_out).astype(F32)


def peers():
    chips = lax.axis_size("tm") // 2
    rel = [(dx, dc) for dx in range(chips) for dc in range(2)]
    index = lambda v: jnp.stack(v).astype(jnp.int32)
    return (
        rel,
        index([peer_index(dx, dc) for dx, dc in rel]),
        index([peer_index(chips - dx if dx else 0, dc) for dx, dc in rel]),
    )


def whole_lanes(like_in, like_out):
    unit = like_out[0] // lax.axis_size("tm")
    return unit % LANES == 0 and unit == like_in[0] and like_in[1] == like_out[1] * lax.axis_size("tm")


def cut_kernel(to, w_in, w_out, *outs, unit):
    size, m = len(outs), w_in.shape[0]
    for i, out in enumerate(outs):
        for j in range(out.shape[1] // unit):
            at = pl.multiple_of(j * size * unit + to[i] * unit, unit)
            out[:m, j * unit : (j + 1) * unit] = w_in[:, pl.ds(at, unit)]
        out[m:, :] = w_out[pl.ds(pl.multiple_of(to[i] * unit, unit), unit), :]


def lay_kernel(order, *refs, size):
    out = refs[-1]
    n, w = refs[0].shape
    for i in range(size):
        out[:n, pl.ds(pl.multiple_of(order[i] * w, w), w)] = refs[i][...]
    at = 0
    for r in refs[size:-1]:
        out[n:, at : at + r.shape[1]] = r[...]
        at += r.shape[1]


def exchanged_ffn(w_in, w_out, more=()):
    size = lax.axis_size("tm")
    rel, order, to = peers()
    m, unit = w_in.shape[0], w_out.shape[0] // size
    w = w_in.shape[1] // size
    pieces = pl.pallas_call(
        functools.partial(cut_kernel, unit=unit),
        in_specs=[SMEM] + vmem(2),
        out_shape=[jax.ShapeDtypeStruct((m + unit, w), BF)] * size,
        compiler_params=params(8),
        cost_estimate=cost(0, w_in, w_out),
    )(to, w_in, w_out)
    got = [pieces[0]] + [from_peer(p, *at) for p, at in zip(pieces[1:], rel[1:])]
    n = m + unit + (more[0].shape[0] if more else 0)
    return pl.pallas_call(
        functools.partial(lay_kernel, size=size),
        in_specs=[SMEM] + vmem(size + len(more)),
        out_shape=jax.ShapeDtypeStruct((n, w * size), BF),
        compiler_params=params(8),
        cost_estimate=cost(0, w_in, w_out),
    )(order, *got, *more)


def split_kernel(to, total, *outs):
    w = outs[0].shape[1]
    for i, out in enumerate(outs):
        out[...] = total[:, pl.ds(pl.multiple_of(to[i] * w, w), w)]


def place_kernel(order, *refs, unit):
    size = len(refs) - 2
    g_in, g_out = refs[-2:]
    m = g_in.shape[0]
    for i in range(size):
        for j in range(refs[i].shape[1] // unit):
            at = pl.multiple_of(j * size * unit + order[i] * unit, unit)
            g_in[:, pl.ds(at, unit)] = refs[i][:m, j * unit : (j + 1) * unit].astype(F32)
        rows = pl.ds(pl.multiple_of(order[i] * unit, unit), unit)
        g_out[rows, :] = refs[i][m:, :].astype(F32)


def returned_ffn(total, like_in, like_out):
    size = lax.axis_size("tm")
    rel, order, to = peers()
    n, w = total.shape[0], total.shape[1] // size
    pieces = pl.pallas_call(
        split_kernel,
        in_specs=[SMEM] + vmem(1),
        out_shape=[jax.ShapeDtypeStruct((n, w), BF)] * size,
        compiler_params=params(8),
        cost_estimate=cost(0, total, total),
    )(to, total)
    got = [pieces[0]] + [from_peer(p, *at) for p, at in zip(pieces[1:], rel[1:])]
    return pl.pallas_call(
        functools.partial(place_kernel, unit=like_out[0] // size),
        in_specs=[SMEM] + vmem(size),
        out_shape=[jax.ShapeDtypeStruct(like_in, F32), jax.ShapeDtypeStruct(like_out, F32)],
        compiler_params=params(8),
        cost_estimate=cost(0, total, total, total),
    )(order, *got)


def head_rows_perm():
    rows, size = lax.axis_size("rows"), lax.axis_size("tm")
    perm = []
    for r in range(rows):
        for t in range(size):
            k, u = divmod(r, size)
            perm.append(((t * (rows // size) + k) * size + u, r * size + t))
    return perm


def whole(shape):
    return pl.BlockSpec(shape, lambda *_: (0,) * len(shape))


def flat(v):
    return v.reshape(-1, v.shape[-1])


class Weight:
    def __init__(self, array, first=0, m=None):
        self.array, self.first, self.m = array, first, m
        if m is not None:
            self.shape = (array.shape[0] * m, array.shape[2])
        else:
            self.shape = array.shape

    def all(self):
        if self.m is None:
            return whole(self.shape)
        unit = self.first // self.m
        return pl.BlockSpec(
            (self.array.shape[0], self.m, self.shape[1]), lambda *_: (0, unit, 0)
        )


def ffn_kernel(h0, h1, w_in, w_out, s_ref, slope_ref, mine, theirs):
    n = h0.shape[0]
    h = jnp.concatenate([h0[...], h1[...]], axis=0)
    w_a, w_b = flat(w_in[...]), flat(w_out[...])
    units = w_a.shape[1]
    total = None
    for half in range(2):
        at = slice(half * units // 2, (half + 1) * units // 2)
        a = mm(h, w_a[:, at])
        sig = jax.nn.sigmoid(a)
        act = (a * sig).astype(BF)
        s_ref[:, at] = act
        slope_ref[:, at] = (sig * (1.0 + a * (1.0 - sig))).astype(BF)
        p = mm(act, w_b[at])
        total = p if total is None else total + p
    mine[...] = total[:n]
    theirs[...] = total[n:].astype(BF)


def ffn(pair, w_in, w_out):
    n, d = pair[0].shape
    units = w_in.shape[1]
    return pl.pallas_call(
        ffn_kernel,
        grid=(1,),
        in_specs=[whole((n, d)), whole((n, d)), w_in.all(), w_out.all()],
        out_specs=[whole((2 * n, units))] * 2 + [whole((n, d))] * 2,
        out_shape=[jax.ShapeDtypeStruct((2 * n, units), BF)] * 2
        + [jax.ShapeDtypeStruct((n, d), F32), jax.ShapeDtypeStruct((n, d), BF)],
        compiler_params=params(24),
        cost_estimate=cost(8 * n * d * units, w_in.array),
    )(*pair, w_in.array, w_out.array)


def ffn_back_kernel(g0, g1, slope, w_in, w_out, da_ref, mine, theirs):
    n = g0.shape[0]
    g = jnp.concatenate([g0[...], g1[...]], axis=0)
    w_a, w_b = flat(w_in[...]), flat(w_out[...])
    units = w_a.shape[1]
    total = None
    for half in range(2):
        at = slice(half * units // 2, (half + 1) * units // 2)
        da = (mm_nt(g, w_b[at]) * slope[:, at].astype(F32)).astype(BF)
        da_ref[:, at] = da
        p = mm_nt(da, w_a[:, at])
        total = p if total is None else total + p
    mine[...] = total[:n]
    theirs[...] = total[n:].astype(BF)


def ffn_back(pair, slope, w_in, w_out):
    n, d = pair[0].shape
    units = w_in.shape[1]
    return pl.pallas_call(
        ffn_back_kernel,
        grid=(1,),
        in_specs=[whole((n, d))] * 2 + [whole((2 * n, units)), w_in.all(), w_out.all()],
        out_specs=[whole((2 * n, units))] + [whole((n, d))] * 2,
        out_shape=[
            jax.ShapeDtypeStruct((2 * n, units), BF),
            jax.ShapeDtypeStruct((n, d), F32),
            jax.ShapeDtypeStruct((n, d), BF),
        ],
        compiler_params=params(24),
        cost_estimate=cost(8 * n * d * units, w_in.array),
    )(*pair, slope, w_in.array, w_out.array)


def ffn_grads_kernel(*refs):
    out = refs[-1]
    count = (len(refs) - 1) // 6
    h, g = refs[: 2 * count], refs[2 * count : 4 * count]
    da, s = refs[4 * count : 5 * count], refs[5 * count : 6 * count]
    half = out.shape[1] // 2
    join = lambda v: jnp.concatenate([r[...] for r in v], axis=0)
    out[:, :half, :] = mm_tn(join(h), join(da)).astype(BF).reshape(out.shape[0], half, -1)
    out[:, half:, :] = mm_tn(join(s), join(g)).astype(BF).reshape(out.shape[0], half, -1)


def ffn_grads(h, g, da, s):
    rows = lax.axis_size("rows")
    n, d = h[0].shape
    units, tile = da[0].shape[1], d // 2
    m = d // rows
    if units != d or tile % m:
        h, g, da, s = (jnp.concatenate(v, axis=0) for v in (h, g, da, s))
        return pack_grads([mm_tn(h, da).astype(BF), mm_tn(s, g).astype(BF)])
    part = pl.BlockSpec((n, tile), lambda j: (0, j))
    column = pl.BlockSpec((2 * n, tile), lambda j: (0, j))
    return pl.pallas_call(
        ffn_grads_kernel,
        grid=(d // tile,),
        in_specs=[part] * len(h)
        + [whole((n, d))] * len(g)
        + [whole((2 * n, units))] * len(da)
        + [column] * len(s),
        out_specs=pl.BlockSpec((tile // m, 2 * m, d), lambda j: (j, 0, 0)),
        out_shape=jax.ShapeDtypeStruct((rows, 2 * m, d), BF),
        compiler_params=params(36),
        cost_estimate=cost(4 * len(h) * n * d * units, *h),
    )(*h, *g, *da, *s)


def half_grads_kernel(odd_ref, *refs, count):
    own, other = refs[-2:]
    refs = refs[:-2]
    join = lambda v: jnp.concatenate([r[...] for r in v], axis=0)
    v = mm_tn(join(refs[:count]), join(refs[count:])).astype(BF)
    v = v.reshape(own.shape[0], 2, own.shape[1], own.shape[2])
    even = odd_ref[0] == 0
    own[...] = jnp.where(even, v[:, 0], v[:, 1])
    other[...] = jnp.where(even, v[:, 1], v[:, 0])


def half_grads(left, right):
    rows = lax.axis_size("rows")
    d, units = left[0].shape[1], right[0].shape[1]
    m = d // rows
    if m % 16:
        v = mm_tn(jnp.concatenate(left, axis=0), jnp.concatenate(right, axis=0)).astype(BF)
        return by_parity(v.reshape(rows, m, units))
    odd = (lax.axis_index("rows") % 2).astype(jnp.int32).reshape(1)
    return pl.pallas_call(
        functools.partial(half_grads_kernel, count=len(left)),
        in_specs=[pl.BlockSpec(memory_space=pltpu.SMEM)]
        + [pl.BlockSpec(memory_space=pltpu.VMEM)] * (len(left) + len(right)),
        out_shape=[jax.ShapeDtypeStruct((rows // 2, m, units), BF)] * 2,
        compiler_params=params(28),
        cost_estimate=cost(2 * len(left) * left[0].shape[0] * d * units, *left),
    )(odd, *left, *right)


def by_parity(packed):
    rows = packed.shape[0]
    odd = lax.axis_index("rows") % 2
    v = packed.reshape(rows // 2, 2, *packed.shape[1:])
    return [
        lax.dynamic_index_in_dim(v, odd, 1, keepdims=False),
        lax.dynamic_index_in_dim(v, 1 - odd, 1, keepdims=False),
    ]


def add_norm_kernel(*refs, scale):
    x_ref, gain, x_new, h_ref = refs[-4:]
    total = refs[0][...]
    for r in refs[1:-4]:
        total = total + r[...].astype(F32)
    x = x_ref[...] + scale * total
    x_new[...] = x
    h_ref[...] = norm_rows(x, gain[...])[0].astype(BF)


def add_norm(parts, x, gain, scale):
    n, d = x.shape
    return pl.pallas_call(
        functools.partial(add_norm_kernel, scale=scale),
        out_shape=[jax.ShapeDtypeStruct((n, d), F32), jax.ShapeDtypeStruct((n, d), BF)],
        compiler_params=params(12),
        cost_estimate=cost(0, x, x, x),
    )(*parts, x, gain[None])


def turn_kernel(*refs):
    x_ref, gain, cot, out, d_ref, g_ref, gain_ref = refs[-7:]
    total = refs[0][...]
    for r in refs[1:-7]:
        total = total + r[...].astype(F32)
    y, normed, inverse = norm_rows(x_ref[...] + 0.5 * total, gain[...])
    out[...] = y.astype(BF)
    back, gain_sum = norm_back(cot[...].astype(F32), normed, inverse, gain[...])
    d_ref[...] = back
    g_ref[...] = (0.5 * back).astype(BF)
    gain_ref[...] = gain_sum[None]


def turn(parts, x, gain, cot):
    n, d = x.shape
    return pl.pallas_call(
        turn_kernel,
        out_shape=[
            jax.ShapeDtypeStruct((n, d), BF),
            jax.ShapeDtypeStruct((n, d), F32),
            jax.ShapeDtypeStruct((n, d), BF),
            jax.ShapeDtypeStruct((1, d), F32),
        ],
        compiler_params=params(14),
        cost_estimate=cost(0, x, x, x),
    )(*parts, x, gain[None], cot)


def back_norm_kernel(*refs, scale):
    x_ref, gain, prev, d_ref, g_ref, gain_ref = refs[-6:]
    total = refs[0][...]
    for r in refs[1:-6]:
        total = total + r[...].astype(F32)
    _, normed, inverse = norm_rows(x_ref[...], gain[...])
    back, gain_sum = norm_back(total, normed, inverse, gain[...])
    d = prev[...] + back
    d_ref[...] = d
    g_ref[...] = (scale * d).astype(BF)
    gain_ref[...] = gain_sum[None]


def back_norm(parts, x, gain, prev, scale):
    n, d = x.shape
    return pl.pallas_call(
        functools.partial(back_norm_kernel, scale=scale),
        out_shape=[
            jax.ShapeDtypeStruct((n, d), F32),
            jax.ShapeDtypeStruct((n, d), BF),
            jax.ShapeDtypeStruct((1, d), F32),
        ],
        compiler_params=params(14),
        cost_estimate=cost(0, x, x, x),
    )(*parts, x, gain[None], prev)


def project_kernel(h0, h1, w, out):
    h = jnp.concatenate([h0[...], h1[...]], axis=0)
    out[...] = mm(h, w[...][:, : out.shape[1]]).astype(BF)


def project(pair, w, width):
    n, d = pair[0].shape
    return pl.pallas_call(
        project_kernel,
        grid=(1,),
        in_specs=[whole((n, d)), whole((n, d)), whole(w.shape)],
        out_specs=whole((2 * n, width)),
        out_shape=jax.ShapeDtypeStruct((2 * n, width), BF),
        compiler_params=params(20),
        cost_estimate=cost(4 * n * d * width, w),
    )(*pair, w)


def joined(v, size, depth):
    groups = v.shape[0] // (size * depth)
    cut = lambda k, u: v[(k * size + u) * depth : (k * size + u + 1) * depth]
    return jnp.concatenate(
        [jnp.concatenate([cut(k, u) for u in range(size)], axis=1) for k in range(groups)], axis=0
    )


def fill_bias(tab_ref, head, strip, length):
    lo, hi = length - LANES, length + 2 * LANES
    first, last = tab_ref[head, 0], tab_ref[head, 2 * RELMAX]
    offset = (
        lax.broadcasted_iota(jnp.int32, (LANES, hi - lo), 1)
        - LANES
        - lax.broadcasted_iota(jnp.int32, (LANES, hi - lo), 0)
    )
    tile = jnp.where(offset <= -RELMAX, first, last)
    for b in range(1, 2 * RELMAX):
        tile = jnp.where(offset == b - RELMAX, tab_ref[head, b], tile)
    strip[:, :lo] = jnp.full((LANES, lo), first, F32)
    strip[:, lo:hi] = tile
    strip[:, hi:] = jnp.full((LANES, 2 * length - hi), last, F32)


def biased(q, k, seg_col, seg_row, strip, first, length):
    raw = mm_nt(q, k) * HEAD_DIM ** (-0.5)
    parts = [
        strip[:, length - (first + a) : 2 * length - (first + a)]
        for a in range(0, q.shape[0], LANES)
    ]
    bias = parts[0] if len(parts) == 1 else jnp.concatenate(parts, axis=0)
    return jnp.where(seg_col == seg_row, raw + bias, -jnp.inf)


def head_columns(n, head, heads):
    return pl.ds(pl.multiple_of((n * heads + head) * HEAD_DIM, HEAD_DIM), HEAD_DIM)


def attend_kernel(order, tab_ref, seg_row_ref, seg_col_ref, w_ref, *refs, size, depth):
    chips = size // 2
    pairs, (qkv, att, lse_ref) = refs[:chips], refs[chips : chips + 3]
    mine, theirs = refs[chips + 3 : 2 * chips + 3], refs[2 * chips + 3 : 3 * chips + 3]
    strip = refs[-1]
    length = qkv.shape[0]
    n = length // size
    head, heads = pl.program_id(0), pl.num_programs(0)
    at = lambda i: pl.ds(pl.multiple_of(order[i] * n, n), n)

    @pl.when(head == 0)
    def _():
        for i in range(size):
            qkv[at(i), :] = pairs[i // 2][(i % 2) * n : (i % 2 + 1) * n, :]

    fill_bias(tab_ref, head, strip, length)
    k, v = qkv[:, head_columns(1, head, heads)], qkv[:, head_columns(2, head, heads)]
    block = min(256, length)
    for first in range(0, length, block):
        own = slice(first, first + block)
        q = qkv[own, head_columns(0, head, heads)]
        sc = biased(q, k, seg_col_ref[own, :], seg_row_ref[...], strip, first, length)
        peak = jnp.max(sc, axis=1, keepdims=True)
        e = jnp.exp(sc - peak)
        total = jnp.sum(e, axis=1, keepdims=True)
        p = (e * (1.0 / total)).astype(BF)
        att[own, head_columns(0, head, heads)] = mm(p, v).astype(BF)
        lse_ref[0, own, :] = peak + jnp.log(total)

    @pl.when(head == heads - 1)
    def _():
        share = att.shape[1]
        w = joined(w_ref[...][:, -share:], size, depth)
        for i in range(size):
            p = mm(att[at(i), :], w)
            if i % 2:
                theirs[i // 2][...] = p.astype(BF)
            else:
                mine[i // 2][...] = p


def attend(order, pairs, seg_row, table, weight):
    size = 2 * len(pairs)
    length, heads = seg_row.shape[0], table.shape[0]
    share, d = heads * HEAD_DIM, weight.shape[0]
    n = length // size
    depth = d // lax.axis_size("rows")
    shape = jax.ShapeDtypeStruct
    out = pl.pallas_call(
        functools.partial(attend_kernel, size=size, depth=depth),
        grid=(heads,),
        in_specs=[
            pl.BlockSpec(memory_space=pltpu.SMEM),
            pl.BlockSpec(memory_space=pltpu.SMEM),
            whole((1, length)),
            whole((length, 1)),
            whole(weight.shape),
        ]
        + [whole((2 * n, 3 * share))] * len(pairs),
        out_specs=[
            whole((length, 3 * share)),
            whole((length, share)),
            pl.BlockSpec((1, length, 1), lambda h: (h, 0, 0)),
        ]
        + [whole((n, d))] * size,
        out_shape=[
            shape((length, 3 * share), BF),
            shape((length, share), BF),
            shape((heads, length, 1), F32),
        ]
        + [shape((n, d), F32)] * len(pairs)
        + [shape((n, d), BF)] * len(pairs),
        scratch_shapes=[pltpu.VMEM((LANES, 2 * length), F32)],
        compiler_params=params(32),
        cost_estimate=cost(6 * length * length * share, *pairs),
    )(order, table, seg_row.reshape(1, length), seg_row.reshape(length, 1), weight, *pairs)
    chips = len(pairs)
    return out[0], out[1], out[2], out[3 : 3 + chips], out[3 + chips :]


def att_grad_kernel(g0, g1, w_ref, out, *, size, depth):
    share = out.shape[1]
    w = joined(w_ref[...][:, -share:], size, depth)
    g = jnp.concatenate([g0[...], g1[...]], axis=0)
    out[...] = mm_nt(g, w).astype(BF)


def att_grad(pair, weight, share):
    n, d = pair[0].shape
    return pl.pallas_call(
        functools.partial(
            att_grad_kernel, size=lax.axis_size("tm"), depth=d // lax.axis_size("rows")
        ),
        grid=(1,),
        in_specs=[whole((n, d)), whole((n, d)), whole(weight.shape)],
        out_specs=whole((2 * n, share)),
        out_shape=jax.ShapeDtypeStruct((2 * n, share), BF),
        compiler_params=params(16),
        cost_estimate=cost(4 * n * d * share, weight),
    )(*pair, weight)


def attend_back_kernel(
    order, tab_ref, seg_row_ref, seg_col_ref, w_ref, qkv, lse_ref, *refs, size
):
    chips = size // 2
    pairs, (dqkv_ref, band_ref) = refs[:chips], refs[chips : chips + 2]
    mine, theirs = refs[chips + 2 : 2 * chips + 2], refs[2 * chips + 2 : 3 * chips + 2]
    strip, dk_sum, dv_sum, grad = refs[-4:]
    length = qkv.shape[0]
    n = length // size
    block = min(256, length)
    head, heads = pl.program_id(0), pl.num_programs(0)
    rows_of = lambda i: pl.ds(pl.multiple_of(order[i] * n, n), n)

    @pl.when(head == 0)
    def _():
        for i in range(size):
            grad[rows_of(i), :] = pairs[i // 2][(i % 2) * n : (i % 2 + 1) * n, :]

    fill_bias(tab_ref, head, strip, length)
    k, v = qkv[:, head_columns(1, head, heads)], qkv[:, head_columns(2, head, heads)]
    scale = HEAD_DIM ** (-0.5)
    at = lambda n: head_columns(n, head, heads)
    low = jnp.zeros((LANES, LANES), F32)
    high = jnp.zeros((LANES, LANES), F32)
    band = [jnp.zeros((LANES, LANES), F32) for _ in range(3)]
    for first in range(0, length, block):
        own = slice(first, first + block)
        q, do = qkv[own, at(0)], grad[own, at(0)]
        sc = biased(q, k, seg_col_ref[own, :], seg_row_ref[...], strip, first, length)
        p = jnp.exp(sc - lse_ref[0, own, :])
        dp = mm_nt(do, v)
        inner = jnp.sum(p * dp, axis=1, keepdims=True)
        ds = (p * (dp - inner)).astype(BF)
        dv = mm_tn(p.astype(BF), do)
        dk = mm_tn(ds, q)
        if first == 0:
            dv_sum[...] = dv
            dk_sum[...] = dk
        else:
            dv_sum[...] += dv
            dk_sum[...] += dk
        dqkv_ref[own, at(0)] = (mm(ds, k) * scale).astype(BF)
        wide = ds.astype(F32)
        for a in range(0, block, LANES):
            for b in range(0, length, LANES):
                part = wide[a : a + LANES, b : b + LANES]
                apart = (b - first - a) // LANES
                if apart < -1:
                    low = low + part
                elif apart > 1:
                    high = high + part
                else:
                    band[apart + 1] = band[apart + 1] + part
    dqkv_ref[:, at(1)] = (dk_sum[...] * scale).astype(BF)
    dqkv_ref[:, at(2)] = dv_sum[...].astype(BF)
    for i, part in enumerate([low] + band + [high]):
        band_ref[0, :, i * LANES : (i + 1) * LANES] = part

    @pl.when(head == heads - 1)
    def _():
        w = w_ref[...][:, : dqkv_ref.shape[1]]
        for i in range(size):
            p = mm_nt(dqkv_ref[rows_of(i), :], w)
            if i % 2:
                theirs[i // 2][...] = p.astype(BF)
            else:
                mine[i // 2][...] = p


def attend_back(order, pairs, qkv, seg_row, table, lse, weight):
    size = 2 * len(pairs)
    length, heads = qkv.shape[0], table.shape[0]
    share, d = heads * HEAD_DIM, weight.shape[0]
    n = length // size
    shape = jax.ShapeDtypeStruct
    out = pl.pallas_call(
        functools.partial(attend_back_kernel, size=size),
        grid=(heads,),
        in_specs=[
            pl.BlockSpec(memory_space=pltpu.SMEM),
            pl.BlockSpec(memory_space=pltpu.SMEM),
            whole((1, length)),
            whole((length, 1)),
            whole(weight.shape),
            whole((length, 3 * share)),
            pl.BlockSpec((1, length, 1), lambda h: (h, 0, 0)),
        ]
        + [whole((2 * n, share))] * len(pairs),
        out_specs=[
            whole((length, 3 * share)),
            pl.BlockSpec((1, LANES, 5 * LANES), lambda h: (h, 0, 0)),
        ]
        + [whole((n, d))] * size,
        out_shape=[
            shape((length, 3 * share), BF),
            shape((heads, LANES, 5 * LANES), F32),
        ]
        + [shape((n, d), F32)] * len(pairs)
        + [shape((n, d), BF)] * len(pairs),
        scratch_shapes=[
            pltpu.VMEM((LANES, 2 * length), F32),
            pltpu.VMEM((length, HEAD_DIM), F32),
            pltpu.VMEM((length, HEAD_DIM), F32),
            pltpu.VMEM((length, share), BF),
        ],
        compiler_params=params(36),
        cost_estimate=cost(12 * length * length * share, *pairs),
    )(
        order,
        table,
        seg_row.reshape(1, length),
        seg_row.reshape(length, 1),
        weight,
        qkv,
        lse,
        *pairs,
    )
    chips = len(pairs)
    return out[0], out[1], out[2 : 2 + chips], out[2 + chips :]


def table_grad(band):
    offset = (
        lax.broadcasted_iota(jnp.int32, (LANES, 3 * LANES), 1)
        - LANES
        - lax.broadcasted_iota(jnp.int32, (LANES, 3 * LANES), 0)
    )
    middle = band[:, :, LANES : 4 * LANES]
    inner = [
        jnp.sum(jnp.where(offset == b, middle, 0.0), axis=(1, 2)) for b in range(1 - RELMAX, RELMAX)
    ]
    lower = jnp.sum(jnp.where(offset <= -RELMAX, middle, 0.0), axis=(1, 2))
    upper = jnp.sum(jnp.where(offset >= RELMAX, middle, 0.0), axis=(1, 2))
    lower = lower + jnp.sum(band[:, :, :LANES], axis=(1, 2))
    upper = upper + jnp.sum(band[:, :, 4 * LANES :], axis=(1, 2))
    return jnp.stack([lower] + inner + [upper], axis=1)


def attend_grads_kernel(order, dqkv, att, *refs):
    out, h_all, g_all = refs[-3:]
    size = (len(refs) - 3) // 2
    h, g = refs[:size], refs[size : 2 * size]
    n = h[0].shape[0]
    wide = dqkv.shape[1]
    for i in range(size):
        at = pl.ds(pl.multiple_of(order[i] * n, n), n)
        h_all[at, :] = h[i][...]
        g_all[at, :] = g[i][...]
    first = mm_tn(h_all[...], dqkv[...]).astype(BF)
    out[:, :, :wide] = first.reshape(out.shape[0], out.shape[1], wide)
    second = mm_tn(att[...], g_all[...]).astype(BF)
    depth, share = out.shape[1], out.shape[2] - wide
    per = second.shape[1] // share
    for i in range(out.shape[0]):
        k, u = divmod(i, per)
        out[i, :, wide:] = second[k * depth : (k + 1) * depth, u * share : (u + 1) * share]


def attend_grads(order, h, g, dqkv, att):
    rows, size = lax.axis_size("rows"), lax.axis_size("tm")
    n, d = h[0].shape
    length, share = att.shape
    m = d // rows
    if share != 2 * m:
        def place(chunks):
            out = jnp.zeros((size, n, d), BF)
            for i, v in enumerate(chunks):
                out = lax.dynamic_update_index_in_dim(out, v, order[i], 0)
            return out.reshape(length, d)

        first = mm_tn(place(h), dqkv).astype(BF)
        second = mm_tn(att, place(g)).astype(BF)
        second = (
            second.reshape(rows // size, m, size, share).transpose(0, 2, 1, 3).reshape(d, share)
        )
        return jnp.concatenate([first, second], axis=1).reshape(rows, m, -1)
    return pl.pallas_call(
        attend_grads_kernel,
        grid=(1,),
        in_specs=[
            pl.BlockSpec(memory_space=pltpu.SMEM),
            whole(dqkv.shape),
            whole(att.shape),
        ]
        + [whole((n, d))] * (2 * size),
        out_specs=whole((rows, m, 4 * share)),
        out_shape=jax.ShapeDtypeStruct((rows, m, 4 * share), BF),
        scratch_shapes=[pltpu.VMEM((length, d), BF)] * 2,
        compiler_params=params(28),
        cost_estimate=cost(8 * length * d * share, *h),
    )(order, dqkv, att, *h, *g)


EDGE = 16


def glu_kernel(h0, h1, w, z, sig_ref, slope_ref):
    h = jnp.concatenate([h0[...], h1[...]], axis=0)
    u = mm(h, w[...])
    share = z.shape[1]
    lin, sig = u[:, :share], jax.nn.sigmoid(u[:, share:])
    z[...] = (lin * sig).astype(BF)
    sig_ref[...] = sig.astype(BF)
    slope_ref[...] = (lin * sig * (1.0 - sig)).astype(BF)


def glu(pair, w):
    n, d = pair[0].shape
    share = w.shape[1] // 2
    return pl.pallas_call(
        glu_kernel,
        out_shape=[jax.ShapeDtypeStruct((2 * n, share), BF)] * 3,
        compiler_params=params(16),
        cost_estimate=cost(8 * n * d * share, w),
    )(*pair, w)


def lay_out(order, pairs, out):
    n = pairs[0].shape[0] // 2
    out[:EDGE, :] = jnp.zeros((EDGE, out.shape[1]), F32)
    out[EDGE + 2 * len(pairs) * n :, :] = jnp.zeros((EDGE, out.shape[1]), F32)
    for i in range(2 * len(pairs)):
        rows = pl.ds(pl.multiple_of(EDGE + order[i] * n, EDGE), n)
        out[rows, :] = pairs[i // 2][(i % 2) * n : (i % 2 + 1) * n, :].astype(F32)


def pick(ref, order, size):
    n = ref.shape[0] // size
    return jnp.concatenate(
        [ref[pl.ds(pl.multiple_of(order[i] * n, EDGE), n), :] for i in range(size)], axis=0
    )


def joined_rows(refs):
    return jnp.concatenate([r[...] for r in refs], axis=0)


def tap_masks(seg, taps, count):
    own = seg[EDGE : EDGE + count, :]
    first = EDGE - taps // 2
    return [(seg[first + k : first + k + count, :] == own).astype(F32) for k in range(taps)]


def convolve_kernel(order, seg, taps_ref, *refs, taps):
    pairs, (conv_ref, sums_ref, wide) = refs[:-3], refs[-3:]
    count = conv_ref.shape[0]
    lay_out(order, pairs, wide)
    first = EDGE - taps // 2
    total = None
    for k, mask in enumerate(tap_masks(seg, taps, count)):
        term = (wide[first + k : first + k + count, :] * mask) * taps_ref[k : k + 1, :]
        total = term if total is None else total + term
    conv_ref[...] = total
    sums_ref[0:1, :] = jnp.sum(total, axis=0, keepdims=True)
    sums_ref[1:2, :] = jnp.sum(total * total, axis=0, keepdims=True)


def convolve(order, seg, taps, pairs):
    count, share = seg.shape[0] - 2 * EDGE, pairs[0].shape[1]
    return pl.pallas_call(
        functools.partial(convolve_kernel, taps=taps.shape[0]),
        in_specs=[SMEM] + vmem(2 + len(pairs)),
        out_shape=[
            jax.ShapeDtypeStruct((count, share), F32),
            jax.ShapeDtypeStruct((2, share), F32),
        ],
        scratch_shapes=[pltpu.VMEM((count + 2 * EDGE, share), F32)],
        compiler_params=params(16),
        cost_estimate=cost(0, *pairs, *pairs, *pairs),
    )(order, seg, taps, *pairs)


def bn_stats(moments, total):
    centre = moments[0:1, :] / total
    return centre, lax.rsqrt(moments[1:2, :] / total - centre * centre + EPS)


def bn_kernel(order, conv, moments, gain, bias, w, e_ref, slope_ref, *refs, total):
    size = len(refs)
    n = conv.shape[0] // size
    centre, inverse = bn_stats(moments[...], total)
    shifted = (pick(conv, order, size) - centre) * inverse * gain[...] + bias[...]
    sig = jax.nn.sigmoid(shifted)
    e = (shifted * sig).astype(BF)
    e_ref[...] = e
    slope_ref[...] = (sig * (1.0 + shifted * (1.0 - sig))).astype(BF)
    p = mm(e, w[...])
    for i in range(size):
        refs[i % 2 * (size // 2) + i // 2][...] = p[i * n : (i + 1) * n].astype(
            BF if i % 2 else F32
        )


def chunk_shapes(n, d, size):
    return [jax.ShapeDtypeStruct((n, d), F32)] * (size // 2) + [
        jax.ShapeDtypeStruct((n, d), BF)
    ] * (size // 2)


def bn_forward(order, conv, moments, gain, bias, w, total):
    count, share = conv.shape
    d, size = w.shape[1], lax.axis_size("tm")
    out = pl.pallas_call(
        functools.partial(bn_kernel, total=total),
        in_specs=[SMEM] + vmem(5),
        out_shape=[jax.ShapeDtypeStruct((count, share), BF)] * 2
        + chunk_shapes(count // size, d, size),
        compiler_params=params(24),
        cost_estimate=cost(2 * count * share * d, conv),
    )(order, conv, moments, gain, bias, w)
    return out[0], out[1], out[2 : 2 + size // 2], out[2 + size // 2 :]


def conv_out_grad_kernel(g0, g1, w, out):
    g = jnp.concatenate([g0[...], g1[...]], axis=0)
    out[...] = mm_nt(g, w[...])


def conv_out_grad(pair, w):
    n, d = pair[0].shape
    return pl.pallas_call(
        conv_out_grad_kernel,
        out_shape=jax.ShapeDtypeStruct((2 * n, w.shape[0]), F32),
        compiler_params=params(12),
        cost_estimate=cost(4 * n * d * w.shape[0], w),
    )(*pair, w)


def bn_sums_kernel(order, conv, slope, moments, *refs, total):
    pairs, (dn_ref, sums_ref) = refs[:-2], refs[-2:]
    dn = joined_rows(pairs) * slope[...].astype(F32)
    dn_ref[...] = dn
    centre, inverse = bn_stats(moments[...], total)
    normed = (pick(conv, order, 2 * len(pairs)) - centre) * inverse
    sums_ref[0:1, :] = jnp.sum(dn, axis=0, keepdims=True)
    sums_ref[1:2, :] = jnp.sum(dn * normed, axis=0, keepdims=True)


def bn_back(order, conv, slope, moments, pairs, total):
    count, share = conv.shape
    return pl.pallas_call(
        functools.partial(bn_sums_kernel, total=total),
        in_specs=[SMEM] + vmem(3 + len(pairs)),
        out_shape=[
            jax.ShapeDtypeStruct((count, share), F32),
            jax.ShapeDtypeStruct((2, share), F32),
        ],
        compiler_params=params(16),
        cost_estimate=cost(0, conv, conv, conv),
    )(order, conv, slope, moments, *pairs)


def conv_back_kernel(
    order, seg, taps_ref, dn, conv, moments, sums, gain, w, *refs, taps, total, size
):
    chips = size // 2
    z, sig, slope = refs[:chips], refs[chips : 2 * chips], refs[2 * chips : 3 * chips]
    du_ref, dk_ref = refs[3 * chips : 3 * chips + 2]
    out, (c_wide, z_wide, dz_ref, dc_ref) = refs[3 * chips + 2 : -4], refs[-4:]
    count, share = dn.shape
    n = count // size
    centre, inverse = bn_stats(moments[...], total)
    normed = (pick(conv, order, size) - centre) * inverse
    dc = dn[...] - sums[0:1, :] / total - normed * (sums[1:2, :] / total)
    dc_ref[...] = (gain[...] * inverse * dc).astype(BF)
    lay_out(order, [dc_ref.at[2 * n * i : 2 * n * (i + 1)] for i in range(chips)], c_wide)
    lay_out(order, z, z_wide)
    first = EDGE - taps // 2
    masks = tap_masks(seg, taps, count)
    own = c_wide[EDGE : EDGE + count, :]
    dz = None
    for k in range(taps):
        mirror = taps - 1 - k
        near = c_wide[first + mirror : first + mirror + count, :] * masks[mirror]
        term = near * taps_ref[k : k + 1, :]
        dz = term if dz is None else dz + term
        dk_ref[k : k + 1, :] = jnp.sum(
            (z_wide[first + k : first + k + count, :] * masks[k]) * own, axis=0, keepdims=True
        )
    dz_ref[...] = dz
    dz = pick(dz_ref, order, size)
    du = jnp.concatenate(
        [dz * joined_rows(sig).astype(F32), dz * joined_rows(slope).astype(F32)], axis=1
    ).astype(BF)
    du_ref[...] = du
    p = mm_nt(du, w[...])
    for i in range(size):
        out[i % 2 * chips + i // 2][...] = p[i * n : (i + 1) * n].astype(BF if i % 2 else F32)


def conv_back(order, seg, taps, dn, conv, moments, sums, gain, w, kept, total):
    count, share = dn.shape
    d, size = w.shape[0], lax.axis_size("tm")
    wide = pltpu.VMEM((count + 2 * EDGE, share), F32)
    z, sig, slope = zip(*kept)
    out = pl.pallas_call(
        functools.partial(conv_back_kernel, taps=taps.shape[0], total=total, size=size),
        in_specs=[SMEM] + vmem(8 + 3 * len(kept)),
        out_shape=[
            jax.ShapeDtypeStruct((count, 2 * share), BF),
            jax.ShapeDtypeStruct((taps.shape[0], share), F32),
        ]
        + chunk_shapes(count // size, d, size),
        scratch_shapes=[
            wide,
            wide,
            pltpu.VMEM((count, share), F32),
            pltpu.VMEM((count, share), BF),
        ],
        compiler_params=params(30),
        cost_estimate=cost(4 * count * share * d, dn, dn, dn),
    )(order, seg, taps, dn, conv, moments, sums, gain, w, *z, *sig, *slope)
    return out[0], out[1], out[2 : 2 + size // 2], out[2 + size // 2 :]


def conv_grads_kernel(du, e, *refs):
    size = (len(refs) - 2) // 2
    in_ref, out_ref = refs[-2:]
    in_ref[...] = mm_tn(joined_rows(refs[:size]), du[...]).astype(BF)
    out_ref[...] = mm_tn(e[...], joined_rows(refs[size : 2 * size])).astype(BF)


def conv_grads(h, g, du, e):
    d, share = h[0].shape[1], e.shape[1]
    return pl.pallas_call(
        conv_grads_kernel,
        out_shape=[
            jax.ShapeDtypeStruct((d, 2 * share), BF),
            jax.ShapeDtypeStruct((share, d), BF),
        ],
        compiler_params=params(24),
        cost_estimate=cost(6 * e.shape[0] * share * d, du, e),
    )(du, e, *h, *g)


def shards(
    frames,
    segments,
    ffn1_in,
    ffn1_out,
    query_w,
    key_w,
    value_w,
    attn_out,
    conv_in,
    conv_out,
    ffn2_in,
    ffn2_out,
    norm_gains,
    conv_kernel,
    bn_gain,
    bn_bias,
    rel_table,
    cotangent,
):
    rows, size = lax.axis_size("rows"), lax.axis_size("tm")
    t = lax.axis_index("tm")
    own, width = frames.shape[1], frames.shape[2]
    length = own * size
    share = width // size
    heads = rel_table.shape[0] // size
    taps = conv_kernel.shape[0]
    frame_total = float(length * rows)
    seg = segments[0]
    table = lax.dynamic_slice_in_dim(rel_table, t * heads, heads, 0)
    depth = width // rows
    unit = depth // size

    def mine(v):
        v = v.reshape(-1, rows, size, unit)
        return lax.dynamic_index_in_dim(v, t, 2, keepdims=False).reshape(-1, share)

    def placed(v):
        n = v.shape[0]
        out = jnp.zeros((n, rows, size, unit), F32)
        return lax.dynamic_update_index_in_dim(
            out, v.reshape(n, rows, unit), t, 2
        ).reshape(n, width)

    kernel_own = mine(conv_kernel)
    bn_gain_own, bn_bias_own = mine(bn_gain[None]), mine(bn_bias[None])
    seg_near = jnp.pad(seg, (EDGE, EDGE), constant_values=-1).reshape(-1, 1)

    perm = head_rows_perm()
    out_block = lax.ppermute(attn_out, ("rows", "tm"), perm)
    order = jnp.stack(
        [peer_index(dx, dc) for dx in range(size // 2) for dc in range(2)]
    ).astype(jnp.int32)
    f1, attn_part, sent = gather_ffn(ffn1_in, ffn1_out, (query_w, key_w, value_w, out_block))
    wide = conv_in.shape[1]
    pieces = exchange_all(
        [
            after(conv_in, sent)
            .reshape(depth, wide // depth, size, unit)
            .transpose(2, 0, 1, 3)
            .reshape(size, depth, wide // size),
            after(conv_out, sent).reshape(size, unit, share),
        ]
    )
    packed = [pack(side_by_side(p), width) for p in pieces]
    sent = jnp.concatenate(packed, axis=0)
    full = lax.all_gather(sent, "rows", axis=0, tiled=False)
    at = packed[0].shape[0]
    conv_in_w, conv_out_w = unpack(full[:, :at], wide), unpack(full[:, at:], width)
    f2, _, sent = gather_ffn(after(ffn2_in, sent), ffn2_out)

    inputs = frames[0].astype(F32)
    n1 = norm_rows(inputs, norm_gains[0])[0]
    h1, _ = spread(n1.astype(BF), lambda near: ())
    h1[0] = (after(h1[0][0], sent), h1[0][1])
    one = [ffn(pair, *f1) for pair in reversed(h1)][::-1]
    parts, attn_w = collect(
        [v[2] for v in one], [v[3] for v in one], lambda ready: ready(attn_part)
    )
    x1, n2 = add_norm(parts, inputs, norm_gains[1], 0.5)

    h2, local = spread(n2, lambda near: project(near, attn_w, 3 * share))
    pairs = [local] + [project(pair, attn_w, 3 * share) for pair in h2[1:]]
    qkv, att, lse, mine_a, theirs_a = attend(order, pairs, seg, table, attn_w)
    parts, _ = collect(mine_a, theirs_a)
    x2, n3 = add_norm(parts, x1, norm_gains[2], 1.0)

    h3, local = spread(n3, lambda near: glu(near, conv_in_w))
    kept = [local] + [glu(pair, conv_in_w) for pair in h3[1:]]
    conv, moments = convolve(order, seg_near, kernel_own, [v[0] for v in kept])
    moments = sum_axis(moments, "rows")
    e, e_slope, mine_c, theirs_c = bn_forward(
        order, conv, moments, bn_gain_own, bn_bias_own, conv_out_w, frame_total
    )
    parts, _ = collect(mine_c, theirs_c)
    x3, n4 = add_norm(parts, x2, norm_gains[3], 1.0)

    h4, local = spread(n4, lambda near: ffn(near, *f2))
    four = [local] + [ffn(pair, *f2) for pair in h4[1:]]
    parts, _ = collect([v[2] for v in four], [v[3] for v in four])
    output, d4, g, gain_five = turn(parts, x3, norm_gains[4], cotangent[0])

    g4, local = spread(g, lambda near: ffn_back(near, four[0][1], *f2))
    back = [local] + [ffn_back(p, four[i][1], *f2) for i, p in enumerate(g4[1:], 1)]
    parts, packed_four = collect(
        [v[1] for v in back],
        [v[2] for v in back],
        lambda ready: ffn_grads(
            [ready(v) for v in sum(h4, ())],
            sum(g4, ()),
            [v[0] for v in back],
            [ready(v[0]) for v in four],
        ),
    )
    d3, g, gain_four = back_norm(parts, x3, norm_gains[3], d4, 1.0)
    sum_four = scatter_rows(packed_four)

    g3, local = spread(g, lambda near: conv_out_grad(near, conv_out_w))
    pairs = [local] + [conv_out_grad(pair, conv_out_w) for pair in g3[1:]]
    dn, bn_part = bn_back(order, conv, e_slope, moments, pairs, frame_total)
    bn_sums = sum_axis(bn_part, "rows")
    du, d_kernel, mine_c, theirs_c = conv_back(
        order,
        seg_near,
        kernel_own,
        dn,
        conv,
        moments,
        bn_sums,
        bn_gain_own,
        conv_in_w,
        kept,
        frame_total,
    )
    parts, _ = collect(mine_c, theirs_c)
    d2, g, gain_three = back_norm(parts, x2, norm_gains[2], d3, 1.0)

    g2, local = spread(
        g,
        lambda near: (
            att_grad(near, attn_w, share),
            conv_grads([after(v, g) for v in sum(h3, ())], sum(g3, ()), du, e),
        ),
    )
    local, parts_three = local
    packed_three = pack_grads(parts_three)
    pairs = [local] + [att_grad(pair, attn_w, share) for pair in g2[1:]]
    dqkv, band, mine_a, theirs_a = attend_back(order, pairs, qkv, seg, table, lse, attn_w)

    def attention_sums(ready):
        packed = attend_grads(
            order, [ready(v) for v in sum(h2, ())], sum(g2, ()), dqkv, att
        )
        if packed.shape[2] == packed_three.shape[2]:
            return (jnp.concatenate([packed, packed_three], axis=1),)
        return packed, packed_three

    parts, packed_mid = collect(mine_a, theirs_a, attention_sums)
    d1, g, gain_two = back_norm(parts, x1, norm_gains[1], d2, 0.5)
    if len(packed_mid) == 1:
        sum_mid = scatter_rows(packed_mid[0])
        sum_two, sum_three = sum_mid[:depth], sum_mid[depth:]
    else:
        sum_two, sum_three = (scatter_rows(v) for v in packed_mid)

    g1, local = spread(g, lambda near: ffn_back(near, one[0][1], *f1))
    back = [local] + [ffn_back(p, one[i][1], *f1) for i, p in enumerate(g1[1:], 1)]
    packed_one = ffn_grads(
        sum(h1, ()), sum(g1, ()), [v[0] for v in back], [v[0] for v in one]
    )
    sum_one = scatter_rows(packed_one)
    parts, _ = collect([v[1] for v in back], [v[2] for v in back])
    grad, _, gain_one = back_norm(parts, inputs, norm_gains[0], d1, 1.0)
    grad_frames = grad.astype(BF)[None]

    def ffn_parts(total):
        if total.shape == (2 * depth, width) and ffn1_in.shape[1] == width:
            return total[:depth], total[depth:]
        like = [
            jax.ShapeDtypeStruct((width, ffn1_in.shape[1]), BF),
            jax.ShapeDtypeStruct((ffn1_in.shape[1], width), BF),
        ]
        return unpack_grads(total, like)

    def ffn_owned(total):
        if whole_lanes(ffn1_in.shape, ffn1_out.shape):
            return returned_ffn(total, ffn1_in.shape, ffn1_out.shape)
        g_in, g_out = ffn_parts(total)
        return (
            ffn_back_in(g_in, ffn1_in.shape, ffn1_out.shape),
            ffn_back_out(g_out, ffn1_out.shape),
        )

    grad_ffn2_in, grad_ffn2_out = ffn_owned(sum_four)
    grad_query, grad_key, grad_value, d_block = (
        sum_two[:, i * share : (i + 1) * share] for i in range(4)
    )
    grad_query, grad_key, grad_value = (v.astype(F32) for v in (grad_query, grad_key, grad_value))
    grad_attn_out = lax.ppermute(d_block, ("rows", "tm"), [(b, a) for a, b in perm]).astype(F32)
    d_in, d_out = unpack_grads(sum_three, parts_three)
    d_in, d_out = exchange_all(
        [
            d_in.reshape(depth, size, -1).transpose(1, 0, 2),
            d_out.reshape(unit, size, share).transpose(1, 0, 2),
        ]
    )
    grad_conv_in = (
        d_in.reshape(size, depth, wide // depth, unit)
        .transpose(1, 2, 0, 3)
        .reshape(depth, wide)
        .astype(F32)
    )
    grad_conv_out = d_out.reshape(depth, share).astype(F32)
    grad_ffn1_in, grad_ffn1_out = ffn_owned(sum_one)

    table_row = lax.dynamic_update_slice_in_dim(
        jnp.zeros(rel_table.shape, F32), table_grad(band), t * heads, 0
    ).reshape(1, -1)
    table_row = jnp.pad(table_row, ((0, 0), (0, width - table_row.shape[1])))
    small = jnp.concatenate(
        [
            gain_one,
            gain_two,
            gain_three,
            gain_four,
            gain_five,
            placed(d_kernel),
            placed(bn_part),
            table_row,
        ],
        axis=0,
    )
    small = sum_axis(sum_axis(small, "tm"), "rows")
    table_size = rel_table.shape[0] * rel_table.shape[1]
    return (
        output[None],
        grad_frames,
        grad_ffn1_in,
        grad_ffn1_out,
        grad_query,
        grad_key,
        grad_value,
        grad_attn_out,
        grad_conv_in,
        grad_conv_out,
        grad_ffn2_in,
        grad_ffn2_out,
        small[:5],
        small[5 : 5 + taps],
        small[6 + taps],
        small[5 + taps],
        small[7 + taps, :table_size].reshape(rel_table.shape),
    )


def solution(mesh):
    split, copied = P("rows", "tm"), P()
    sequence = P("rows", "tm", None)
    return jax.shard_map(
        shards,
        mesh=mesh,
        in_specs=(sequence, P("rows", None)) + (split,) * 10 + (copied,) * 5 + (sequence,),
        out_specs=(sequence, sequence) + (split,) * 10 + (copied,) * 5,
        check_vma=False,
    )
```

```python
import functools

import jax
import jax.numpy as jnp
from jax import lax
from jax.experimental import pallas as pl
from jax.experimental.pallas import tpu as pltpu
from jax.sharding import PartitionSpec as P

HEAD_DIM = 128
RELMAX = 8
LANES = 128
EPS = 1e-05
LOG2E = 1.4426950408889634
BF = jnp.bfloat16
F32 = jnp.float32
SMEM = pl.BlockSpec(memory_space=pltpu.SMEM)


def vmem(count):
    return [pl.BlockSpec(memory_space=pltpu.VMEM)] * count


def params(limit):
    return pltpu.CompilerParams(vmem_limit_bytes=limit * 1024 * 1024)


def cost(flops, *arrays):
    return pl.CostEstimate(
        flops=flops, bytes_accessed=sum(a.size * a.dtype.itemsize for a in arrays), transcendentals=0
    )


def mm(a, b):
    return jnp.dot(a, b, preferred_element_type=F32)


def mm_tn(a, b):
    return lax.dot_general(a, b, (((0,), (0,)), ((), ())), preferred_element_type=F32)


def mm_nt(a, b):
    return lax.dot_general(a, b, (((1,), (1,)), ((), ())), preferred_element_type=F32)


def norm_rows(v, g):
    center = v - jnp.mean(v, axis=-1, keepdims=True)
    spread = jnp.mean(center * center, axis=-1, keepdims=True)
    inverse = lax.rsqrt(spread + EPS)
    normed = center * inverse
    return normed * g, normed, inverse


def norm_back(grad, normed, inverse, g):
    scaled = grad * g
    back = inverse * (
        scaled
        - jnp.mean(scaled, axis=-1, keepdims=True)
        - normed * jnp.mean(scaled * normed, axis=-1, keepdims=True)
    )
    return back, jnp.sum(grad * normed, axis=0)


def tm_peer(dx, dc):
    size = lax.axis_size("tm")
    chips = size // 2
    return [
        (((t // 2 + dx) % chips) * 2 + ((t % 2) ^ dc), t) for t in range(size)
    ]


def from_peer(a, dx, dc):
    return lax.ppermute(a, "tm", tm_peer(dx, dc))


def peer_index(dx, dc):
    chips = lax.axis_size("tm") // 2
    t = lax.axis_index("tm")
    return lax.rem(t // 2 + dx, chips) * 2 + jnp.bitwise_xor(t % 2, dc)


def spread(a, local):
    chips = lax.axis_size("tm") // 2
    far = [from_peer(a, dx, 0) for dx in range(1, chips)]
    near = (a, from_peer(a, 0, 1))
    done = local(near)
    far = [after(b, *jax.tree.leaves(done)) for b in far]
    return [near] + [(b, from_peer(b, 0, 1)) for b in far], done


def collect(mine, theirs, beside=None):
    chips = lax.axis_size("tm") // 2
    sent = [
        (mine[dx] + from_peer(theirs[dx], 0, 1).astype(F32)).astype(BF) for dx in range(1, chips)
    ]
    near = from_peer(theirs[0], 0, 1)
    got = [from_peer(q, chips - dx, 0) for dx, q in enumerate(sent, 1)]
    done = beside(lambda v: after(v, *sent)) if beside else None
    got = [after(v, near, *jax.tree.leaves(done)) for v in got]
    return [mine[0], near] + got, done


def exchange_tm(pieces):
    size = lax.axis_size("tm")
    chips = size // 2
    t = lax.axis_index("tm")
    out = jnp.zeros(pieces.shape, pieces.dtype)
    out = lax.dynamic_update_index_in_dim(
        out, lax.dynamic_index_in_dim(pieces, t, 0, keepdims=False), t, 0
    )
    for dx in range(chips):
        for dc in range(2):
            if dx or dc:
                piece = lax.dynamic_index_in_dim(
                    pieces, peer_index(chips - dx, dc), 0, keepdims=False
                )
                out = lax.dynamic_update_index_in_dim(
                    out, from_peer(piece, dx, dc), peer_index(dx, dc), 0
                )
    return out


def sum_axis(v, axis):
    size, bit = lax.axis_size(axis), 1
    while bit < size:
        v = v + lax.ppermute(v, axis, [(i, i ^ bit) for i in range(size)])
        bit *= 2
    return v


def pack(a, width):
    m, w = a.shape
    f = width // w
    if f * w != width or m % f:
        return a.reshape(-1, width)
    return jnp.concatenate([a[i * (m // f) : (i + 1) * (m // f)] for i in range(f)], axis=1)


def unpack(full, w):
    rows, n, width = full.shape
    f = width // w
    if f * w != width:
        return full.reshape(-1, w)
    if f == 1:
        return full.reshape(-1, w)
    parts = [full[:, None, :, i * w : (i + 1) * w] for i in range(f)]
    return jnp.concatenate(parts, axis=1).reshape(-1, w)


def pack_rows(p, width):
    rows = lax.axis_size("rows")
    m, w = p.shape[0] // rows, p.shape[1]
    f = width // w
    q = p.reshape(rows, m, w)
    if f * w != width or m % f:
        return q.reshape(rows, -1, width)
    return jnp.concatenate([q[:, i * (m // f) : (i + 1) * (m // f)] for i in range(f)], axis=2)


def pack_grads(parts):
    width = max(p.shape[1] for p in parts)
    return jnp.concatenate([pack_rows(p, width) for p in parts], axis=1)


def unpack_grads(total, parts):
    rows = lax.axis_size("rows")
    width = total.shape[1]
    out, at = [], 0
    for p in parts:
        n = p.size // (rows * width)
        out.append(unpack(total[None, at : at + n], p.shape[1]))
        at += n
    return out


def scatter_parity(own, other):
    rows = lax.axis_size("rows")
    near = lax.ppermute(other, "rows", [(i, i ^ 1) for i in range(rows)])
    packed = (own.astype(F32) + near.astype(F32)).astype(BF)
    return lax.psum_scatter(
        packed,
        "rows",
        scatter_dimension=0,
        tiled=False,
        axis_index_groups=[list(range(y, rows, 2)) for y in range(2)],
    )


def scatter_rows(packed):
    return lax.psum_scatter(packed, "rows", scatter_dimension=0, tiled=False)


def gather_ffn(w_in, w_out, more=()):
    m, width = w_in.shape[0], w_out.shape[1] * lax.axis_size("tm")
    side = sum(v.shape[1] for v in more)
    if whole_lanes(w_in.shape, w_out.shape) and (not more or side == width):
        sent = exchanged_ffn(w_in, w_out, more)
        full = lax.all_gather(sent, "rows", axis=0, tiled=False)
        return (Weight(full, 0, m), Weight(full, m, m)), full[:, 2 * m :].reshape(-1, width), sent
    sent = [side_by_side(p) for p in exchange_all(ffn_pieces(w_in, w_out))]
    full = [
        lax.all_gather(p, "rows", axis=0, tiled=True)
        for p in sent + ([jnp.concatenate(more, axis=1)] if more else [])
    ]
    return (Weight(full[0]), Weight(full[1])), full[-1], sent[0]


def exchange_all(pieces):
    size = lax.axis_size("tm")
    width = max(p.shape[2] for p in pieces)
    if any(p[0].size % width for p in pieces):
        return [exchange_tm(p) for p in pieces]
    flat = [p.reshape(size, -1, width) for p in pieces]
    got = exchange_tm(jnp.concatenate(flat, axis=1))
    out, at = [], 0
    for p, q in zip(pieces, flat):
        out.append(got[:, at : at + q.shape[1]].reshape(p.shape))
        at += q.shape[1]
    return out


def after(a, *others):
    return lax.optimization_barrier((a,) + others)[0]


def ffn_pieces(w_in, w_out):
    size = lax.axis_size("tm")
    unit = w_out.shape[0] // size
    m, w = w_in.shape
    a = w_in.reshape(m, w // (size * unit), size, unit).transpose(2, 0, 1, 3)
    return [a.reshape(size, m, w // size), w_out.reshape(size, unit, w_out.shape[1])]


def side_by_side(pieces):
    return pieces.transpose(1, 0, 2).reshape(pieces.shape[1], -1)


def ffn_back_in(a, like_in, like_out):
    size = lax.axis_size("tm")
    m, w = like_in
    unit = like_out[0] // size
    a = exchange_tm(a.reshape(m, size, -1).transpose(1, 0, 2))
    a = a.reshape(size, m, w // (size * unit), unit).transpose(1, 2, 0, 3).reshape(m, w)
    return a.astype(F32)


def ffn_back_out(b, like_out):
    size = lax.axis_size("tm")
    b = exchange_tm(b.reshape(b.shape[0], size, -1).transpose(1, 0, 2))
    return b.reshape(like_out).astype(F32)


def peers():
    chips = lax.axis_size("tm") // 2
    rel = [(dx, dc) for dx in range(chips) for dc in range(2)]
    index = lambda v: jnp.stack(v).astype(jnp.int32)
    return (
        rel,
        index([peer_index(dx, dc) for dx, dc in rel]),
        index([peer_index(chips - dx if dx else 0, dc) for dx, dc in rel]),
    )


def whole_lanes(like_in, like_out):
    unit = like_out[0] // lax.axis_size("tm")
    return unit % LANES == 0 and unit == like_in[0] and like_in[1] == like_out[1] * lax.axis_size("tm")


def cut_kernel(to, w_in, w_out, *outs, unit):
    size, m = len(outs), w_in.shape[0]
    for i, out in enumerate(outs):
        for j in range(out.shape[1] // unit):
            at = pl.multiple_of(j * size * unit + to[i] * unit, unit)
            out[:m, j * unit : (j + 1) * unit] = w_in[:, pl.ds(at, unit)]
        out[m:, :] = w_out[pl.ds(pl.multiple_of(to[i] * unit, unit), unit), :]


def lay_kernel(order, *refs, size):
    out = refs[-1]
    n, w = refs[0].shape
    for i in range(size):
        out[:n, pl.ds(pl.multiple_of(order[i] * w, w), w)] = refs[i][...]
    at = 0
    for r in refs[size:-1]:
        out[n:, at : at + r.shape[1]] = r[...]
        at += r.shape[1]


def exchanged_ffn(w_in, w_out, more=()):
    size = lax.axis_size("tm")
    rel, order, to = peers()
    m, unit = w_in.shape[0], w_out.shape[0] // size
    w = w_in.shape[1] // size
    pieces = pl.pallas_call(
        functools.partial(cut_kernel, unit=unit),
        in_specs=[SMEM] + vmem(2),
        out_shape=[jax.ShapeDtypeStruct((m + unit, w), BF)] * size,
        compiler_params=params(60),
        cost_estimate=cost(0, w_in, w_out),
    )(to, w_in, w_out)
    got = [pieces[0]] + [from_peer(p, *at) for p, at in zip(pieces[1:], rel[1:])]
    n = m + unit + (more[0].shape[0] if more else 0)
    return pl.pallas_call(
        functools.partial(lay_kernel, size=size),
        in_specs=[SMEM] + vmem(size + len(more)),
        out_shape=jax.ShapeDtypeStruct((n, w * size), BF),
        compiler_params=params(60),
        cost_estimate=cost(0, w_in, w_out),
    )(order, *got, *more)


def split_kernel(to, total, *outs):
    w = outs[0].shape[1]
    for i, out in enumerate(outs):
        out[...] = total[:, pl.ds(pl.multiple_of(to[i] * w, w), w)]


def place_kernel(order, *refs, unit):
    size = len(refs) - 2
    g_in, g_out = refs[-2:]
    m = g_in.shape[0]
    for i in range(size):
        for j in range(refs[i].shape[1] // unit):
            at = pl.multiple_of(j * size * unit + order[i] * unit, unit)
            g_in[:, pl.ds(at, unit)] = refs[i][:m, j * unit : (j + 1) * unit].astype(F32)
        rows = pl.ds(pl.multiple_of(order[i] * unit, unit), unit)
        g_out[rows, :] = refs[i][m:, :].astype(F32)


def returned_ffn(total, like_in, like_out):
    size = lax.axis_size("tm")
    rel, order, to = peers()
    n, w = total.shape[0], total.shape[1] // size
    pieces = pl.pallas_call(
        split_kernel,
        in_specs=[SMEM] + vmem(1),
        out_shape=[jax.ShapeDtypeStruct((n, w), BF)] * size,
        compiler_params=params(8),
        cost_estimate=cost(0, total, total),
    )(to, total)
    got = [pieces[0]] + [from_peer(p, *at) for p, at in zip(pieces[1:], rel[1:])]
    return pl.pallas_call(
        functools.partial(place_kernel, unit=like_out[0] // size),
        in_specs=[SMEM] + vmem(size),
        out_shape=[jax.ShapeDtypeStruct(like_in, F32), jax.ShapeDtypeStruct(like_out, F32)],
        compiler_params=params(8),
        cost_estimate=cost(0, total, total, total),
    )(order, *got)


def head_rows_perm():
    rows, size = lax.axis_size("rows"), lax.axis_size("tm")
    perm = []
    for r in range(rows):
        for t in range(size):
            k, u = divmod(r, size)
            perm.append(((t * (rows // size) + k) * size + u, r * size + t))
    return perm


def whole(shape):
    return pl.BlockSpec(shape, lambda *_: (0,) * len(shape))


def flat(v):
    return v.reshape(-1, v.shape[-1])


class Weight:
    def __init__(self, array, first=0, m=None):
        self.array, self.first, self.m = array, first, m
        if m is not None:
            self.shape = (array.shape[0] * m, array.shape[2])
        else:
            self.shape = array.shape

    def all(self):
        if self.m is None:
            return whole(self.shape)
        unit = self.first // self.m
        return pl.BlockSpec(
            (self.array.shape[0], self.m, self.shape[1]), lambda *_: (0, unit, 0)
        )


def ffn_kernel(h0, h1, w_in, w_out, s_ref, slope_ref, mine, theirs):
    n = h0.shape[0]
    h = jnp.concatenate([h0[...], h1[...]], axis=0)
    w_a, w_b = flat(w_in[...]), flat(w_out[...])
    units = w_a.shape[1]
    total = None
    for half in range(2):
        at = slice(half * units // 2, (half + 1) * units // 2)
        a = mm(h, w_a[:, at])
        sig = jax.nn.sigmoid(a)
        act = (a * sig).astype(BF)
        s_ref[:, at] = act
        slope_ref[:, at] = (sig * (1.0 + a * (1.0 - sig))).astype(BF)
        p = mm(act, w_b[at])
        total = p if total is None else total + p
    mine[...] = total[:n]
    theirs[...] = total[n:].astype(BF)


def ffn(pair, w_in, w_out):
    n, d = pair[0].shape
    units = w_in.shape[1]
    return pl.pallas_call(
        ffn_kernel,
        grid=(1,),
        in_specs=[whole((n, d)), whole((n, d)), w_in.all(), w_out.all()],
        out_specs=[whole((2 * n, units))] * 2 + [whole((n, d))] * 2,
        out_shape=[jax.ShapeDtypeStruct((2 * n, units), BF)] * 2
        + [jax.ShapeDtypeStruct((n, d), F32), jax.ShapeDtypeStruct((n, d), BF)],
        compiler_params=params(24),
        cost_estimate=cost(8 * n * d * units, w_in.array),
    )(*pair, w_in.array, w_out.array)


def ffn_back_kernel(g0, g1, slope, w_in, w_out, da_ref, mine, theirs):
    n = g0.shape[0]
    g = jnp.concatenate([g0[...], g1[...]], axis=0)
    w_a, w_b = flat(w_in[...]), flat(w_out[...])
    units = w_a.shape[1]
    total = None
    for half in range(2):
        at = slice(half * units // 2, (half + 1) * units // 2)
        da = (mm_nt(g, w_b[at]) * slope[:, at].astype(F32)).astype(BF)
        da_ref[:, at] = da
        p = mm_nt(da, w_a[:, at])
        total = p if total is None else total + p
    mine[...] = total[:n]
    theirs[...] = total[n:].astype(BF)


def ffn_back(pair, slope, w_in, w_out):
    n, d = pair[0].shape
    units = w_in.shape[1]
    return pl.pallas_call(
        ffn_back_kernel,
        grid=(1,),
        in_specs=[whole((n, d))] * 2 + [whole((2 * n, units)), w_in.all(), w_out.all()],
        out_specs=[whole((2 * n, units))] + [whole((n, d))] * 2,
        out_shape=[
            jax.ShapeDtypeStruct((2 * n, units), BF),
            jax.ShapeDtypeStruct((n, d), F32),
            jax.ShapeDtypeStruct((n, d), BF),
        ],
        compiler_params=params(24),
        cost_estimate=cost(8 * n * d * units, w_in.array),
    )(*pair, slope, w_in.array, w_out.array)


def ffn_grads_kernel(*refs):
    out = refs[-1]
    count = (len(refs) - 1) // 6
    h, g = refs[: 2 * count], refs[2 * count : 4 * count]
    da, s = refs[4 * count : 5 * count], refs[5 * count : 6 * count]
    half = out.shape[1] // 2
    join = lambda v: jnp.concatenate([r[...] for r in v], axis=0)
    out[:, :half, :] = mm_tn(join(h), join(da)).astype(BF).reshape(out.shape[0], half, -1)
    out[:, half:, :] = mm_tn(join(s), join(g)).astype(BF).reshape(out.shape[0], half, -1)


def ffn_grads(h, g, da, s):
    rows = lax.axis_size("rows")
    n, d = h[0].shape
    units, tile = da[0].shape[1], d // 2
    m = d // rows
    if units != d or tile % m:
        h, g, da, s = (jnp.concatenate(v, axis=0) for v in (h, g, da, s))
        return pack_grads([mm_tn(h, da).astype(BF), mm_tn(s, g).astype(BF)])
    part = pl.BlockSpec((n, tile), lambda j: (0, j))
    column = pl.BlockSpec((2 * n, tile), lambda j: (0, j))
    return pl.pallas_call(
        ffn_grads_kernel,
        grid=(d // tile,),
        in_specs=[part] * len(h)
        + [whole((n, d))] * len(g)
        + [whole((2 * n, units))] * len(da)
        + [column] * len(s),
        out_specs=pl.BlockSpec((tile // m, 2 * m, d), lambda j: (j, 0, 0)),
        out_shape=jax.ShapeDtypeStruct((rows, 2 * m, d), BF),
        compiler_params=params(36),
        cost_estimate=cost(4 * len(h) * n * d * units, *h),
    )(*h, *g, *da, *s)


def half_grads_kernel(odd_ref, *refs, count):
    own, other = refs[-2:]
    refs = refs[:-2]
    join = lambda v: jnp.concatenate([r[...] for r in v], axis=0)
    v = mm_tn(join(refs[:count]), join(refs[count:])).astype(BF)
    v = v.reshape(own.shape[0], 2, own.shape[1], own.shape[2])
    even = odd_ref[0] == 0
    own[...] = jnp.where(even, v[:, 0], v[:, 1])
    other[...] = jnp.where(even, v[:, 1], v[:, 0])


def half_grads(left, right):
    rows = lax.axis_size("rows")
    d, units = left[0].shape[1], right[0].shape[1]
    m = d // rows
    if m % 16:
        v = mm_tn(jnp.concatenate(left, axis=0), jnp.concatenate(right, axis=0)).astype(BF)
        return by_parity(v.reshape(rows, m, units))
    odd = (lax.axis_index("rows") % 2).astype(jnp.int32).reshape(1)
    return pl.pallas_call(
        functools.partial(half_grads_kernel, count=len(left)),
        in_specs=[pl.BlockSpec(memory_space=pltpu.SMEM)]
        + [pl.BlockSpec(memory_space=pltpu.VMEM)] * (len(left) + len(right)),
        out_shape=[jax.ShapeDtypeStruct((rows // 2, m, units), BF)] * 2,
        compiler_params=params(28),
        cost_estimate=cost(2 * len(left) * left[0].shape[0] * d * units, *left),
    )(odd, *left, *right)


def by_parity(packed):
    rows = packed.shape[0]
    odd = lax.axis_index("rows") % 2
    v = packed.reshape(rows // 2, 2, *packed.shape[1:])
    return [
        lax.dynamic_index_in_dim(v, odd, 1, keepdims=False),
        lax.dynamic_index_in_dim(v, 1 - odd, 1, keepdims=False),
    ]


def add_norm_kernel(*refs, scale):
    x_ref, gain, x_new, h_ref = refs[-4:]
    total = refs[0][...]
    for r in refs[1:-4]:
        total = total + r[...].astype(F32)
    x = x_ref[...] + scale * total
    x_new[...] = x
    h_ref[...] = norm_rows(x, gain[...])[0].astype(BF)


def add_norm(parts, x, gain, scale):
    n, d = x.shape
    return pl.pallas_call(
        functools.partial(add_norm_kernel, scale=scale),
        out_shape=[pltpu.HBM((n, d), F32), jax.ShapeDtypeStruct((n, d), BF)],
        compiler_params=params(12),
        cost_estimate=cost(0, x, x, x),
    )(*parts, x, gain[None])


def turn_kernel(*refs):
    x_ref, gain, cot, out, d_ref, g_ref, gain_ref = refs[-7:]
    total = refs[0][...]
    for r in refs[1:-7]:
        total = total + r[...].astype(F32)
    y, normed, inverse = norm_rows(x_ref[...] + 0.5 * total, gain[...])
    out[...] = y.astype(BF)
    back, gain_sum = norm_back(cot[...].astype(F32), normed, inverse, gain[...])
    d_ref[...] = back
    g_ref[...] = (0.5 * back).astype(BF)
    gain_ref[...] = gain_sum[None]


def turn(parts, x, gain, cot):
    n, d = x.shape
    return pl.pallas_call(
        turn_kernel,
        out_shape=[
            jax.ShapeDtypeStruct((n, d), BF),
            pltpu.HBM((n, d), F32),
            jax.ShapeDtypeStruct((n, d), BF),
            jax.ShapeDtypeStruct((1, d), F32),
        ],
        compiler_params=params(14),
        cost_estimate=cost(0, x, x, x),
    )(*parts, x, gain[None], cot)


def back_norm_kernel(*refs, scale):
    x_ref, gain, prev, d_ref, g_ref, gain_ref = refs[-6:]
    total = refs[0][...]
    for r in refs[1:-6]:
        total = total + r[...].astype(F32)
    _, normed, inverse = norm_rows(x_ref[...], gain[...])
    back, gain_sum = norm_back(total, normed, inverse, gain[...])
    d = prev[...] + back
    d_ref[...] = d
    g_ref[...] = (scale * d).astype(BF)
    gain_ref[...] = gain_sum[None]


def back_norm(parts, x, gain, prev, scale):
    n, d = x.shape
    return pl.pallas_call(
        functools.partial(back_norm_kernel, scale=scale),
        out_shape=[
            pltpu.HBM((n, d), F32),
            jax.ShapeDtypeStruct((n, d), BF),
            jax.ShapeDtypeStruct((1, d), F32),
        ],
        compiler_params=params(14),
        cost_estimate=cost(0, x, x, x),
    )(*parts, x, gain[None], prev)


def project_kernel(h0, h1, w, out):
    h = jnp.concatenate([h0[...], h1[...]], axis=0)
    out[...] = mm(h, w[...][:, : out.shape[1]]).astype(BF)


def project(pair, w, width):
    n, d = pair[0].shape
    return pl.pallas_call(
        project_kernel,
        grid=(1,),
        in_specs=[whole((n, d)), whole((n, d)), whole(w.shape)],
        out_specs=whole((2 * n, width)),
        out_shape=jax.ShapeDtypeStruct((2 * n, width), BF),
        compiler_params=params(20),
        cost_estimate=cost(4 * n * d * width, w),
    )(*pair, w)


def joined(v, size, depth):
    groups = v.shape[0] // (size * depth)
    cut = lambda k, u: v[(k * size + u) * depth : (k * size + u + 1) * depth]
    return jnp.concatenate(
        [jnp.concatenate([cut(k, u) for u in range(size)], axis=1) for k in range(groups)], axis=0
    )


def fill_bias(tab_ref, head, strip, length):
    lo, hi = length - LANES, length + 2 * LANES
    entry = lambda b: tab_ref[head, b] * LOG2E
    first, last = entry(0), entry(2 * RELMAX)
    offset = (
        lax.broadcasted_iota(jnp.int32, (LANES, hi - lo), 1)
        - LANES
        - lax.broadcasted_iota(jnp.int32, (LANES, hi - lo), 0)
    )
    tile = jnp.where(offset <= -RELMAX, first, last)
    for b in range(1, 2 * RELMAX):
        tile = jnp.where(offset == b - RELMAX, entry(b), tile)
    strip[:, :lo] = jnp.full((LANES, lo), first, F32)
    strip[:, lo:hi] = tile
    strip[:, hi:] = jnp.full((LANES, 2 * length - hi), last, F32)


def biased(q, k, seg_col, seg_row, strip, first, length):
    raw = mm_nt(q, k) * (HEAD_DIM ** (-0.5) * LOG2E)
    parts = [
        strip[:, length - (first + a) : 2 * length - (first + a)]
        for a in range(0, q.shape[0], LANES)
    ]
    bias = parts[0] if len(parts) == 1 else jnp.concatenate(parts, axis=0)
    return jnp.where(seg_col == seg_row, raw + bias, -jnp.inf)


def head_columns(n, head, heads):
    return pl.ds(pl.multiple_of((n * heads + head) * HEAD_DIM, HEAD_DIM), HEAD_DIM)


def attend_kernel(order, tab_ref, seg_row_ref, seg_col_ref, w_ref, *refs, size, depth):
    chips = size // 2
    pairs, (qkv, att, lse_ref) = refs[:chips], refs[chips : chips + 3]
    mine, theirs = refs[chips + 3 : 2 * chips + 3], refs[2 * chips + 3 : 3 * chips + 3]
    strip = refs[-1]
    length = qkv.shape[0]
    n = length // size
    head, heads = pl.program_id(0), pl.num_programs(0)
    at = lambda i: pl.ds(pl.multiple_of(order[i] * n, n), n)

    @pl.when(head == 0)
    def _():
        for i in range(size):
            qkv[at(i), :] = pairs[i // 2][(i % 2) * n : (i % 2 + 1) * n, :]

    fill_bias(tab_ref, head, strip, length)
    k, v = qkv[:, head_columns(1, head, heads)], qkv[:, head_columns(2, head, heads)]
    block = min(256, length)
    for first in range(0, length, block):
        own = slice(first, first + block)
        q = qkv[own, head_columns(0, head, heads)]
        sc = biased(q, k, seg_col_ref[own, :], seg_row_ref[...], strip, first, length)
        peak = jnp.max(sc, axis=1, keepdims=True)
        e = jnp.exp2(sc - peak)
        total = jnp.sum(e, axis=1, keepdims=True)
        inverse = 1.0 / total
        att[own, head_columns(0, head, heads)] = (mm(e.astype(BF), v) * inverse).astype(BF)
        lse_ref[0, own, :] = peak + jnp.log(total) * LOG2E

    @pl.when(head == heads - 1)
    def _():
        share = att.shape[1]
        w = joined(w_ref[...][:, -share:], size, depth)
        for i in range(size):
            p = mm(att[at(i), :], w)
            if i % 2:
                theirs[i // 2][...] = p.astype(BF)
            else:
                mine[i // 2][...] = p


def attend(order, pairs, seg_row, table, weight):
    size = 2 * len(pairs)
    length, heads = seg_row.shape[0], table.shape[0]
    share, d = heads * HEAD_DIM, weight.shape[0]
    n = length // size
    depth = d // lax.axis_size("rows")
    shape = jax.ShapeDtypeStruct
    out = pl.pallas_call(
        functools.partial(attend_kernel, size=size, depth=depth),
        grid=(heads,),
        in_specs=[
            pl.BlockSpec(memory_space=pltpu.SMEM),
            pl.BlockSpec(memory_space=pltpu.SMEM),
            whole((1, length)),
            whole((length, 1)),
            whole(weight.shape),
        ]
        + [whole((2 * n, 3 * share))] * len(pairs),
        out_specs=[
            whole((length, 3 * share)),
            whole((length, share)),
            pl.BlockSpec((1, length, 1), lambda h: (h, 0, 0)),
        ]
        + [whole((n, d))] * size,
        out_shape=[
            shape((length, 3 * share), BF),
            shape((length, share), BF),
            shape((heads, length, 1), F32),
        ]
        + [shape((n, d), F32)] * len(pairs)
        + [shape((n, d), BF)] * len(pairs),
        scratch_shapes=[pltpu.VMEM((LANES, 2 * length), F32)],
        compiler_params=params(32),
        cost_estimate=cost(6 * length * length * share, *pairs),
    )(order, table, seg_row.reshape(1, length), seg_row.reshape(length, 1), weight, *pairs)
    chips = len(pairs)
    return out[0], out[1], out[2], out[3 : 3 + chips], out[3 + chips :]


def att_grad_kernel(g0, g1, w_ref, out, *, size, depth):
    share = out.shape[1]
    w = joined(w_ref[...][:, -share:], size, depth)
    g = jnp.concatenate([g0[...], g1[...]], axis=0)
    out[...] = mm_nt(g, w).astype(BF)


def att_grad(pair, weight, share):
    n, d = pair[0].shape
    return pl.pallas_call(
        functools.partial(
            att_grad_kernel, size=lax.axis_size("tm"), depth=d // lax.axis_size("rows")
        ),
        grid=(1,),
        in_specs=[whole((n, d)), whole((n, d)), whole(weight.shape)],
        out_specs=whole((2 * n, share)),
        out_shape=jax.ShapeDtypeStruct((2 * n, share), BF),
        compiler_params=params(16),
        cost_estimate=cost(4 * n * d * share, weight),
    )(*pair, weight)


def attend_back_kernel(
    order, tab_ref, seg_row_ref, seg_col_ref, w_ref, qkv, lse_ref, *refs, size
):
    chips = size // 2
    pairs, (dqkv_ref, band_ref) = refs[:chips], refs[chips : chips + 2]
    mine, theirs = refs[chips + 2 : 2 * chips + 2], refs[2 * chips + 2 : 3 * chips + 2]
    strip, dk_sum, dv_sum, grad = refs[-4:]
    length = qkv.shape[0]
    n = length // size
    block = min(256, length)
    head, heads = pl.program_id(0), pl.num_programs(0)
    rows_of = lambda i: pl.ds(pl.multiple_of(order[i] * n, n), n)

    @pl.when(head == 0)
    def _():
        for i in range(size):
            grad[rows_of(i), :] = pairs[i // 2][(i % 2) * n : (i % 2 + 1) * n, :]

    fill_bias(tab_ref, head, strip, length)
    k, v = qkv[:, head_columns(1, head, heads)], qkv[:, head_columns(2, head, heads)]
    scale = HEAD_DIM ** (-0.5)
    at = lambda n: head_columns(n, head, heads)
    low = jnp.zeros((LANES, LANES), F32)
    high = jnp.zeros((LANES, LANES), F32)
    band = [jnp.zeros((LANES, LANES), F32) for _ in range(3)]
    for first in range(0, length, block):
        own = slice(first, first + block)
        q, do = qkv[own, at(0)], grad[own, at(0)]
        sc = biased(q, k, seg_col_ref[own, :], seg_row_ref[...], strip, first, length)
        p = jnp.exp2(sc - lse_ref[0, own, :])
        dp = mm_nt(do, v)
        inner = jnp.sum(p * dp, axis=1, keepdims=True)
        ds = (p * (dp - inner)).astype(BF)
        dv = mm_tn(p.astype(BF), do)
        dk = mm_tn(ds, q)
        if first == 0:
            dv_sum[...] = dv
            dk_sum[...] = dk
        else:
            dv_sum[...] += dv
            dk_sum[...] += dk
        dqkv_ref[own, at(0)] = (mm(ds, k) * scale).astype(BF)
        wide = ds.astype(F32)
        for a in range(0, block, LANES):
            for b in range(0, length, LANES):
                part = wide[a : a + LANES, b : b + LANES]
                apart = (b - first - a) // LANES
                if apart < -1:
                    low = low + part
                elif apart > 1:
                    high = high + part
                else:
                    band[apart + 1] = band[apart + 1] + part
    dqkv_ref[:, at(1)] = (dk_sum[...] * scale).astype(BF)
    dqkv_ref[:, at(2)] = dv_sum[...].astype(BF)
    for i, part in enumerate([low] + band + [high]):
        band_ref[0, :, i * LANES : (i + 1) * LANES] = part

    @pl.when(head == heads - 1)
    def _():
        w = w_ref[...][:, : dqkv_ref.shape[1]]
        for i in range(size):
            p = mm_nt(dqkv_ref[rows_of(i), :], w)
            if i % 2:
                theirs[i // 2][...] = p.astype(BF)
            else:
                mine[i // 2][...] = p


def attend_back(order, pairs, qkv, seg_row, table, lse, weight):
    size = 2 * len(pairs)
    length, heads = qkv.shape[0], table.shape[0]
    share, d = heads * HEAD_DIM, weight.shape[0]
    n = length // size
    shape = jax.ShapeDtypeStruct
    out = pl.pallas_call(
        functools.partial(attend_back_kernel, size=size),
        grid=(heads,),
        in_specs=[
            pl.BlockSpec(memory_space=pltpu.SMEM),
            pl.BlockSpec(memory_space=pltpu.SMEM),
            whole((1, length)),
            whole((length, 1)),
            whole(weight.shape),
            whole((length, 3 * share)),
            pl.BlockSpec((1, length, 1), lambda h: (h, 0, 0)),
        ]
        + [whole((2 * n, share))] * len(pairs),
        out_specs=[
            whole((length, 3 * share)),
            pl.BlockSpec((1, LANES, 5 * LANES), lambda h: (h, 0, 0)),
        ]
        + [whole((n, d))] * size,
        out_shape=[
            shape((length, 3 * share), BF),
            shape((heads, LANES, 5 * LANES), F32),
        ]
        + [shape((n, d), F32)] * len(pairs)
        + [shape((n, d), BF)] * len(pairs),
        scratch_shapes=[
            pltpu.VMEM((LANES, 2 * length), F32),
            pltpu.VMEM((length, HEAD_DIM), F32),
            pltpu.VMEM((length, HEAD_DIM), F32),
            pltpu.VMEM((length, share), BF),
        ],
        compiler_params=params(36),
        cost_estimate=cost(12 * length * length * share, *pairs),
    )(
        order,
        table,
        seg_row.reshape(1, length),
        seg_row.reshape(length, 1),
        weight,
        qkv,
        lse,
        *pairs,
    )
    chips = len(pairs)
    return out[0], out[1], out[2 : 2 + chips], out[2 + chips :]


def table_grad(band):
    offset = (
        lax.broadcasted_iota(jnp.int32, (LANES, 3 * LANES), 1)
        - LANES
        - lax.broadcasted_iota(jnp.int32, (LANES, 3 * LANES), 0)
    )
    middle = band[:, :, LANES : 4 * LANES]
    inner = [
        jnp.sum(jnp.where(offset == b, middle, 0.0), axis=(1, 2)) for b in range(1 - RELMAX, RELMAX)
    ]
    lower = jnp.sum(jnp.where(offset <= -RELMAX, middle, 0.0), axis=(1, 2))
    upper = jnp.sum(jnp.where(offset >= RELMAX, middle, 0.0), axis=(1, 2))
    lower = lower + jnp.sum(band[:, :, :LANES], axis=(1, 2))
    upper = upper + jnp.sum(band[:, :, 4 * LANES :], axis=(1, 2))
    return jnp.stack([lower] + inner + [upper], axis=1)


def attend_grads_kernel(order, dqkv, att, *refs):
    out, h_all, g_all = refs[-3:]
    size = (len(refs) - 3) // 2
    h, g = refs[:size], refs[size : 2 * size]
    n = h[0].shape[0]
    wide = dqkv.shape[1]
    for i in range(size):
        at = pl.ds(pl.multiple_of(order[i] * n, n), n)
        h_all[at, :] = h[i][...]
        g_all[at, :] = g[i][...]
    first = mm_tn(h_all[...], dqkv[...]).astype(BF)
    out[:, :, :wide] = first.reshape(out.shape[0], out.shape[1], wide)
    second = mm_tn(att[...], g_all[...]).astype(BF)
    depth, share = out.shape[1], out.shape[2] - wide
    per = second.shape[1] // share
    for i in range(out.shape[0]):
        k, u = divmod(i, per)
        out[i, :, wide:] = second[k * depth : (k + 1) * depth, u * share : (u + 1) * share]


def attend_grads(order, h, g, dqkv, att):
    rows, size = lax.axis_size("rows"), lax.axis_size("tm")
    n, d = h[0].shape
    length, share = att.shape
    m = d // rows
    if share != 2 * m:
        def place(chunks):
            out = jnp.zeros((size, n, d), BF)
            for i, v in enumerate(chunks):
                out = lax.dynamic_update_index_in_dim(out, v, order[i], 0)
            return out.reshape(length, d)

        first = mm_tn(place(h), dqkv).astype(BF)
        second = mm_tn(att, place(g)).astype(BF)
        second = (
            second.reshape(rows // size, m, size, share).transpose(0, 2, 1, 3).reshape(d, share)
        )
        return jnp.concatenate([first, second], axis=1).reshape(rows, m, -1)
    return pl.pallas_call(
        attend_grads_kernel,
        grid=(1,),
        in_specs=[
            pl.BlockSpec(memory_space=pltpu.SMEM),
            whole(dqkv.shape),
            whole(att.shape),
        ]
        + [whole((n, d))] * (2 * size),
        out_specs=whole((rows, m, 4 * share)),
        out_shape=jax.ShapeDtypeStruct((rows, m, 4 * share), BF),
        scratch_shapes=[pltpu.VMEM((length, d), BF)] * 2,
        compiler_params=params(28),
        cost_estimate=cost(8 * length * d * share, *h),
    )(order, dqkv, att, *h, *g)


EDGE = 16


def glu_kernel(h0, h1, w, z, sig_ref, slope_ref):
    h = jnp.concatenate([h0[...], h1[...]], axis=0)
    u = mm(h, w[...])
    share = z.shape[1]
    lin, sig = u[:, :share], jax.nn.sigmoid(u[:, share:])
    z[...] = (lin * sig).astype(BF)
    sig_ref[...] = sig.astype(BF)
    slope_ref[...] = (lin * sig * (1.0 - sig)).astype(BF)


def glu(pair, w):
    n, d = pair[0].shape
    share = w.shape[1] // 2
    return pl.pallas_call(
        glu_kernel,
        out_shape=[jax.ShapeDtypeStruct((2 * n, share), BF)] * 3,
        compiler_params=params(16),
        cost_estimate=cost(8 * n * d * share, w),
    )(*pair, w)


def lay_out(order, pairs, out):
    n = pairs[0].shape[0] // 2
    out[:EDGE, :] = jnp.zeros((EDGE, out.shape[1]), F32)
    out[EDGE + 2 * len(pairs) * n :, :] = jnp.zeros((EDGE, out.shape[1]), F32)
    for i in range(2 * len(pairs)):
        rows = pl.ds(pl.multiple_of(EDGE + order[i] * n, EDGE), n)
        out[rows, :] = pairs[i // 2][(i % 2) * n : (i % 2 + 1) * n, :].astype(F32)


def pick(ref, order, size):
    n = ref.shape[0] // size
    return jnp.concatenate(
        [ref[pl.ds(pl.multiple_of(order[i] * n, EDGE), n), :] for i in range(size)], axis=0
    )


def joined_rows(refs):
    return jnp.concatenate([r[...] for r in refs], axis=0)


def tap_masks(seg, taps, count):
    own = seg[EDGE : EDGE + count, :]
    first = EDGE - taps // 2
    return [(seg[first + k : first + k + count, :] == own).astype(F32) for k in range(taps)]


def convolve_kernel(order, seg, taps_ref, *refs, taps):
    pairs, (conv_ref, sums_ref, wide) = refs[:-3], refs[-3:]
    count = conv_ref.shape[0]
    lay_out(order, pairs, wide)
    first = EDGE - taps // 2
    total = None
    for k, mask in enumerate(tap_masks(seg, taps, count)):
        term = (wide[first + k : first + k + count, :] * mask) * taps_ref[k : k + 1, :]
        total = term if total is None else total + term
    conv_ref[...] = total
    sums_ref[0:1, :] = jnp.sum(total, axis=0, keepdims=True)
    sums_ref[1:2, :] = jnp.sum(total * total, axis=0, keepdims=True)


def convolve(order, seg, taps, pairs):
    count, share = seg.shape[0] - 2 * EDGE, pairs[0].shape[1]
    return pl.pallas_call(
        functools.partial(convolve_kernel, taps=taps.shape[0]),
        in_specs=[SMEM] + vmem(2 + len(pairs)),
        out_shape=[
            jax.ShapeDtypeStruct((count, share), F32),
            jax.ShapeDtypeStruct((2, share), F32),
        ],
        scratch_shapes=[pltpu.VMEM((count + 2 * EDGE, share), F32)],
        compiler_params=params(16),
        cost_estimate=cost(0, *pairs, *pairs, *pairs),
    )(order, seg, taps, *pairs)


def bn_stats(moments, total):
    centre = moments[0:1, :] / total
    return centre, lax.rsqrt(moments[1:2, :] / total - centre * centre + EPS)


def bn_kernel(order, conv, moments, gain, bias, w, e_ref, slope_ref, *refs, total):
    size = len(refs)
    n = conv.shape[0] // size
    centre, inverse = bn_stats(moments[...], total)
    shifted = (pick(conv, order, size) - centre) * inverse * gain[...] + bias[...]
    sig = jax.nn.sigmoid(shifted)
    e = (shifted * sig).astype(BF)
    e_ref[...] = e
    slope_ref[...] = (sig * (1.0 + shifted * (1.0 - sig))).astype(BF)
    p = mm(e, w[...])
    for i in range(size):
        refs[i % 2 * (size // 2) + i // 2][...] = p[i * n : (i + 1) * n].astype(
            BF if i % 2 else F32
        )


def chunk_shapes(n, d, size):
    return [jax.ShapeDtypeStruct((n, d), F32)] * (size // 2) + [
        jax.ShapeDtypeStruct((n, d), BF)
    ] * (size // 2)


def bn_forward(order, conv, moments, gain, bias, w, total):
    count, share = conv.shape
    d, size = w.shape[1], lax.axis_size("tm")
    out = pl.pallas_call(
        functools.partial(bn_kernel, total=total),
        in_specs=[SMEM] + vmem(5),
        out_shape=[jax.ShapeDtypeStruct((count, share), BF)] * 2
        + chunk_shapes(count // size, d, size),
        compiler_params=params(24),
        cost_estimate=cost(2 * count * share * d, conv),
    )(order, conv, moments, gain, bias, w)
    return out[0], out[1], out[2 : 2 + size // 2], out[2 + size // 2 :]


def conv_out_grad_kernel(g0, g1, w, out):
    g = jnp.concatenate([g0[...], g1[...]], axis=0)
    out[...] = mm_nt(g, w[...])


def conv_out_grad(pair, w):
    n, d = pair[0].shape
    return pl.pallas_call(
        conv_out_grad_kernel,
        out_shape=jax.ShapeDtypeStruct((2 * n, w.shape[0]), F32),
        compiler_params=params(12),
        cost_estimate=cost(4 * n * d * w.shape[0], w),
    )(*pair, w)


def bn_sums_kernel(order, conv, slope, moments, *refs, total):
    pairs, (dn_ref, sums_ref) = refs[:-2], refs[-2:]
    dn = joined_rows(pairs) * slope[...].astype(F32)
    dn_ref[...] = dn
    centre, inverse = bn_stats(moments[...], total)
    normed = (pick(conv, order, 2 * len(pairs)) - centre) * inverse
    sums_ref[0:1, :] = jnp.sum(dn, axis=0, keepdims=True)
    sums_ref[1:2, :] = jnp.sum(dn * normed, axis=0, keepdims=True)


def bn_back(order, conv, slope, moments, pairs, total):
    count, share = conv.shape
    return pl.pallas_call(
        functools.partial(bn_sums_kernel, total=total),
        in_specs=[SMEM] + vmem(3 + len(pairs)),
        out_shape=[
            jax.ShapeDtypeStruct((count, share), F32),
            jax.ShapeDtypeStruct((2, share), F32),
        ],
        compiler_params=params(16),
        cost_estimate=cost(0, conv, conv, conv),
    )(order, conv, slope, moments, *pairs)


def conv_back_kernel(
    order, seg, taps_ref, dn, conv, moments, sums, gain, w, *refs, taps, total, size
):
    chips = size // 2
    z, sig, slope = refs[:chips], refs[chips : 2 * chips], refs[2 * chips : 3 * chips]
    du_ref, dk_ref = refs[3 * chips : 3 * chips + 2]
    out, (c_wide, z_wide, dz_ref, dc_ref) = refs[3 * chips + 2 : -4], refs[-4:]
    count, share = dn.shape
    n = count // size
    centre, inverse = bn_stats(moments[...], total)
    normed = (pick(conv, order, size) - centre) * inverse
    dc = dn[...] - sums[0:1, :] / total - normed * (sums[1:2, :] / total)
    dc_ref[...] = (gain[...] * inverse * dc).astype(BF)
    lay_out(order, [dc_ref.at[2 * n * i : 2 * n * (i + 1)] for i in range(chips)], c_wide)
    lay_out(order, z, z_wide)
    first = EDGE - taps // 2
    masks = tap_masks(seg, taps, count)
    own = c_wide[EDGE : EDGE + count, :]
    dz = None
    for k in range(taps):
        mirror = taps - 1 - k
        near = c_wide[first + mirror : first + mirror + count, :] * masks[mirror]
        term = near * taps_ref[k : k + 1, :]
        dz = term if dz is None else dz + term
        dk_ref[k : k + 1, :] = jnp.sum(
            (z_wide[first + k : first + k + count, :] * masks[k]) * own, axis=0, keepdims=True
        )
    dz_ref[...] = dz
    dz = pick(dz_ref, order, size)
    du = jnp.concatenate(
        [dz * joined_rows(sig).astype(F32), dz * joined_rows(slope).astype(F32)], axis=1
    ).astype(BF)
    du_ref[...] = du
    p = mm_nt(du, w[...])
    for i in range(size):
        out[i % 2 * chips + i // 2][...] = p[i * n : (i + 1) * n].astype(BF if i % 2 else F32)


def conv_back(order, seg, taps, dn, conv, moments, sums, gain, w, kept, total):
    count, share = dn.shape
    d, size = w.shape[0], lax.axis_size("tm")
    wide = pltpu.VMEM((count + 2 * EDGE, share), F32)
    z, sig, slope = zip(*kept)
    out = pl.pallas_call(
        functools.partial(conv_back_kernel, taps=taps.shape[0], total=total, size=size),
        in_specs=[SMEM] + vmem(8 + 3 * len(kept)),
        out_shape=[
            jax.ShapeDtypeStruct((count, 2 * share), BF),
            jax.ShapeDtypeStruct((taps.shape[0], share), F32),
        ]
        + chunk_shapes(count // size, d, size),
        scratch_shapes=[
            wide,
            wide,
            pltpu.VMEM((count, share), F32),
            pltpu.VMEM((count, share), BF),
        ],
        compiler_params=params(30),
        cost_estimate=cost(4 * count * share * d, dn, dn, dn),
    )(order, seg, taps, dn, conv, moments, sums, gain, w, *z, *sig, *slope)
    return out[0], out[1], out[2 : 2 + size // 2], out[2 + size // 2 :]


def conv_grads_kernel(du, e, *refs):
    size = (len(refs) - 2) // 2
    in_ref, out_ref = refs[-2:]
    in_ref[...] = mm_tn(joined_rows(refs[:size]), du[...]).astype(BF)
    out_ref[...] = mm_tn(e[...], joined_rows(refs[size : 2 * size])).astype(BF)


def conv_grads(h, g, du, e):
    d, share = h[0].shape[1], e.shape[1]
    return pl.pallas_call(
        conv_grads_kernel,
        out_shape=[
            jax.ShapeDtypeStruct((d, 2 * share), BF),
            jax.ShapeDtypeStruct((share, d), BF),
        ],
        compiler_params=params(24),
        cost_estimate=cost(6 * e.shape[0] * share * d, du, e),
    )(du, e, *h, *g)


def shards(
    frames,
    segments,
    ffn1_in,
    ffn1_out,
    query_w,
    key_w,
    value_w,
    attn_out,
    conv_in,
    conv_out,
    ffn2_in,
    ffn2_out,
    norm_gains,
    conv_kernel,
    bn_gain,
    bn_bias,
    rel_table,
    cotangent,
):
    rows, size = lax.axis_size("rows"), lax.axis_size("tm")
    t = lax.axis_index("tm")
    own, width = frames.shape[1], frames.shape[2]
    length = own * size
    share = width // size
    heads = rel_table.shape[0] // size
    taps = conv_kernel.shape[0]
    frame_total = float(length * rows)
    seg = segments[0]
    table = lax.dynamic_slice_in_dim(rel_table, t * heads, heads, 0)
    depth = width // rows
    unit = depth // size

    def mine(v):
        v = v.reshape(-1, rows, size, unit)
        return lax.dynamic_index_in_dim(v, t, 2, keepdims=False).reshape(-1, share)

    def placed(v):
        n = v.shape[0]
        out = jnp.zeros((n, rows, size, unit), F32)
        return lax.dynamic_update_index_in_dim(
            out, v.reshape(n, rows, unit), t, 2
        ).reshape(n, width)

    kernel_own = mine(conv_kernel)
    bn_gain_own, bn_bias_own = mine(bn_gain[None]), mine(bn_bias[None])
    seg_near = jnp.pad(seg, (EDGE, EDGE), constant_values=-1).reshape(-1, 1)

    perm = head_rows_perm()
    out_block = lax.ppermute(attn_out, ("rows", "tm"), perm)
    order = jnp.stack(
        [peer_index(dx, dc) for dx in range(size // 2) for dc in range(2)]
    ).astype(jnp.int32)
    f1, attn_part, sent = gather_ffn(ffn1_in, ffn1_out, (query_w, key_w, value_w, out_block))
    wide = conv_in.shape[1]
    pieces = exchange_all(
        [
            after(conv_in, sent)
            .reshape(depth, wide // depth, size, unit)
            .transpose(2, 0, 1, 3)
            .reshape(size, depth, wide // size),
            after(conv_out, sent).reshape(size, unit, share),
        ]
    )
    packed = [pack(side_by_side(p), width) for p in pieces]
    sent = jnp.concatenate(packed, axis=0)
    full = lax.all_gather(sent, "rows", axis=0, tiled=False)
    at = packed[0].shape[0]
    conv_in_w, conv_out_w = unpack(full[:, :at], wide), unpack(full[:, at:], width)
    f2, _, sent = gather_ffn(after(ffn2_in, sent), ffn2_out)

    inputs = frames[0].astype(F32)
    n1 = norm_rows(inputs, norm_gains[0])[0]
    h1, _ = spread(n1.astype(BF), lambda near: ())
    h1[0] = (after(h1[0][0], sent), h1[0][1])
    one = [ffn(pair, *f1) for pair in reversed(h1)][::-1]
    parts, attn_w = collect(
        [v[2] for v in one], [v[3] for v in one], lambda ready: ready(attn_part)
    )
    x1, n2 = add_norm(parts, inputs, norm_gains[1], 0.5)

    h2, local = spread(n2, lambda near: project(near, attn_w, 3 * share))
    pairs = [local] + [project(pair, attn_w, 3 * share) for pair in h2[1:]]
    qkv, att, lse, mine_a, theirs_a = attend(order, pairs, seg, table, attn_w)
    parts, _ = collect(mine_a, theirs_a)
    x2, n3 = add_norm(parts, x1, norm_gains[2], 1.0)

    h3, local = spread(n3, lambda near: glu(near, conv_in_w))
    kept = [local] + [glu(pair, conv_in_w) for pair in h3[1:]]
    conv, moments = convolve(order, seg_near, kernel_own, [v[0] for v in kept])
    moments = sum_axis(moments, "rows")
    e, e_slope, mine_c, theirs_c = bn_forward(
        order, conv, moments, bn_gain_own, bn_bias_own, conv_out_w, frame_total
    )
    parts, _ = collect(mine_c, theirs_c)
    x3, n4 = add_norm(parts, x2, norm_gains[3], 1.0)

    h4, local = spread(n4, lambda near: ffn(near, *f2))
    four = [local] + [ffn(pair, *f2) for pair in h4[1:]]
    parts, _ = collect([v[2] for v in four], [v[3] for v in four])
    output, d4, g, gain_five = turn(parts, x3, norm_gains[4], cotangent[0])

    g4, local = spread(g, lambda near: ffn_back(near, four[0][1], *f2))
    back = [local] + [ffn_back(p, four[i][1], *f2) for i, p in enumerate(g4[1:], 1)]
    parts, packed_four = collect(
        [v[1] for v in back],
        [v[2] for v in back],
        lambda ready: ffn_grads(
            [ready(v) for v in sum(h4, ())],
            sum(g4, ()),
            [v[0] for v in back],
            [ready(v[0]) for v in four],
        ),
    )
    d3, g, gain_four = back_norm(parts, x3, norm_gains[3], d4, 1.0)
    sum_four = scatter_rows(after(packed_four, g))

    g3, local = spread(g, lambda near: conv_out_grad(near, conv_out_w))
    pairs = [local] + [conv_out_grad(pair, conv_out_w) for pair in g3[1:]]
    dn, bn_part = bn_back(order, conv, e_slope, moments, pairs, frame_total)
    bn_sums = sum_axis(bn_part, "rows")
    du, d_kernel, mine_c, theirs_c = conv_back(
        order,
        seg_near,
        kernel_own,
        dn,
        conv,
        moments,
        bn_sums,
        bn_gain_own,
        conv_in_w,
        kept,
        frame_total,
    )
    parts, _ = collect(mine_c, theirs_c)
    d2, g, gain_three = back_norm(parts, x2, norm_gains[2], d3, 1.0)

    g2, local = spread(
        g,
        lambda near: (
            att_grad(near, attn_w, share),
            conv_grads([after(v, g) for v in sum(h3, ())], sum(g3, ()), du, e),
        ),
    )
    local, parts_three = local
    packed_three = pack_grads(parts_three)
    pairs = [local] + [att_grad(pair, attn_w, share) for pair in g2[1:]]
    dqkv, band, mine_a, theirs_a = attend_back(order, pairs, qkv, seg, table, lse, attn_w)

    def attention_sums(ready):
        packed = attend_grads(
            order, [ready(v) for v in sum(h2, ())], sum(g2, ()), dqkv, att
        )
        if packed.shape[2] == packed_three.shape[2]:
            return (jnp.concatenate([packed, packed_three], axis=1),)
        return packed, packed_three

    parts, packed_mid = collect(mine_a, theirs_a, attention_sums)
    d1, g, gain_two = back_norm(parts, x1, norm_gains[1], d2, 0.5)
    if len(packed_mid) == 1:
        sum_mid = scatter_rows(packed_mid[0])
        sum_two, sum_three = sum_mid[:depth], sum_mid[depth:]
    else:
        sum_two, sum_three = (scatter_rows(v) for v in packed_mid)

    g1, local = spread(g, lambda near: ffn_back(near, one[0][1], *f1))
    back = [local] + [ffn_back(p, one[i][1], *f1) for i, p in enumerate(g1[1:], 1)]
    packed_one = ffn_grads(
        sum(h1, ()), sum(g1, ()), [v[0] for v in back], [v[0] for v in one]
    )
    sum_one = scatter_rows(packed_one)
    parts, _ = collect([v[1] for v in back], [v[2] for v in back])
    grad, _, gain_one = back_norm(parts, inputs, norm_gains[0], d1, 1.0)
    grad_frames = grad.astype(BF)[None]

    def ffn_parts(total):
        if total.shape == (2 * depth, width) and ffn1_in.shape[1] == width:
            return total[:depth], total[depth:]
        like = [
            jax.ShapeDtypeStruct((width, ffn1_in.shape[1]), BF),
            jax.ShapeDtypeStruct((ffn1_in.shape[1], width), BF),
        ]
        return unpack_grads(total, like)

    def ffn_owned(total):
        if whole_lanes(ffn1_in.shape, ffn1_out.shape):
            return returned_ffn(total, ffn1_in.shape, ffn1_out.shape)
        g_in, g_out = ffn_parts(total)
        return (
            ffn_back_in(g_in, ffn1_in.shape, ffn1_out.shape),
            ffn_back_out(g_out, ffn1_out.shape),
        )

    grad_ffn2_in, grad_ffn2_out = ffn_owned(sum_four)
    grad_query, grad_key, grad_value, d_block = (
        sum_two[:, i * share : (i + 1) * share] for i in range(4)
    )
    grad_query, grad_key, grad_value = (v.astype(F32) for v in (grad_query, grad_key, grad_value))
    grad_attn_out = lax.ppermute(d_block, ("rows", "tm"), [(b, a) for a, b in perm]).astype(F32)
    d_in, d_out = unpack_grads(sum_three, parts_three)
    d_in, d_out = exchange_all(
        [
            d_in.reshape(depth, size, -1).transpose(1, 0, 2),
            d_out.reshape(unit, size, share).transpose(1, 0, 2),
        ]
    )
    grad_conv_in = (
        d_in.reshape(size, depth, wide // depth, unit)
        .transpose(1, 2, 0, 3)
        .reshape(depth, wide)
        .astype(F32)
    )
    grad_conv_out = d_out.reshape(depth, share).astype(F32)
    grad_ffn1_in, grad_ffn1_out = ffn_owned(sum_one)

    table_row = lax.dynamic_update_slice_in_dim(
        jnp.zeros(rel_table.shape, F32), table_grad(band), t * heads, 0
    ).reshape(1, -1)
    table_row = jnp.pad(table_row, ((0, 0), (0, width - table_row.shape[1])))
    small = jnp.concatenate(
        [
            gain_one,
            gain_two,
            gain_three,
            gain_four,
            gain_five,
            placed(d_kernel),
            placed(bn_part),
            table_row,
        ],
        axis=0,
    )
    small = sum_axis(sum_axis(small, "tm"), "rows")
    table_size = rel_table.shape[0] * rel_table.shape[1]
    return (
        output[None],
        grad_frames,
        grad_ffn1_in,
        grad_ffn1_out,
        grad_query,
        grad_key,
        grad_value,
        grad_attn_out,
        grad_conv_in,
        grad_conv_out,
        grad_ffn2_in,
        grad_ffn2_out,
        small[:5],
        small[5 : 5 + taps],
        small[6 + taps],
        small[5 + taps],
        small[7 + taps, :table_size].reshape(rel_table.shape),
    )


def solution(mesh):
    split, copied = P("rows", "tm"), P()
    sequence = P("rows", "tm", None)
    return jax.shard_map(
        shards,
        mesh=mesh,
        in_specs=(sequence, P("rows", None)) + (split,) * 10 + (copied,) * 5 + (sequence,),
        out_specs=(sequence, sequence) + (split,) * 10 + (copied,) * 5,
        check_vma=False,
    )
```

```python
import functools

import jax
import jax.numpy as jnp
from jax import lax
from jax.experimental import pallas as pl
from jax.experimental.pallas import tpu as pltpu
from jax.sharding import PartitionSpec as P

HEAD_DIM = 128
RELMAX = 8
LANES = 128
EPS = 1e-05
LOG2E = 1.4426950408889634
BF = jnp.bfloat16
F32 = jnp.float32
SMEM = pl.BlockSpec(memory_space=pltpu.SMEM)


def vmem(count):
    return [pl.BlockSpec(memory_space=pltpu.VMEM)] * count


def params(limit):
    return pltpu.CompilerParams(vmem_limit_bytes=limit * 1024 * 1024)


def cost(flops, *arrays):
    return pl.CostEstimate(
        flops=flops, bytes_accessed=sum(a.size * a.dtype.itemsize for a in arrays), transcendentals=0
    )


def mm(a, b):
    return jnp.dot(a, b, preferred_element_type=F32)


def mm_tn(a, b):
    return lax.dot_general(a, b, (((0,), (0,)), ((), ())), preferred_element_type=F32)


def mm_nt(a, b):
    return lax.dot_general(a, b, (((1,), (1,)), ((), ())), preferred_element_type=F32)


def norm_rows(v, g):
    center = v - jnp.mean(v, axis=-1, keepdims=True)
    spread = jnp.mean(center * center, axis=-1, keepdims=True)
    inverse = lax.rsqrt(spread + EPS)
    normed = center * inverse
    return normed * g, normed, inverse


def norm_back(grad, normed, inverse, g):
    scaled = grad * g
    back = inverse * (
        scaled
        - jnp.mean(scaled, axis=-1, keepdims=True)
        - normed * jnp.mean(scaled * normed, axis=-1, keepdims=True)
    )
    return back, jnp.sum(grad * normed, axis=0)


def tm_peer(dx, dc):
    size = lax.axis_size("tm")
    chips = size // 2
    return [
        (((t // 2 + dx) % chips) * 2 + ((t % 2) ^ dc), t) for t in range(size)
    ]


def from_peer(a, dx, dc):
    return lax.ppermute(a, "tm", tm_peer(dx, dc))


def peer_index(dx, dc):
    chips = lax.axis_size("tm") // 2
    t = lax.axis_index("tm")
    return lax.rem(t // 2 + dx, chips) * 2 + jnp.bitwise_xor(t % 2, dc)


def spread(a, local):
    chips = lax.axis_size("tm") // 2
    far = [from_peer(a, dx, 0) for dx in range(1, chips)]
    near = (a, from_peer(a, 0, 1))
    done = local(near)
    far = [after(b, *jax.tree.leaves(done)) for b in far]
    return [near] + [(b, from_peer(b, 0, 1)) for b in far], done


def collect(mine, theirs, beside=None):
    chips = lax.axis_size("tm") // 2
    sent = [
        (mine[dx] + from_peer(theirs[dx], 0, 1).astype(F32)).astype(BF) for dx in range(1, chips)
    ]
    near = from_peer(theirs[0], 0, 1)
    got = [from_peer(q, chips - dx, 0) for dx, q in enumerate(sent, 1)]
    done = beside(lambda v: after(v, *sent)) if beside else None
    got = [after(v, near, *jax.tree.leaves(done)) for v in got]
    return [mine[0], near] + got, done


def exchange_tm(pieces):
    size = lax.axis_size("tm")
    chips = size // 2
    t = lax.axis_index("tm")
    out = jnp.zeros(pieces.shape, pieces.dtype)
    out = lax.dynamic_update_index_in_dim(
        out, lax.dynamic_index_in_dim(pieces, t, 0, keepdims=False), t, 0
    )
    for dx in range(chips):
        for dc in range(2):
            if dx or dc:
                piece = lax.dynamic_index_in_dim(
                    pieces, peer_index(chips - dx, dc), 0, keepdims=False
                )
                out = lax.dynamic_update_index_in_dim(
                    out, from_peer(piece, dx, dc), peer_index(dx, dc), 0
                )
    return out


def sum_axis(v, axis):
    size, bit = lax.axis_size(axis), 1
    while bit < size:
        v = v + lax.ppermute(v, axis, [(i, i ^ bit) for i in range(size)])
        bit *= 2
    return v


def pack(a, width):
    m, w = a.shape
    f = width // w
    if f * w != width or m % f:
        return a.reshape(-1, width)
    return jnp.concatenate([a[i * (m // f) : (i + 1) * (m // f)] for i in range(f)], axis=1)


def unpack(full, w):
    rows, n, width = full.shape
    f = width // w
    if f * w != width:
        return full.reshape(-1, w)
    if f == 1:
        return full.reshape(-1, w)
    parts = [full[:, None, :, i * w : (i + 1) * w] for i in range(f)]
    return jnp.concatenate(parts, axis=1).reshape(-1, w)


def pack_rows(p, width):
    rows = lax.axis_size("rows")
    m, w = p.shape[0] // rows, p.shape[1]
    f = width // w
    q = p.reshape(rows, m, w)
    if f * w != width or m % f:
        return q.reshape(rows, -1, width)
    return jnp.concatenate([q[:, i * (m // f) : (i + 1) * (m // f)] for i in range(f)], axis=2)


def pack_grads(parts):
    width = max(p.shape[1] for p in parts)
    return jnp.concatenate([pack_rows(p, width) for p in parts], axis=1)


def unpack_grads(total, parts):
    rows = lax.axis_size("rows")
    width = total.shape[1]
    out, at = [], 0
    for p in parts:
        n = p.size // (rows * width)
        out.append(unpack(total[None, at : at + n], p.shape[1]))
        at += n
    return out


def scatter_parity(own, near):
    rows = lax.axis_size("rows")
    packed = (own.astype(F32) + near.astype(F32)).astype(BF)
    return lax.psum_scatter(
        packed,
        "rows",
        scatter_dimension=0,
        tiled=False,
        axis_index_groups=[list(range(y, rows, 2)) for y in range(2)],
    )


def scatter_rows(packed):
    return lax.psum_scatter(packed, "rows", scatter_dimension=0, tiled=False)


def gather_ffn(w_in, w_out, more=()):
    m, width = w_in.shape[0], w_out.shape[1] * lax.axis_size("tm")
    side = sum(v.shape[1] for v in more)
    if whole_lanes(w_in.shape, w_out.shape) and (not more or side == width):
        sent = exchanged_ffn(w_in, w_out, more)
        full = lax.all_gather(sent, "rows", axis=0, tiled=False)
        return (Weight(full, 0, m), Weight(full, m, m)), full[:, 2 * m :].reshape(-1, width), sent
    sent = [side_by_side(p) for p in exchange_all(ffn_pieces(w_in, w_out))]
    full = [
        lax.all_gather(p, "rows", axis=0, tiled=True)
        for p in sent + ([jnp.concatenate(more, axis=1)] if more else [])
    ]
    return (Weight(full[0]), Weight(full[1])), full[-1], sent[0]


def exchange_all(pieces):
    size = lax.axis_size("tm")
    width = max(p.shape[2] for p in pieces)
    if any(p[0].size % width for p in pieces):
        return [exchange_tm(p) for p in pieces]
    flat = [p.reshape(size, -1, width) for p in pieces]
    got = exchange_tm(jnp.concatenate(flat, axis=1))
    out, at = [], 0
    for p, q in zip(pieces, flat):
        out.append(got[:, at : at + q.shape[1]].reshape(p.shape))
        at += q.shape[1]
    return out


def after(a, *others):
    return lax.optimization_barrier((a,) + others)[0]


def ffn_pieces(w_in, w_out):
    size = lax.axis_size("tm")
    unit = w_out.shape[0] // size
    m, w = w_in.shape
    a = w_in.reshape(m, w // (size * unit), size, unit).transpose(2, 0, 1, 3)
    return [a.reshape(size, m, w // size), w_out.reshape(size, unit, w_out.shape[1])]


def side_by_side(pieces):
    return pieces.transpose(1, 0, 2).reshape(pieces.shape[1], -1)


def ffn_back_in(a, like_in, like_out):
    size = lax.axis_size("tm")
    m, w = like_in
    unit = like_out[0] // size
    a = exchange_tm(a.reshape(m, size, -1).transpose(1, 0, 2))
    a = a.reshape(size, m, w // (size * unit), unit).transpose(1, 2, 0, 3).reshape(m, w)
    return a.astype(F32)


def ffn_back_out(b, like_out):
    size = lax.axis_size("tm")
    b = exchange_tm(b.reshape(b.shape[0], size, -1).transpose(1, 0, 2))
    return b.reshape(like_out).astype(F32)


def peers():
    chips = lax.axis_size("tm") // 2
    rel = [(dx, dc) for dx in range(chips) for dc in range(2)]
    index = lambda v: jnp.stack(v).astype(jnp.int32)
    return (
        rel,
        index([peer_index(dx, dc) for dx, dc in rel]),
        index([peer_index(chips - dx if dx else 0, dc) for dx, dc in rel]),
    )


def whole_lanes(like_in, like_out):
    unit = like_out[0] // lax.axis_size("tm")
    return unit % LANES == 0 and unit == like_in[0] and like_in[1] == like_out[1] * lax.axis_size("tm")


def cut_kernel(to, w_in, w_out, *outs, unit):
    size, m = len(outs), w_in.shape[0]
    for i, out in enumerate(outs):
        for j in range(out.shape[1] // unit):
            at = pl.multiple_of(j * size * unit + to[i] * unit, unit)
            out[:m, j * unit : (j + 1) * unit] = w_in[:, pl.ds(at, unit)]
        out[m:, :] = w_out[pl.ds(pl.multiple_of(to[i] * unit, unit), unit), :]


def lay_kernel(order, *refs, size):
    out = refs[-1]
    n, w = refs[0].shape
    for i in range(size):
        out[:n, pl.ds(pl.multiple_of(order[i] * w, w), w)] = refs[i][...]
    at = 0
    for r in refs[size:-1]:
        out[n:, at : at + r.shape[1]] = r[...]
        at += r.shape[1]


def exchanged_ffn(w_in, w_out, more=()):
    size = lax.axis_size("tm")
    rel, order, to = peers()
    m, unit = w_in.shape[0], w_out.shape[0] // size
    w = w_in.shape[1] // size
    pieces = pl.pallas_call(
        functools.partial(cut_kernel, unit=unit),
        in_specs=[SMEM] + vmem(2),
        out_shape=[jax.ShapeDtypeStruct((m + unit, w), BF)] * size,
        compiler_params=params(60),
        cost_estimate=cost(0, w_in, w_out),
    )(to, w_in, w_out)
    got = [pieces[0]] + [from_peer(p, *at) for p, at in zip(pieces[1:], rel[1:])]
    n = m + unit + (more[0].shape[0] if more else 0)
    return pl.pallas_call(
        functools.partial(lay_kernel, size=size),
        in_specs=[SMEM] + vmem(size + len(more)),
        out_shape=jax.ShapeDtypeStruct((n, w * size), BF),
        compiler_params=params(60),
        cost_estimate=cost(0, w_in, w_out),
    )(order, *got, *more)


def split_kernel(to, total, *outs):
    w = outs[0].shape[1]
    for i, out in enumerate(outs):
        out[...] = total[:, pl.ds(pl.multiple_of(to[i] * w, w), w)]


def place_kernel(order, *refs, unit):
    size = len(refs) - 2
    g_in, g_out = refs[-2:]
    m = g_in.shape[0]
    for i in range(size):
        for j in range(refs[i].shape[1] // unit):
            at = pl.multiple_of(j * size * unit + order[i] * unit, unit)
            g_in[:, pl.ds(at, unit)] = refs[i][:m, j * unit : (j + 1) * unit].astype(F32)
        rows = pl.ds(pl.multiple_of(order[i] * unit, unit), unit)
        g_out[rows, :] = refs[i][m:, :].astype(F32)


def returned_ffn(total, like_in, like_out):
    size = lax.axis_size("tm")
    rel, order, to = peers()
    n, w = total.shape[0], total.shape[1] // size
    pieces = pl.pallas_call(
        split_kernel,
        in_specs=[SMEM] + vmem(1),
        out_shape=[jax.ShapeDtypeStruct((n, w), BF)] * size,
        compiler_params=params(8),
        cost_estimate=cost(0, total, total),
    )(to, total)
    got = [pieces[0]] + [from_peer(p, *at) for p, at in zip(pieces[1:], rel[1:])]
    return pl.pallas_call(
        functools.partial(place_kernel, unit=like_out[0] // size),
        in_specs=[SMEM] + vmem(size),
        out_shape=[jax.ShapeDtypeStruct(like_in, F32), jax.ShapeDtypeStruct(like_out, F32)],
        compiler_params=params(8),
        cost_estimate=cost(0, total, total, total),
    )(order, *got)


def head_rows_perm():
    rows, size = lax.axis_size("rows"), lax.axis_size("tm")
    perm = []
    for r in range(rows):
        for t in range(size):
            k, u = divmod(r, size)
            perm.append(((t * (rows // size) + k) * size + u, r * size + t))
    return perm


def whole(shape):
    return pl.BlockSpec(shape, lambda *_: (0,) * len(shape))


def flat(v):
    return v.reshape(-1, v.shape[-1])


class Weight:
    def __init__(self, array, first=0, m=None):
        self.array, self.first, self.m = array, first, m
        if m is not None:
            self.shape = (array.shape[0] * m, array.shape[2])
        else:
            self.shape = array.shape

    def all(self):
        if self.m is None:
            return whole(self.shape)
        unit = self.first // self.m
        return pl.BlockSpec(
            (self.array.shape[0], self.m, self.shape[1]), lambda *_: (0, unit, 0)
        )


def ffn_kernel(h0, h1, w_in, w_out, s_ref, slope_ref, mine, theirs):
    n = h0.shape[0]
    h = jnp.concatenate([h0[...], h1[...]], axis=0)
    w_a, w_b = flat(w_in[...]), flat(w_out[...])
    units = w_a.shape[1]
    total = None
    for half in range(2):
        at = slice(half * units // 2, (half + 1) * units // 2)
        a = mm(h, w_a[:, at])
        sig = jax.nn.sigmoid(a)
        act = (a * sig).astype(BF)
        s_ref[:, at] = act
        slope_ref[:, at] = (sig * (1.0 + a * (1.0 - sig))).astype(BF)
        p = mm(act, w_b[at])
        total = p if total is None else total + p
    mine[...] = total[:n]
    theirs[...] = total[n:].astype(BF)


def ffn(pair, w_in, w_out):
    n, d = pair[0].shape
    units = w_in.shape[1]
    return pl.pallas_call(
        ffn_kernel,
        grid=(1,),
        in_specs=[whole((n, d)), whole((n, d)), w_in.all(), w_out.all()],
        out_specs=[whole((2 * n, units))] * 2 + [whole((n, d))] * 2,
        out_shape=[jax.ShapeDtypeStruct((2 * n, units), BF)] * 2
        + [jax.ShapeDtypeStruct((n, d), F32), jax.ShapeDtypeStruct((n, d), BF)],
        compiler_params=params(24),
        cost_estimate=cost(8 * n * d * units, w_in.array),
    )(*pair, w_in.array, w_out.array)


def ffn_back_kernel(g0, g1, slope, w_in, w_out, da_ref, mine, theirs):
    n = g0.shape[0]
    g = jnp.concatenate([g0[...], g1[...]], axis=0)
    w_a, w_b = flat(w_in[...]), flat(w_out[...])
    units = w_a.shape[1]
    total = None
    for half in range(2):
        at = slice(half * units // 2, (half + 1) * units // 2)
        da = (mm_nt(g, w_b[at]) * slope[:, at].astype(F32)).astype(BF)
        da_ref[:, at] = da
        p = mm_nt(da, w_a[:, at])
        total = p if total is None else total + p
    mine[...] = total[:n]
    theirs[...] = total[n:].astype(BF)


def ffn_back(pair, slope, w_in, w_out):
    n, d = pair[0].shape
    units = w_in.shape[1]
    return pl.pallas_call(
        ffn_back_kernel,
        grid=(1,),
        in_specs=[whole((n, d))] * 2 + [whole((2 * n, units)), w_in.all(), w_out.all()],
        out_specs=[whole((2 * n, units))] + [whole((n, d))] * 2,
        out_shape=[
            jax.ShapeDtypeStruct((2 * n, units), BF),
            jax.ShapeDtypeStruct((n, d), F32),
            jax.ShapeDtypeStruct((n, d), BF),
        ],
        compiler_params=params(24),
        cost_estimate=cost(8 * n * d * units, w_in.array),
    )(*pair, slope, w_in.array, w_out.array)


def ffn_grads_kernel(*refs):
    out = refs[-1]
    count = (len(refs) - 1) // 6
    h, g = refs[: 2 * count], refs[2 * count : 4 * count]
    da, s = refs[4 * count : 5 * count], refs[5 * count : 6 * count]
    half = out.shape[1] // 2
    join = lambda v: jnp.concatenate([r[...] for r in v], axis=0)
    out[:, :half, :] = mm_tn(join(h), join(da)).astype(BF).reshape(out.shape[0], half, -1)
    out[:, half:, :] = mm_tn(join(s), join(g)).astype(BF).reshape(out.shape[0], half, -1)


def ffn_grads(h, g, da, s):
    rows = lax.axis_size("rows")
    n, d = h[0].shape
    units, tile = da[0].shape[1], d // 2
    m = d // rows
    if units != d or tile % m:
        h, g, da, s = (jnp.concatenate(v, axis=0) for v in (h, g, da, s))
        return pack_grads([mm_tn(h, da).astype(BF), mm_tn(s, g).astype(BF)])
    part = pl.BlockSpec((n, tile), lambda j: (0, j))
    column = pl.BlockSpec((2 * n, tile), lambda j: (0, j))
    return pl.pallas_call(
        ffn_grads_kernel,
        grid=(d // tile,),
        in_specs=[part] * len(h)
        + [whole((n, d))] * len(g)
        + [whole((2 * n, units))] * len(da)
        + [column] * len(s),
        out_specs=pl.BlockSpec((tile // m, 2 * m, d), lambda j: (j, 0, 0)),
        out_shape=jax.ShapeDtypeStruct((rows, 2 * m, d), BF),
        compiler_params=params(36),
        cost_estimate=cost(4 * len(h) * n * d * units, *h),
    )(*h, *g, *da, *s)


def by_parity(packed):
    rows = packed.shape[0]
    odd = lax.axis_index("rows") % 2
    v = packed.reshape(rows // 2, 2, *packed.shape[1:])
    return [
        lax.dynamic_index_in_dim(v, odd, 1, keepdims=False),
        lax.dynamic_index_in_dim(v, 1 - odd, 1, keepdims=False),
    ]


def parity_grads_kernel(odd_ref, *refs):
    outs, refs = refs[-2:], refs[:-2]
    count = len(refs) // 6
    h, g = refs[: 2 * count], refs[2 * count : 4 * count]
    da, s = refs[4 * count : 5 * count], refs[5 * count : 6 * count]
    steps, m2, width = outs[0].shape
    half = m2 // 2
    join = lambda v: jnp.concatenate([r[...] for r in v], axis=0)
    even = odd_ref[0] == 0
    for i, (a, b) in enumerate(((h, da), (s, g))):
        v = mm_tn(join(a), join(b)).astype(BF).reshape(steps, 2, half, width)
        rows = slice(i * half, (i + 1) * half)
        outs[0][:, rows, :] = jnp.where(even, v[:, 0], v[:, 1])
        outs[1][:, rows, :] = jnp.where(even, v[:, 1], v[:, 0])


def parity_grads(h, g, da, s):
    rows = lax.axis_size("rows")
    n, d = h[0].shape
    units, tile = da[0].shape[1], d // 2
    m = d // rows
    odd = (lax.axis_index("rows") % 2).astype(jnp.int32)
    if units != d or tile % (2 * m):
        h, g, da, s = (jnp.concatenate(v, axis=0) for v in (h, g, da, s))
        return by_parity(pack_grads([mm_tn(h, da).astype(BF), mm_tn(s, g).astype(BF)]))
    part = pl.BlockSpec((n, tile), lambda j: (0, j))
    column = pl.BlockSpec((2 * n, tile), lambda j: (0, j))
    return pl.pallas_call(
        parity_grads_kernel,
        grid=(d // tile,),
        in_specs=[pl.BlockSpec(memory_space=pltpu.SMEM)]
        + [part] * len(h)
        + [whole((n, d))] * len(g)
        + [whole((2 * n, units))] * len(da)
        + [column] * len(s),
        out_specs=[pl.BlockSpec((tile // m // 2, 2 * m, d), lambda j: (j, 0, 0))] * 2,
        out_shape=[jax.ShapeDtypeStruct((rows // 2, 2 * m, d), BF)] * 2,
        compiler_params=params(36),
        cost_estimate=cost(4 * len(h) * n * d * units, *h),
    )(odd.reshape(1), *h, *g, *da, *s)


def add_norm_kernel(*refs, scale):
    x_ref, gain, x_new, h_ref = refs[-4:]
    total = refs[0][...]
    for r in refs[1:-4]:
        total = total + r[...].astype(F32)
    x = x_ref[...] + scale * total
    x_new[...] = x
    h_ref[...] = norm_rows(x, gain[...])[0].astype(BF)


def add_norm(parts, x, gain, scale):
    n, d = x.shape
    return pl.pallas_call(
        functools.partial(add_norm_kernel, scale=scale),
        out_shape=[pltpu.HBM((n, d), F32), jax.ShapeDtypeStruct((n, d), BF)],
        compiler_params=params(12),
        cost_estimate=cost(0, x, x, x),
    )(*parts, x, gain[None])


def turn_kernel(*refs):
    x_ref, gain, cot, out, d_ref, g_ref, gain_ref = refs[-7:]
    total = refs[0][...]
    for r in refs[1:-7]:
        total = total + r[...].astype(F32)
    y, normed, inverse = norm_rows(x_ref[...] + 0.5 * total, gain[...])
    out[...] = y.astype(BF)
    back, gain_sum = norm_back(cot[...].astype(F32), normed, inverse, gain[...])
    d_ref[...] = back
    g_ref[...] = (0.5 * back).astype(BF)
    gain_ref[...] = gain_sum[None]


def turn(parts, x, gain, cot):
    n, d = x.shape
    return pl.pallas_call(
        turn_kernel,
        out_shape=[
            jax.ShapeDtypeStruct((n, d), BF),
            pltpu.HBM((n, d), F32),
            jax.ShapeDtypeStruct((n, d), BF),
            jax.ShapeDtypeStruct((1, d), F32),
        ],
        compiler_params=params(14),
        cost_estimate=cost(0, x, x, x),
    )(*parts, x, gain[None], cot)


def back_norm_kernel(*refs, scale):
    x_ref, gain, prev, d_ref, g_ref, gain_ref = refs[-6:]
    total = refs[0][...]
    for r in refs[1:-6]:
        total = total + r[...].astype(F32)
    _, normed, inverse = norm_rows(x_ref[...], gain[...])
    back, gain_sum = norm_back(total, normed, inverse, gain[...])
    d = prev[...] + back
    d_ref[...] = d
    g_ref[...] = (scale * d).astype(BF)
    gain_ref[...] = gain_sum[None]


def back_norm(parts, x, gain, prev, scale):
    n, d = x.shape
    return pl.pallas_call(
        functools.partial(back_norm_kernel, scale=scale),
        out_shape=[
            pltpu.HBM((n, d), F32),
            jax.ShapeDtypeStruct((n, d), BF),
            jax.ShapeDtypeStruct((1, d), F32),
        ],
        compiler_params=params(14),
        cost_estimate=cost(0, x, x, x),
    )(*parts, x, gain[None], prev)


def project_kernel(h0, h1, w, out):
    h = jnp.concatenate([h0[...], h1[...]], axis=0)
    out[...] = mm(h, w[...][:, : out.shape[1]]).astype(BF)


def project(pair, w, width):
    n, d = pair[0].shape
    return pl.pallas_call(
        project_kernel,
        grid=(1,),
        in_specs=[whole((n, d)), whole((n, d)), whole(w.shape)],
        out_specs=whole((2 * n, width)),
        out_shape=jax.ShapeDtypeStruct((2 * n, width), BF),
        compiler_params=params(20),
        cost_estimate=cost(4 * n * d * width, w),
    )(*pair, w)


def joined(v, size, depth):
    groups = v.shape[0] // (size * depth)
    cut = lambda k, u: v[(k * size + u) * depth : (k * size + u + 1) * depth]
    return jnp.concatenate(
        [jnp.concatenate([cut(k, u) for u in range(size)], axis=1) for k in range(groups)], axis=0
    )


def fill_bias(tab_ref, head, strip, length):
    lo, hi = length - LANES, length + 2 * LANES
    entry = lambda b: tab_ref[head, b] * LOG2E
    first, last = entry(0), entry(2 * RELMAX)
    offset = (
        lax.broadcasted_iota(jnp.int32, (LANES, hi - lo), 1)
        - LANES
        - lax.broadcasted_iota(jnp.int32, (LANES, hi - lo), 0)
    )
    tile = jnp.where(offset <= -RELMAX, first, last)
    for b in range(1, 2 * RELMAX):
        tile = jnp.where(offset == b - RELMAX, entry(b), tile)
    strip[:, :lo] = jnp.full((LANES, lo), first, F32)
    strip[:, lo:hi] = tile
    strip[:, hi:] = jnp.full((LANES, 2 * length - hi), last, F32)


def biased(q, k, seg_col, seg_row, strip, first, length):
    raw = mm_nt(q, k) * (HEAD_DIM ** (-0.5) * LOG2E)
    parts = [
        strip[:, length - (first + a) : 2 * length - (first + a)]
        for a in range(0, q.shape[0], LANES)
    ]
    bias = parts[0] if len(parts) == 1 else jnp.concatenate(parts, axis=0)
    return jnp.where(seg_col == seg_row, raw + bias, -jnp.inf)


def head_columns(n, head, heads):
    return pl.ds(pl.multiple_of((n * heads + head) * HEAD_DIM, HEAD_DIM), HEAD_DIM)


def attend_kernel(order, tab_ref, seg_row_ref, seg_col_ref, w_ref, *refs, size, depth):
    chips = size // 2
    pairs, (qkv, att, lse_ref) = refs[:chips], refs[chips : chips + 3]
    mine, theirs = refs[chips + 3 : 2 * chips + 3], refs[2 * chips + 3 : 3 * chips + 3]
    strip = refs[-1]
    length = qkv.shape[0]
    n = length // size
    head, heads = pl.program_id(0), pl.num_programs(0)
    at = lambda i: pl.ds(pl.multiple_of(order[i] * n, n), n)

    @pl.when(head == 0)
    def _():
        for i in range(size):
            qkv[at(i), :] = pairs[i // 2][(i % 2) * n : (i % 2 + 1) * n, :]

    fill_bias(tab_ref, head, strip, length)
    k, v = qkv[:, head_columns(1, head, heads)], qkv[:, head_columns(2, head, heads)]
    block = min(256, length)
    for first in range(0, length, block):
        own = slice(first, first + block)
        q = qkv[own, head_columns(0, head, heads)]
        sc = biased(q, k, seg_col_ref[own, :], seg_row_ref[...], strip, first, length)
        peak = jnp.max(sc, axis=1, keepdims=True)
        e = jnp.exp2(sc - peak)
        total = jnp.sum(e, axis=1, keepdims=True)
        inverse = 1.0 / total
        att[own, head_columns(0, head, heads)] = (mm(e.astype(BF), v) * inverse).astype(BF)
        lse_ref[0, own, :] = peak + jnp.log(total) * LOG2E

    @pl.when(head == heads - 1)
    def _():
        share = att.shape[1]
        w = joined(w_ref[...][:, -share:], size, depth)
        for i in range(size):
            p = mm(att[at(i), :], w)
            if i % 2:
                theirs[i // 2][...] = p.astype(BF)
            else:
                mine[i // 2][...] = p


def attend(order, pairs, seg_row, table, weight):
    size = 2 * len(pairs)
    length, heads = seg_row.shape[0], table.shape[0]
    share, d = heads * HEAD_DIM, weight.shape[0]
    n = length // size
    depth = d // lax.axis_size("rows")
    shape = jax.ShapeDtypeStruct
    out = pl.pallas_call(
        functools.partial(attend_kernel, size=size, depth=depth),
        grid=(heads,),
        in_specs=[
            pl.BlockSpec(memory_space=pltpu.SMEM),
            pl.BlockSpec(memory_space=pltpu.SMEM),
            whole((1, length)),
            whole((length, 1)),
            whole(weight.shape),
        ]
        + [whole((2 * n, 3 * share))] * len(pairs),
        out_specs=[
            whole((length, 3 * share)),
            whole((length, share)),
            pl.BlockSpec((1, length, 1), lambda h: (h, 0, 0)),
        ]
        + [whole((n, d))] * size,
        out_shape=[
            shape((length, 3 * share), BF),
            shape((length, share), BF),
            shape((heads, length, 1), F32),
        ]
        + [shape((n, d), F32)] * len(pairs)
        + [shape((n, d), BF)] * len(pairs),
        scratch_shapes=[pltpu.VMEM((LANES, 2 * length), F32)],
        compiler_params=params(32),
        cost_estimate=cost(6 * length * length * share, *pairs),
    )(order, table, seg_row.reshape(1, length), seg_row.reshape(length, 1), weight, *pairs)
    chips = len(pairs)
    return out[0], out[1], out[2], out[3 : 3 + chips], out[3 + chips :]


def att_grad_kernel(g0, g1, w_ref, out, *, size, depth):
    share = out.shape[1]
    w = joined(w_ref[...][:, -share:], size, depth)
    g = jnp.concatenate([g0[...], g1[...]], axis=0)
    out[...] = mm_nt(g, w).astype(BF)


def att_grad(pair, weight, share):
    n, d = pair[0].shape
    return pl.pallas_call(
        functools.partial(
            att_grad_kernel, size=lax.axis_size("tm"), depth=d // lax.axis_size("rows")
        ),
        grid=(1,),
        in_specs=[whole((n, d)), whole((n, d)), whole(weight.shape)],
        out_specs=whole((2 * n, share)),
        out_shape=jax.ShapeDtypeStruct((2 * n, share), BF),
        compiler_params=params(16),
        cost_estimate=cost(4 * n * d * share, weight),
    )(*pair, weight)


def attend_back_kernel(
    order, tab_ref, seg_row_ref, seg_col_ref, w_ref, qkv, lse_ref, *refs, size
):
    chips = size // 2
    pairs, (dqkv_ref, band_ref) = refs[:chips], refs[chips : chips + 2]
    mine, theirs = refs[chips + 2 : 2 * chips + 2], refs[2 * chips + 2 : 3 * chips + 2]
    strip, dk_sum, dv_sum, grad = refs[-4:]
    length = qkv.shape[0]
    n = length // size
    block = min(256, length)
    head, heads = pl.program_id(0), pl.num_programs(0)
    rows_of = lambda i: pl.ds(pl.multiple_of(order[i] * n, n), n)

    @pl.when(head == 0)
    def _():
        for i in range(size):
            grad[rows_of(i), :] = pairs[i // 2][(i % 2) * n : (i % 2 + 1) * n, :]

    fill_bias(tab_ref, head, strip, length)
    k, v = qkv[:, head_columns(1, head, heads)], qkv[:, head_columns(2, head, heads)]
    scale = HEAD_DIM ** (-0.5)
    at = lambda n: head_columns(n, head, heads)
    low = jnp.zeros((LANES, LANES), F32)
    high = jnp.zeros((LANES, LANES), F32)
    band = [jnp.zeros((LANES, LANES), F32) for _ in range(3)]
    for first in range(0, length, block):
        own = slice(first, first + block)
        q, do = qkv[own, at(0)], grad[own, at(0)]
        sc = biased(q, k, seg_col_ref[own, :], seg_row_ref[...], strip, first, length)
        p = jnp.exp2(sc - lse_ref[0, own, :])
        dp = mm_nt(do, v)
        inner = jnp.sum(p * dp, axis=1, keepdims=True)
        ds = (p * (dp - inner)).astype(BF)
        dv = mm_tn(p.astype(BF), do)
        dk = mm_tn(ds, q)
        if first == 0:
            dv_sum[...] = dv
            dk_sum[...] = dk
        else:
            dv_sum[...] += dv
            dk_sum[...] += dk
        dqkv_ref[own, at(0)] = (mm(ds, k) * scale).astype(BF)
        wide = ds.astype(F32)
        for a in range(0, block, LANES):
            for b in range(0, length, LANES):
                part = wide[a : a + LANES, b : b + LANES]
                apart = (b - first - a) // LANES
                if apart < -1:
                    low = low + part
                elif apart > 1:
                    high = high + part
                else:
                    band[apart + 1] = band[apart + 1] + part
    dqkv_ref[:, at(1)] = (dk_sum[...] * scale).astype(BF)
    dqkv_ref[:, at(2)] = dv_sum[...].astype(BF)
    for i, part in enumerate([low] + band + [high]):
        band_ref[0, :, i * LANES : (i + 1) * LANES] = part

    @pl.when(head == heads - 1)
    def _():
        w = w_ref[...][:, : dqkv_ref.shape[1]]
        for i in range(size):
            p = mm_nt(dqkv_ref[rows_of(i), :], w)
            if i % 2:
                theirs[i // 2][...] = p.astype(BF)
            else:
                mine[i // 2][...] = p


def attend_back(order, pairs, qkv, seg_row, table, lse, weight):
    size = 2 * len(pairs)
    length, heads = qkv.shape[0], table.shape[0]
    share, d = heads * HEAD_DIM, weight.shape[0]
    n = length // size
    shape = jax.ShapeDtypeStruct
    out = pl.pallas_call(
        functools.partial(attend_back_kernel, size=size),
        grid=(heads,),
        in_specs=[
            pl.BlockSpec(memory_space=pltpu.SMEM),
            pl.BlockSpec(memory_space=pltpu.SMEM),
            whole((1, length)),
            whole((length, 1)),
            whole(weight.shape),
            whole((length, 3 * share)),
            pl.BlockSpec((1, length, 1), lambda h: (h, 0, 0)),
        ]
        + [whole((2 * n, share))] * len(pairs),
        out_specs=[
            whole((length, 3 * share)),
            pl.BlockSpec((1, LANES, 5 * LANES), lambda h: (h, 0, 0)),
        ]
        + [whole((n, d))] * size,
        out_shape=[
            shape((length, 3 * share), BF),
            shape((heads, LANES, 5 * LANES), F32),
        ]
        + [shape((n, d), F32)] * len(pairs)
        + [shape((n, d), BF)] * len(pairs),
        scratch_shapes=[
            pltpu.VMEM((LANES, 2 * length), F32),
            pltpu.VMEM((length, HEAD_DIM), F32),
            pltpu.VMEM((length, HEAD_DIM), F32),
            pltpu.VMEM((length, share), BF),
        ],
        compiler_params=params(36),
        cost_estimate=cost(12 * length * length * share, *pairs),
    )(
        order,
        table,
        seg_row.reshape(1, length),
        seg_row.reshape(length, 1),
        weight,
        qkv,
        lse,
        *pairs,
    )
    chips = len(pairs)
    return out[0], out[1], out[2 : 2 + chips], out[2 + chips :]


def table_grad(band):
    offset = (
        lax.broadcasted_iota(jnp.int32, (LANES, 3 * LANES), 1)
        - LANES
        - lax.broadcasted_iota(jnp.int32, (LANES, 3 * LANES), 0)
    )
    middle = band[:, :, LANES : 4 * LANES]
    inner = [
        jnp.sum(jnp.where(offset == b, middle, 0.0), axis=(1, 2)) for b in range(1 - RELMAX, RELMAX)
    ]
    lower = jnp.sum(jnp.where(offset <= -RELMAX, middle, 0.0), axis=(1, 2))
    upper = jnp.sum(jnp.where(offset >= RELMAX, middle, 0.0), axis=(1, 2))
    lower = lower + jnp.sum(band[:, :, :LANES], axis=(1, 2))
    upper = upper + jnp.sum(band[:, :, 4 * LANES :], axis=(1, 2))
    return jnp.stack([lower] + inner + [upper], axis=1)


def attend_grads_kernel(order, dqkv, att, *refs):
    out, h_all, g_all = refs[-3:]
    size = (len(refs) - 3) // 2
    h, g = refs[:size], refs[size : 2 * size]
    n = h[0].shape[0]
    wide = dqkv.shape[1]
    for i in range(size):
        at = pl.ds(pl.multiple_of(order[i] * n, n), n)
        h_all[at, :] = h[i][...]
        g_all[at, :] = g[i][...]
    first = mm_tn(h_all[...], dqkv[...]).astype(BF)
    out[:, :, :wide] = first.reshape(out.shape[0], out.shape[1], wide)
    second = mm_tn(att[...], g_all[...]).astype(BF)
    depth, share = out.shape[1], out.shape[2] - wide
    per = second.shape[1] // share
    for i in range(out.shape[0]):
        k, u = divmod(i, per)
        out[i, :, wide:] = second[k * depth : (k + 1) * depth, u * share : (u + 1) * share]


def attend_grads(order, h, g, dqkv, att):
    rows, size = lax.axis_size("rows"), lax.axis_size("tm")
    n, d = h[0].shape
    length, share = att.shape
    m = d // rows
    if share != 2 * m:
        def place(chunks):
            out = jnp.zeros((size, n, d), BF)
            for i, v in enumerate(chunks):
                out = lax.dynamic_update_index_in_dim(out, v, order[i], 0)
            return out.reshape(length, d)

        first = mm_tn(place(h), dqkv).astype(BF)
        second = mm_tn(att, place(g)).astype(BF)
        second = (
            second.reshape(rows // size, m, size, share).transpose(0, 2, 1, 3).reshape(d, share)
        )
        return jnp.concatenate([first, second], axis=1).reshape(rows, m, -1)
    return pl.pallas_call(
        attend_grads_kernel,
        grid=(1,),
        in_specs=[
            pl.BlockSpec(memory_space=pltpu.SMEM),
            whole(dqkv.shape),
            whole(att.shape),
        ]
        + [whole((n, d))] * (2 * size),
        out_specs=whole((rows, m, 4 * share)),
        out_shape=jax.ShapeDtypeStruct((rows, m, 4 * share), BF),
        scratch_shapes=[pltpu.VMEM((length, d), BF)] * 2,
        compiler_params=params(28),
        cost_estimate=cost(8 * length * d * share, *h),
    )(order, dqkv, att, *h, *g)


EDGE = 16


def glu_kernel(h0, h1, w, z, sig_ref, slope_ref):
    h = jnp.concatenate([h0[...], h1[...]], axis=0)
    u = mm(h, w[...])
    share = z.shape[1]
    lin, sig = u[:, :share], jax.nn.sigmoid(u[:, share:])
    z[...] = (lin * sig).astype(BF)
    sig_ref[...] = sig.astype(BF)
    slope_ref[...] = (lin * sig * (1.0 - sig)).astype(BF)


def glu(pair, w):
    n, d = pair[0].shape
    share = w.shape[1] // 2
    return pl.pallas_call(
        glu_kernel,
        out_shape=[jax.ShapeDtypeStruct((2 * n, share), BF)] * 3,
        compiler_params=params(16),
        cost_estimate=cost(8 * n * d * share, w),
    )(*pair, w)


def lay_out(order, pairs, out):
    n = pairs[0].shape[0] // 2
    out[:EDGE, :] = jnp.zeros((EDGE, out.shape[1]), F32)
    out[EDGE + 2 * len(pairs) * n :, :] = jnp.zeros((EDGE, out.shape[1]), F32)
    for i in range(2 * len(pairs)):
        rows = pl.ds(pl.multiple_of(EDGE + order[i] * n, EDGE), n)
        out[rows, :] = pairs[i // 2][(i % 2) * n : (i % 2 + 1) * n, :].astype(F32)


def pick(ref, order, size):
    n = ref.shape[0] // size
    return jnp.concatenate(
        [ref[pl.ds(pl.multiple_of(order[i] * n, EDGE), n), :] for i in range(size)], axis=0
    )


def joined_rows(refs):
    return jnp.concatenate([r[...] for r in refs], axis=0)


def tap_masks(seg, taps, count):
    own = seg[EDGE : EDGE + count, :]
    first = EDGE - taps // 2
    return [(seg[first + k : first + k + count, :] == own).astype(F32) for k in range(taps)]


def convolve_kernel(order, seg, taps_ref, *refs, taps):
    pairs, (conv_ref, sums_ref, wide) = refs[:-3], refs[-3:]
    count = conv_ref.shape[0]
    lay_out(order, pairs, wide)
    first = EDGE - taps // 2
    total = None
    for k, mask in enumerate(tap_masks(seg, taps, count)):
        term = (wide[first + k : first + k + count, :] * mask) * taps_ref[k : k + 1, :]
        total = term if total is None else total + term
    conv_ref[...] = total
    sums_ref[0:1, :] = jnp.sum(total, axis=0, keepdims=True)
    sums_ref[1:2, :] = jnp.sum(total * total, axis=0, keepdims=True)


def convolve(order, seg, taps, pairs):
    count, share = seg.shape[0] - 2 * EDGE, pairs[0].shape[1]
    return pl.pallas_call(
        functools.partial(convolve_kernel, taps=taps.shape[0]),
        in_specs=[SMEM] + vmem(2 + len(pairs)),
        out_shape=[
            jax.ShapeDtypeStruct((count, share), F32),
            jax.ShapeDtypeStruct((2, share), F32),
        ],
        scratch_shapes=[pltpu.VMEM((count + 2 * EDGE, share), F32)],
        compiler_params=params(16),
        cost_estimate=cost(0, *pairs, *pairs, *pairs),
    )(order, seg, taps, *pairs)


def bn_stats(moments, total):
    centre = moments[0:1, :] / total
    return centre, lax.rsqrt(moments[1:2, :] / total - centre * centre + EPS)


def bn_kernel(order, conv, moments, gain, bias, w, e_ref, slope_ref, *refs, total):
    size = len(refs)
    n = conv.shape[0] // size
    centre, inverse = bn_stats(moments[...], total)
    shifted = (pick(conv, order, size) - centre) * inverse * gain[...] + bias[...]
    sig = jax.nn.sigmoid(shifted)
    e = (shifted * sig).astype(BF)
    e_ref[...] = e
    slope_ref[...] = (sig * (1.0 + shifted * (1.0 - sig))).astype(BF)
    p = mm(e, w[...])
    for i in range(size):
        refs[i % 2 * (size // 2) + i // 2][...] = p[i * n : (i + 1) * n].astype(
            BF if i % 2 else F32
        )


def chunk_shapes(n, d, size):
    return [jax.ShapeDtypeStruct((n, d), F32)] * (size // 2) + [
        jax.ShapeDtypeStruct((n, d), BF)
    ] * (size // 2)


def bn_forward(order, conv, moments, gain, bias, w, total):
    count, share = conv.shape
    d, size = w.shape[1], lax.axis_size("tm")
    out = pl.pallas_call(
        functools.partial(bn_kernel, total=total),
        in_specs=[SMEM] + vmem(5),
        out_shape=[jax.ShapeDtypeStruct((count, share), BF)] * 2
        + chunk_shapes(count // size, d, size),
        compiler_params=params(24),
        cost_estimate=cost(2 * count * share * d, conv),
    )(order, conv, moments, gain, bias, w)
    return out[0], out[1], out[2 : 2 + size // 2], out[2 + size // 2 :]


def conv_out_grad_kernel(g0, g1, w, out):
    g = jnp.concatenate([g0[...], g1[...]], axis=0)
    out[...] = mm_nt(g, w[...])


def conv_out_grad(pair, w):
    n, d = pair[0].shape
    return pl.pallas_call(
        conv_out_grad_kernel,
        out_shape=jax.ShapeDtypeStruct((2 * n, w.shape[0]), F32),
        compiler_params=params(12),
        cost_estimate=cost(4 * n * d * w.shape[0], w),
    )(*pair, w)


def bn_sums_kernel(order, conv, slope, moments, *refs, total):
    pairs, (dn_ref, sums_ref) = refs[:-2], refs[-2:]
    dn = joined_rows(pairs) * slope[...].astype(F32)
    dn_ref[...] = dn
    centre, inverse = bn_stats(moments[...], total)
    normed = (pick(conv, order, 2 * len(pairs)) - centre) * inverse
    sums_ref[0:1, :] = jnp.sum(dn, axis=0, keepdims=True)
    sums_ref[1:2, :] = jnp.sum(dn * normed, axis=0, keepdims=True)


def bn_back(order, conv, slope, moments, pairs, total):
    count, share = conv.shape
    return pl.pallas_call(
        functools.partial(bn_sums_kernel, total=total),
        in_specs=[SMEM] + vmem(3 + len(pairs)),
        out_shape=[
            jax.ShapeDtypeStruct((count, share), F32),
            jax.ShapeDtypeStruct((2, share), F32),
        ],
        compiler_params=params(16),
        cost_estimate=cost(0, conv, conv, conv),
    )(order, conv, slope, moments, *pairs)


def conv_back_kernel(
    order, seg, taps_ref, dn, conv, moments, sums, gain, w, *refs, taps, total, size
):
    chips = size // 2
    z, sig, slope = refs[:chips], refs[chips : 2 * chips], refs[2 * chips : 3 * chips]
    du_ref, dk_ref = refs[3 * chips : 3 * chips + 2]
    out, (c_wide, z_wide, dz_ref, dc_ref) = refs[3 * chips + 2 : -4], refs[-4:]
    count, share = dn.shape
    n = count // size
    centre, inverse = bn_stats(moments[...], total)
    normed = (pick(conv, order, size) - centre) * inverse
    dc = dn[...] - sums[0:1, :] / total - normed * (sums[1:2, :] / total)
    dc_ref[...] = (gain[...] * inverse * dc).astype(BF)
    lay_out(order, [dc_ref.at[2 * n * i : 2 * n * (i + 1)] for i in range(chips)], c_wide)
    lay_out(order, z, z_wide)
    first = EDGE - taps // 2
    masks = tap_masks(seg, taps, count)
    own = c_wide[EDGE : EDGE + count, :]
    dz = None
    for k in range(taps):
        mirror = taps - 1 - k
        near = c_wide[first + mirror : first + mirror + count, :] * masks[mirror]
        term = near * taps_ref[k : k + 1, :]
        dz = term if dz is None else dz + term
        dk_ref[k : k + 1, :] = jnp.sum(
            (z_wide[first + k : first + k + count, :] * masks[k]) * own, axis=0, keepdims=True
        )
    dz_ref[...] = dz
    dz = pick(dz_ref, order, size)
    du = jnp.concatenate(
        [dz * joined_rows(sig).astype(F32), dz * joined_rows(slope).astype(F32)], axis=1
    ).astype(BF)
    du_ref[...] = du
    p = mm_nt(du, w[...])
    for i in range(size):
        out[i % 2 * chips + i // 2][...] = p[i * n : (i + 1) * n].astype(BF if i % 2 else F32)


def conv_back(order, seg, taps, dn, conv, moments, sums, gain, w, kept, total):
    count, share = dn.shape
    d, size = w.shape[0], lax.axis_size("tm")
    wide = pltpu.VMEM((count + 2 * EDGE, share), F32)
    z, sig, slope = zip(*kept)
    out = pl.pallas_call(
        functools.partial(conv_back_kernel, taps=taps.shape[0], total=total, size=size),
        in_specs=[SMEM] + vmem(8 + 3 * len(kept)),
        out_shape=[
            jax.ShapeDtypeStruct((count, 2 * share), BF),
            jax.ShapeDtypeStruct((taps.shape[0], share), F32),
        ]
        + chunk_shapes(count // size, d, size),
        scratch_shapes=[
            wide,
            wide,
            pltpu.VMEM((count, share), F32),
            pltpu.VMEM((count, share), BF),
        ],
        compiler_params=params(30),
        cost_estimate=cost(4 * count * share * d, dn, dn, dn),
    )(order, seg, taps, dn, conv, moments, sums, gain, w, *z, *sig, *slope)
    return out[0], out[1], out[2 : 2 + size // 2], out[2 + size // 2 :]


def conv_grads_kernel(du, e, *refs):
    size = (len(refs) - 2) // 2
    in_ref, out_ref = refs[-2:]
    in_ref[...] = mm_tn(joined_rows(refs[:size]), du[...]).astype(BF)
    out_ref[...] = mm_tn(e[...], joined_rows(refs[size : 2 * size])).astype(BF)


def conv_grads(h, g, du, e):
    d, share = h[0].shape[1], e.shape[1]
    return pl.pallas_call(
        conv_grads_kernel,
        out_shape=[
            jax.ShapeDtypeStruct((d, 2 * share), BF),
            jax.ShapeDtypeStruct((share, d), BF),
        ],
        compiler_params=params(24),
        cost_estimate=cost(6 * e.shape[0] * share * d, du, e),
    )(du, e, *h, *g)


def shards(
    frames,
    segments,
    ffn1_in,
    ffn1_out,
    query_w,
    key_w,
    value_w,
    attn_out,
    conv_in,
    conv_out,
    ffn2_in,
    ffn2_out,
    norm_gains,
    conv_kernel,
    bn_gain,
    bn_bias,
    rel_table,
    cotangent,
):
    rows, size = lax.axis_size("rows"), lax.axis_size("tm")
    t = lax.axis_index("tm")
    own, width = frames.shape[1], frames.shape[2]
    length = own * size
    share = width // size
    heads = rel_table.shape[0] // size
    taps = conv_kernel.shape[0]
    frame_total = float(length * rows)
    seg = segments[0]
    table = lax.dynamic_slice_in_dim(rel_table, t * heads, heads, 0)
    depth = width // rows
    unit = depth // size

    def mine(v):
        v = v.reshape(-1, rows, size, unit)
        return lax.dynamic_index_in_dim(v, t, 2, keepdims=False).reshape(-1, share)

    def placed(v):
        n = v.shape[0]
        out = jnp.zeros((n, rows, size, unit), F32)
        return lax.dynamic_update_index_in_dim(
            out, v.reshape(n, rows, unit), t, 2
        ).reshape(n, width)

    kernel_own = mine(conv_kernel)
    bn_gain_own, bn_bias_own = mine(bn_gain[None]), mine(bn_bias[None])
    seg_near = jnp.pad(seg, (EDGE, EDGE), constant_values=-1).reshape(-1, 1)

    perm = head_rows_perm()
    out_block = lax.ppermute(attn_out, ("rows", "tm"), perm)
    order = jnp.stack(
        [peer_index(dx, dc) for dx in range(size // 2) for dc in range(2)]
    ).astype(jnp.int32)
    f1, attn_part, sent = gather_ffn(ffn1_in, ffn1_out, (query_w, key_w, value_w, out_block))
    wide = conv_in.shape[1]
    pieces = exchange_all(
        [
            after(conv_in, sent)
            .reshape(depth, wide // depth, size, unit)
            .transpose(2, 0, 1, 3)
            .reshape(size, depth, wide // size),
            after(conv_out, sent).reshape(size, unit, share),
        ]
    )
    packed = [pack(side_by_side(p), width) for p in pieces]
    sent = jnp.concatenate(packed, axis=0)
    full = lax.all_gather(sent, "rows", axis=0, tiled=False)
    at = packed[0].shape[0]
    conv_in_w, conv_out_w = unpack(full[:, :at], wide), unpack(full[:, at:], width)
    f2, _, sent = gather_ffn(after(ffn2_in, sent), ffn2_out)

    inputs = frames[0].astype(F32)
    n1 = norm_rows(inputs, norm_gains[0])[0]
    h1, _ = spread(n1.astype(BF), lambda near: ())
    h1[0] = (after(h1[0][0], sent), h1[0][1])
    one = [ffn(pair, *f1) for pair in reversed(h1)][::-1]
    parts, attn_w = collect(
        [v[2] for v in one], [v[3] for v in one], lambda ready: ready(attn_part)
    )
    x1, n2 = add_norm(parts, inputs, norm_gains[1], 0.5)

    h2, local = spread(n2, lambda near: project(near, attn_w, 3 * share))
    pairs = [local] + [project(pair, attn_w, 3 * share) for pair in h2[1:]]
    qkv, att, lse, mine_a, theirs_a = attend(order, pairs, seg, table, attn_w)
    parts, _ = collect(mine_a, theirs_a)
    x2, n3 = add_norm(parts, x1, norm_gains[2], 1.0)

    h3, local = spread(n3, lambda near: glu(near, conv_in_w))
    kept = [local] + [glu(pair, conv_in_w) for pair in h3[1:]]
    conv, moments = convolve(order, seg_near, kernel_own, [v[0] for v in kept])
    moments = sum_axis(moments, "rows")
    e, e_slope, mine_c, theirs_c = bn_forward(
        order, conv, moments, bn_gain_own, bn_bias_own, conv_out_w, frame_total
    )
    parts, _ = collect(mine_c, theirs_c)
    x3, n4 = add_norm(parts, x2, norm_gains[3], 1.0)

    h4, local = spread(n4, lambda near: ffn(near, *f2))
    four = [local] + [ffn(pair, *f2) for pair in h4[1:]]
    parts, _ = collect([v[2] for v in four], [v[3] for v in four])
    output, d4, g, gain_five = turn(parts, x3, norm_gains[4], cotangent[0])

    g4, local = spread(g, lambda near: ffn_back(near, four[0][1], *f2))
    back = [local] + [ffn_back(p, four[i][1], *f2) for i, p in enumerate(g4[1:], 1)]
    parts, packed_four = collect(
        [v[1] for v in back],
        [v[2] for v in back],
        lambda ready: ffn_grads(
            [ready(v) for v in sum(h4, ())],
            sum(g4, ()),
            [v[0] for v in back],
            [ready(v[0]) for v in four],
        ),
    )
    d3, g, gain_four = back_norm(parts, x3, norm_gains[3], d4, 1.0)
    sum_four = scatter_rows(after(packed_four, g))

    g3, local = spread(g, lambda near: conv_out_grad(near, conv_out_w))
    pairs = [local] + [conv_out_grad(pair, conv_out_w) for pair in g3[1:]]
    dn, bn_part = bn_back(order, conv, e_slope, moments, pairs, frame_total)
    bn_sums = sum_axis(bn_part, "rows")
    du, d_kernel, mine_c, theirs_c = conv_back(
        order,
        seg_near,
        kernel_own,
        dn,
        conv,
        moments,
        bn_sums,
        bn_gain_own,
        conv_in_w,
        kept,
        frame_total,
    )
    parts, _ = collect(mine_c, theirs_c)
    d2, g, gain_three = back_norm(parts, x2, norm_gains[2], d3, 1.0)

    g2, local = spread(
        g,
        lambda near: (
            att_grad(near, attn_w, share),
            conv_grads([after(v, g) for v in sum(h3, ())], sum(g3, ()), du, e),
        ),
    )
    local, parts_three = local
    packed_three = pack_grads(parts_three)
    pairs = [local] + [att_grad(pair, attn_w, share) for pair in g2[1:]]
    dqkv, band, mine_a, theirs_a = attend_back(order, pairs, qkv, seg, table, lse, attn_w)

    def attention_sums(ready):
        packed = attend_grads(
            order, [ready(v) for v in sum(h2, ())], sum(g2, ()), dqkv, att
        )
        if packed.shape[2] == packed_three.shape[2]:
            return (jnp.concatenate([packed, packed_three], axis=1),)
        return packed, packed_three

    parts, packed_mid = collect(mine_a, theirs_a, attention_sums)
    d1, g, gain_two = back_norm(parts, x1, norm_gains[1], d2, 0.5)
    if len(packed_mid) == 1:
        sum_mid = scatter_rows(packed_mid[0])
        sum_two, sum_three = sum_mid[:depth], sum_mid[depth:]
    else:
        sum_two, sum_three = (scatter_rows(v) for v in packed_mid)

    g1, local = spread(g, lambda near: ffn_back(near, one[0][1], *f1))
    back = [local] + [ffn_back(p, one[i][1], *f1) for i, p in enumerate(g1[1:], 1)]
    part_one, other = parity_grads(
        sum(h1, ()), sum(g1, ()), [v[0] for v in back], [v[0] for v in one]
    )
    rows_near = lax.ppermute(other, "rows", [(i, i ^ 1) for i in range(rows)])
    parts, _ = collect([v[1] for v in back], [v[2] for v in back])
    grad, _, gain_one = back_norm(parts, inputs, norm_gains[0], d1, 1.0)
    grad_frames = grad.astype(BF)[None]

    def ffn_parts(total):
        if total.shape == (2 * depth, width) and ffn1_in.shape[1] == width:
            return total[:depth], total[depth:]
        like = [
            jax.ShapeDtypeStruct((width, ffn1_in.shape[1]), BF),
            jax.ShapeDtypeStruct((ffn1_in.shape[1], width), BF),
        ]
        return unpack_grads(total, like)

    def ffn_owned(total):
        if whole_lanes(ffn1_in.shape, ffn1_out.shape):
            return returned_ffn(total, ffn1_in.shape, ffn1_out.shape)
        g_in, g_out = ffn_parts(total)
        return (
            ffn_back_in(g_in, ffn1_in.shape, ffn1_out.shape),
            ffn_back_out(g_out, ffn1_out.shape),
        )

    grad_ffn2_in, grad_ffn2_out = ffn_owned(sum_four)
    sum_one = scatter_parity(
        part_one, after(rows_near, grad, grad_ffn2_in, grad_ffn2_out)
    )
    grad_query, grad_key, grad_value, d_block = (
        sum_two[:, i * share : (i + 1) * share] for i in range(4)
    )
    grad_query, grad_key, grad_value = (v.astype(F32) for v in (grad_query, grad_key, grad_value))
    grad_attn_out = lax.ppermute(d_block, ("rows", "tm"), [(b, a) for a, b in perm]).astype(F32)
    d_in, d_out = unpack_grads(sum_three, parts_three)
    d_in, d_out = exchange_all(
        [
            d_in.reshape(depth, size, -1).transpose(1, 0, 2),
            d_out.reshape(unit, size, share).transpose(1, 0, 2),
        ]
    )
    grad_conv_in = (
        d_in.reshape(size, depth, wide // depth, unit)
        .transpose(1, 2, 0, 3)
        .reshape(depth, wide)
        .astype(F32)
    )
    grad_conv_out = d_out.reshape(depth, share).astype(F32)
    grad_ffn1_in, grad_ffn1_out = ffn_owned(sum_one)

    table_row = lax.dynamic_update_slice_in_dim(
        jnp.zeros(rel_table.shape, F32), table_grad(band), t * heads, 0
    ).reshape(1, -1)
    table_row = jnp.pad(table_row, ((0, 0), (0, width - table_row.shape[1])))
    small = jnp.concatenate(
        [
            gain_one,
            gain_two,
            gain_three,
            gain_four,
            gain_five,
            placed(d_kernel),
            placed(bn_part),
            table_row,
        ],
        axis=0,
    )
    small = sum_axis(sum_axis(after(small, rows_near), "tm"), "rows")
    table_size = rel_table.shape[0] * rel_table.shape[1]
    return (
        output[None],
        grad_frames,
        grad_ffn1_in,
        grad_ffn1_out,
        grad_query,
        grad_key,
        grad_value,
        grad_attn_out,
        grad_conv_in,
        grad_conv_out,
        grad_ffn2_in,
        grad_ffn2_out,
        small[:5],
        small[5 : 5 + taps],
        small[6 + taps],
        small[5 + taps],
        small[7 + taps, :table_size].reshape(rel_table.shape),
    )


def solution(mesh):
    split, copied = P("rows", "tm"), P()
    sequence = P("rows", "tm", None)
    return jax.shard_map(
        shards,
        mesh=mesh,
        in_specs=(sequence, P("rows", None)) + (split,) * 10 + (copied,) * 5 + (sequence,),
        out_specs=(sequence, sequence) + (split,) * 10 + (copied,) * 5,
        check_vma=False,
    )
```
